32 devices in a mesh: groups: 2 (over y), tm: 4 (over z), space: 2 (over x), chan: 2 (over core).
Axes of the slice: x: 2, y: 2, z: 4, core: 2. Of those that a mesh axis runs over, the one named last changes fastest.
Arguments:
- latents: bfloat16 [4, 8, 4, 8, 512], P('groups', 'tm', 'space', None, 'chan'), parts along dimension 0, may hold values from -60 to 60
- conv_weight: bfloat16 [3, 3, 3, 512, 512], P(None, None, None, 'tm', 'chan'), may hold values from -0.0546875 to 0.0546875
- conv_bias: float32 [512], P('chan'), may hold values from -4 to 4
- gn_gain: float32 [512], P('chan'), may hold values from 0.5 to 1.5
- gn_shift: float32 [512], P('chan'), may hold values from -3 to 3
- up_weight: bfloat16 [3, 3, 512, 512], P(None, None, None, 'chan'), may hold values from -0.09375 to 0.09375
- up_bias: float32 [512], P('chan'), may hold values from -3 to 3
Outputs:
- decoded: bfloat16 [4, 8, 8, 16, 512], P('groups', None, 'space', 'tm', 'chan'), parts along dimension 0
The draws below stay inside these ranges and needn't reach their ends.
There are 2 independent parts, one for each index of `groups`. The reference program is written for one: setup_inputs(seed, part) draws one part's arguments, and reference() takes and returns one part's arrays. A program takes and returns all parts, laid end to end along the dimension named above; an argument that names none is the same for every part. Nothing has to cross between parts.
All inputs are finite; a program needn't handle non-finite values.
Results may differ from the reference program's by a relative error of at most 0.0052.
The reference program's roundings to bfloat16 on the way count: a program that leaves them out, or rounds other values in their place, can miss the bound.
Values may be sent and summed in bfloat16 or wider, within the bound.
No kernel may reach another device: no remote copies, remote signals or barrier semaphores. Data moves between devices by JAX's collectives and lax.ppermute only.
A program may use at most 64 MiB of HBM per device.

```python
import math
import jax
import jax.numpy as jnp
from jax import lax

C = 512
GROUPS = 32
TF = 2
CLIPS = 2
LATENT_FRAMES = 8
LATENT_ROWS = 4
LATENT_COLUMNS = 8


def rough_scale(key, count):
    return 10.0 ** jax.random.uniform(key, (count,), jnp.float32, 0.0, 0.25)


def shared_field(amp_key, phase_key, freq_key):
    amplitudes = jax.random.uniform(amp_key, (CLIPS, 2), jnp.float32, 1.0, 2.0)
    phases = jax.random.uniform(phase_key, (CLIPS, 2), jnp.float32, -math.pi, math.pi)
    freqs = jax.random.randint(freq_key, (CLIPS, 3), 1, 3).astype(jnp.float32)
    two_pi = 2.0 * math.pi
    frame_pos = jnp.arange(LATENT_FRAMES, dtype=jnp.float32) / LATENT_FRAMES
    row_pos = jnp.arange(LATENT_ROWS, dtype=jnp.float32) / LATENT_ROWS
    col_pos = jnp.arange(LATENT_COLUMNS, dtype=jnp.float32) / LATENT_COLUMNS
    temporal = amplitudes[:, 0, None] * jnp.cos(two_pi * freqs[:, 0, None] * frame_pos[None, :] + phases[:, 0, None])
    angle = two_pi * (freqs[:, 1, None, None] * row_pos[None, :, None] + freqs[:, 2, None, None] * col_pos[None, None, :])
    spatial = amplitudes[:, 1, None, None] * jnp.cos(angle + phases[:, 1, None, None])
    return temporal[:, :, None, None, None] + spatial[:, None, :, :, None]


def draw_latents(key, part):
    keys = jax.random.split(key, 10)
    layout = (CLIPS, LATENT_FRAMES, LATENT_ROWS, LATENT_COLUMNS, C)
    base = jax.random.truncated_normal(keys[0], -4.0, 4.0, layout, jnp.float32)
    shared = shared_field(keys[6], keys[7], keys[8])
    mixed = 0.7 * base + 0.7 * shared
    trend_frames = 2.0 ** (jnp.arange(LATENT_FRAMES, dtype=jnp.float32) / LATENT_FRAMES)
    trend_rows = 2.0 ** (jnp.arange(LATENT_ROWS, dtype=jnp.float32) / LATENT_ROWS)
    frame_scale = (trend_frames * rough_scale(keys[2], LATENT_FRAMES))[:, None, None, None]
    row_scale = (trend_rows * rough_scale(keys[3], LATENT_ROWS))[:, None, None]
    col_scale = rough_scale(keys[4], LATENT_COLUMNS)[:, None]
    upper_scale = rough_scale(keys[5], C)
    lower_scale = rough_scale(keys[9], C)
    lower_rows = jnp.arange(LATENT_ROWS) >= LATENT_ROWS // 2
    chan_scale = jnp.where(lower_rows[:, None], lower_scale[None, :], upper_scale[None, :])[:, None, :]
    scaled = mixed * frame_scale * row_scale * col_scale * chan_scale / 4.5
    return scaled.astype(jnp.bfloat16)


def block_scale(stream_key, dims, shards, least, high):
    loudness, own = 1.0, jax.random.fold_in(stream_key, 6)
    for axis_at, blocks in shards:
        draws = jnp.exp(jax.random.uniform(jax.random.fold_in(own, axis_at), (blocks,), jnp.float32, least / len(shards), high / len(shards)))
        loudness = loudness * jnp.repeat(draws, dims[axis_at] // blocks).reshape([-1 if axis == axis_at else 1 for axis in range(len(dims))])
    return loudness


def centred(stream_key, dims, width, most, pieces=(), kind=jnp.bfloat16):
    drawn = width * jax.random.normal(stream_key, dims, jnp.float32)
    if pieces:
        drawn = drawn * block_scale(stream_key, dims, pieces, -0.22, 0.18)
    return jnp.clip(drawn, -most, most).astype(kind)


def setup_inputs(seed: int = 0, part: int = 0) -> dict:
    splits = jax.random.split(jax.random.key(seed), 8)
    part_splits = jax.random.split(jax.random.fold_in(splits[7], part), 8)
    return {
        "latents": draw_latents(jax.random.fold_in(jax.random.fold_in(splits[7], part), 71), part),
        "conv_weight": centred(splits[1], (3, 3, 3, C, C), (27 * C) ** -0.5, 0.0546875, ((3, 4), (4, 2))),
        "conv_bias": centred(splits[2], (C,), 1.0, 4.0, ((0, 2),), jnp.float32),
        "gn_gain": jnp.clip(0.5 + 1.0 * jax.random.uniform(splits[3], (C,), jnp.float32) ** block_scale(splits[3], (C,), ((0, 2),), -0.2, 0.2), 0.5, 1.5),
        "gn_shift": centred(splits[4], (C,), 0.5, 3.0, ((0, 2),), jnp.float32),
        "up_weight": centred(splits[5], (3, 3, C, C), (9 * C) ** -0.5, 0.09375, ((3, 2),)),
        "up_bias": centred(splits[6], (C,), 0.5, 3.0, ((0, 2),), jnp.float32),
    }


def causal_conv(latents, conv_weight, conv_bias):
    ordered = jnp.stack([jnp.roll(latents[clip_index], -clip_index * TF, axis=0) for clip_index in range(CLIPS)])
    padded = jnp.pad(ordered.astype(jnp.float32), ((0, 0), (2, 0), (1, 1), (1, 1), (0, 0)))
    summed = lax.conv_general_dilated(padded, conv_weight.astype(jnp.float32), (1, 1, 1), 'VALID', dimension_numbers=('NDHWC', 'DHWIO', 'NDHWC'), precision=lax.Precision.HIGHEST)
    conved = (summed + conv_bias).astype(jnp.bfloat16)
    return jnp.stack([jnp.roll(conved[clip_index], clip_index * TF, axis=0) for clip_index in range(CLIPS)])

def reference(latents, conv_weight, conv_bias, gn_gain, gn_shift, up_weight, up_bias):
    conved = causal_conv(latents, conv_weight, conv_bias)
    group_width = C // GROUPS
    grouped_values = conved.astype(jnp.float32).reshape(CLIPS, LATENT_FRAMES, LATENT_ROWS, LATENT_COLUMNS, GROUPS, group_width)
    element_count = float(LATENT_FRAMES * LATENT_ROWS * LATENT_COLUMNS * group_width)
    group_mean = lax.optimization_barrier(jnp.sum(grouped_values, axis=(1, 2, 3, 5))) / element_count
    group_variance = lax.optimization_barrier(jnp.sum(grouped_values * grouped_values, axis=(1, 2, 3, 5))) / element_count - group_mean * group_mean
    factor = lax.rsqrt(group_variance + 1e-06)
    normed = (grouped_values - group_mean[:, None, None, None, :, None]) * factor[:, None, None, None, :, None]
    normed = normed.reshape(CLIPS, LATENT_FRAMES, LATENT_ROWS, LATENT_COLUMNS, C) * gn_gain + gn_shift
    active = jax.nn.silu(normed).astype(jnp.bfloat16)
    widened = jnp.repeat(jnp.repeat(active, 2, axis=2), 2, axis=3)
    padded = jnp.pad(widened.astype(jnp.float32), ((0, 0), (0, 0), (1, 1), (1, 1), (0, 0)))
    flat = padded.reshape(CLIPS * LATENT_FRAMES, 2 * LATENT_ROWS + 2, 2 * LATENT_COLUMNS + 2, C)
    output = lax.conv_general_dilated(flat, up_weight.astype(jnp.float32), (1, 1), 'VALID', dimension_numbers=('NHWC', 'HWIO', 'NHWC'), precision=lax.Precision.HIGHEST)
    output = output + up_bias
    return output.reshape(CLIPS, LATENT_FRAMES, 2 * LATENT_ROWS, 2 * LATENT_COLUMNS, C).astype(jnp.bfloat16)
```

```python
import jax
import jax.numpy as jnp
from jax import lax
from jax.sharding import PartitionSpec as P

C = 512
GROUPS = 32


def shifted(value, axis, step):
    count = lax.axis_size(axis)
    pairs = [(i, i + step) for i in range(count) if 0 <= i + step < count]
    return lax.ppermute(value, axis, pairs)


def rows_around(block, axis_rows, depth):
    low = shifted(lax.slice_in_dim(block, block.shape[axis_rows] - depth, None, axis=axis_rows), "space", 1)
    high = shifted(lax.slice_in_dim(block, 0, depth, axis=axis_rows), "space", -1)
    return jnp.concatenate([low, block, high], axis=axis_rows)


def input_slice(latents):
    clips, span, rows, cols, half = latents.shape
    spans, spaces, chans = lax.axis_size("tm"), lax.axis_size("space"), lax.axis_size("chan")
    me, row_block = lax.axis_index("tm"), lax.axis_index("space")
    depth = half * chans // spans
    per_half = half // depth
    if spaces == 2:
        whole = lax.all_gather(latents, ("tm", "space", "chan"))
        whole = whole.reshape(spans, spaces, chans, clips, span, rows, cols, per_half, depth)
        mine = lax.dynamic_index_in_dim(whole, me // per_half, axis=2, keepdims=False)
        mine = lax.dynamic_index_in_dim(mine, me % per_half, axis=7 - 1, keepdims=False)
        mine = mine.transpose(2, 0, 3, 1, 4, 5, 6).reshape(clips, spans * span, spaces * rows, cols, depth)
        mine = jnp.pad(mine, ((0, 0), (0, 0), (1, 1), (0, 0), (0, 0)))
        mine = lax.dynamic_slice_in_dim(mine, row_block * rows, rows + 2, axis=2)
    else:
        bordered = rows_around(latents, 2, 1)
        whole = lax.all_gather(bordered, ("tm", "chan"))
        whole = whole.reshape((spans, chans) + bordered.shape[:4] + (per_half, depth))
        mine = lax.dynamic_index_in_dim(whole, me // per_half, axis=1, keepdims=False)
        mine = lax.dynamic_index_in_dim(mine, me % per_half, axis=5, keepdims=False)
        mine = mine.transpose(1, 0, 2, 3, 4, 5).reshape(clips, spans * span, rows + 2, cols, depth)
    return jnp.stack([jnp.roll(mine[c], -c * span, axis=0) for c in range(clips)])


def on_device(latents, conv_weight, conv_bias, gn_gain, gn_shift, up_weight, up_bias):
    clips, span, rows, cols, half = latents.shape
    spans, spaces, chans = lax.axis_size("tm"), lax.axis_size("space"), lax.axis_size("chan")
    me, row_block = lax.axis_index("tm"), lax.axis_index("space")
    frames, width = span * spans, cols // spans
    group_width = C // GROUPS

    mine = input_slice(latents)
    padded = jnp.pad(mine, ((0, 0), (2, 0), (0, 0), (1, 1), (0, 0)))
    partial = lax.conv_general_dilated(
        padded,
        conv_weight,
        (1, 1, 1),
        "VALID",
        dimension_numbers=("NDHWC", "DHWIO", "NDHWC"),
        preferred_element_type=jnp.float32,
    )
    partial = jnp.stack([jnp.roll(partial[c], c * span, axis=0) for c in range(clips)])
    parts = partial.reshape(clips, frames, rows, spans, width, half)
    parts = parts.transpose(3, 0, 1, 2, 4, 5)
    parts = lax.all_to_all(parts, "tm", split_axis=0, concat_axis=0, tiled=True)
    conved = (jnp.sum(parts, axis=0) + conv_bias).astype(jnp.bfloat16)

    values = conved.astype(jnp.float32).reshape(-1, half)
    values = values.reshape(clips, frames * rows * width, half // group_width, group_width)
    if spaces == 2:
        every = lax.all_gather(conved, ("tm", "space", "chan"))
        every = every.reshape(spans, spaces, chans, clips, frames, rows, width, half)
        every = every.transpose(3, 4, 1, 5, 0, 6, 2, 7).reshape(clips, frames, spaces * rows, cols, C)
        gain = lax.all_gather(gn_gain, "chan", tiled=True)
        shift = lax.all_gather(gn_shift, "chan", tiled=True)
        values = every.astype(jnp.float32).reshape(clips, -1, GROUPS, group_width)
        sums = jnp.sum(values, axis=(1, 3))
        squares = jnp.sum(values * values, axis=(1, 3))
        count = float(values.shape[1] * group_width)
        mean = sums / count
        factor = lax.rsqrt(squares / count - mean * mean + 1e-06)
        edged = jnp.pad(every, ((0, 0), (0, 0), (1, 1), (1, 1), (0, 0)))
        tile = lax.dynamic_slice(
            edged, (0, 0, row_block * rows, me * width, 0), (clips, frames, rows + 2, width + 2, C)
        )
    else:
        sums = jnp.sum(values, axis=(1, 3))
        squares = jnp.sum(values * values, axis=(1, 3))
        sums, squares = lax.psum((sums, squares), ("tm", "space"))
        count = float(values.shape[1] * group_width * spans * spaces)
        mean = sums / count
        factor = lax.rsqrt(squares / count - mean * mean + 1e-06)
        bordered = rows_around(conved, 2, 1)
        left = shifted(bordered[:, :, :, -1:], "tm", 1)
        right = shifted(bordered[:, :, :, :1], "tm", -1)
        tile = jnp.concatenate([left, bordered, right], axis=3)
        tile = lax.all_gather(tile, "chan", axis=4, tiled=True)
        gain, shift, mean, factor = (
            lax.all_gather(v, "chan", axis=v.ndim - 1, tiled=True) for v in (gn_gain, gn_shift, mean, factor)
        )
    mean = jnp.repeat(mean, group_width, axis=1)[:, None, None, None]
    factor = jnp.repeat(factor, group_width, axis=1)[:, None, None, None]
    normed = (tile.astype(jnp.float32) - mean) * factor * gain + shift
    row_at = row_block * rows - 1 + jnp.arange(rows + 2)
    col_at = me * width - 1 + jnp.arange(width + 2)
    inside = ((row_at >= 0) & (row_at < rows * spaces))[:, None] & ((col_at >= 0) & (col_at < cols))[None]
    active = jnp.where(inside[None, None, :, :, None], jax.nn.silu(normed), 0.0).astype(jnp.bfloat16)
    wide = jnp.repeat(jnp.repeat(active, 2, axis=2), 2, axis=3)[:, :, 1:-1, 1:-1]
    flat = wide.reshape((clips * frames,) + wide.shape[2:])
    output = lax.conv_general_dilated(
        flat,
        up_weight,
        (1, 1),
        "VALID",
        dimension_numbers=("NHWC", "HWIO", "NHWC"),
        preferred_element_type=jnp.float32,
    )
    output = (output + up_bias).astype(jnp.bfloat16)
    return output.reshape(clips, frames, 2 * rows, 2 * width, half)


def solution(mesh):
    placed = (
        P("groups", "tm", "space", None, "chan"),
        P(None, None, None, "tm", "chan"),
        P("chan"),
        P("chan"),
        P("chan"),
        P(None, None, None, "chan"),
        P("chan"),
    )
    return jax.shard_map(
        on_device,
        mesh=mesh,
        in_specs=placed,
        out_specs=P("groups", None, "space", "tm", "chan"),
        check_vma=False,
    )
```

```python
import jax
import jax.numpy as jnp
from jax import lax
from jax.experimental import pallas as pl
from jax.experimental.pallas import tpu as pltpu
from jax.sharding import Mesh
from jax.sharding import PartitionSpec as P

C = 512
GROUPS = 32


def shifted(value, axis, step):
    count = lax.axis_size(axis)
    pairs = [(i, i + step) for i in range(count) if 0 <= i + step < count]
    return lax.ppermute(value, axis, pairs)


def rows_around(block, axis_rows, depth):
    low = shifted(lax.slice_in_dim(block, block.shape[axis_rows] - depth, None, axis=axis_rows), "space", 1)
    high = shifted(lax.slice_in_dim(block, 0, depth, axis=axis_rows), "space", -1)
    return jnp.concatenate([low, block, high], axis=axis_rows)


def input_slice(latents):
    clips, span, rows, cols, half = latents.shape
    spans, spaces, chans = lax.axis_size("tm"), lax.axis_size("space"), lax.axis_size("chan")
    me, row_block = lax.axis_index("tm"), lax.axis_index("space")
    depth = half * chans // spans
    per_half = half // depth
    if spaces == 2:
        whole = lax.all_gather(latents, ("tm", "space", "chan"))
        whole = whole.reshape(spans, spaces, chans, clips, span, rows, cols, per_half, depth)
        mine = lax.dynamic_index_in_dim(whole, me // per_half, axis=2, keepdims=False)
        mine = lax.dynamic_index_in_dim(mine, me % per_half, axis=7 - 1, keepdims=False)
        mine = mine.transpose(2, 0, 3, 1, 4, 5, 6).reshape(clips, spans * span, spaces * rows, cols, depth)
        mine = jnp.pad(mine, ((0, 0), (0, 0), (1, 1), (0, 0), (0, 0)))
        mine = lax.dynamic_slice_in_dim(mine, row_block * rows, rows + 2, axis=2)
    else:
        bordered = rows_around(latents, 2, 1)
        whole = lax.all_gather(bordered, ("tm", "chan"))
        whole = whole.reshape((spans, chans) + bordered.shape[:4] + (per_half, depth))
        mine = lax.dynamic_index_in_dim(whole, me // per_half, axis=1, keepdims=False)
        mine = lax.dynamic_index_in_dim(mine, me % per_half, axis=5, keepdims=False)
        mine = mine.transpose(1, 0, 2, 3, 4, 5).reshape(clips, spans * span, rows + 2, cols, depth)
    return jnp.stack([jnp.roll(mine[c], -c * span, axis=0) for c in range(clips)])


def general_plan(latents, conv_weight, conv_bias, gn_gain, gn_shift, up_weight, up_bias):
    clips, span, rows, cols, half = latents.shape
    spans, spaces, chans = lax.axis_size("tm"), lax.axis_size("space"), lax.axis_size("chan")
    me, row_block = lax.axis_index("tm"), lax.axis_index("space")
    frames, width = span * spans, cols // spans
    group_width = C // GROUPS

    mine = input_slice(latents)
    padded = jnp.pad(mine, ((0, 0), (2, 0), (0, 0), (1, 1), (0, 0)))
    partial = lax.conv_general_dilated(
        padded,
        conv_weight,
        (1, 1, 1),
        "VALID",
        dimension_numbers=("NDHWC", "DHWIO", "NDHWC"),
        preferred_element_type=jnp.float32,
    )
    partial = jnp.stack([jnp.roll(partial[c], c * span, axis=0) for c in range(clips)])
    parts = partial.reshape(clips, frames, rows, spans, width, half)
    parts = parts.transpose(3, 0, 1, 2, 4, 5)
    parts = lax.all_to_all(parts, "tm", split_axis=0, concat_axis=0, tiled=True)
    conved = (jnp.sum(parts, axis=0) + conv_bias).astype(jnp.bfloat16)

    values = conved.astype(jnp.float32).reshape(-1, half)
    values = values.reshape(clips, frames * rows * width, half // group_width, group_width)
    if spaces == 2:
        every = lax.all_gather(conved, ("tm", "space", "chan"))
        every = every.reshape(spans, spaces, chans, clips, frames, rows, width, half)
        every = every.transpose(3, 4, 1, 5, 0, 6, 2, 7).reshape(clips, frames, spaces * rows, cols, C)
        gain = lax.all_gather(gn_gain, "chan", tiled=True)
        shift = lax.all_gather(gn_shift, "chan", tiled=True)
        values = every.astype(jnp.float32).reshape(clips, -1, GROUPS, group_width)
        sums = jnp.sum(values, axis=(1, 3))
        squares = jnp.sum(values * values, axis=(1, 3))
        count = float(values.shape[1] * group_width)
        mean = sums / count
        factor = lax.rsqrt(squares / count - mean * mean + 1e-06)
        edged = jnp.pad(every, ((0, 0), (0, 0), (1, 1), (1, 1), (0, 0)))
        tile = lax.dynamic_slice(
            edged, (0, 0, row_block * rows, me * width, 0), (clips, frames, rows + 2, width + 2, C)
        )
    else:
        sums = jnp.sum(values, axis=(1, 3))
        squares = jnp.sum(values * values, axis=(1, 3))
        sums, squares = lax.psum((sums, squares), ("tm", "space"))
        count = float(values.shape[1] * group_width * spans * spaces)
        mean = sums / count
        factor = lax.rsqrt(squares / count - mean * mean + 1e-06)
        bordered = rows_around(conved, 2, 1)
        left = shifted(bordered[:, :, :, -1:], "tm", 1)
        right = shifted(bordered[:, :, :, :1], "tm", -1)
        tile = jnp.concatenate([left, bordered, right], axis=3)
        tile = lax.all_gather(tile, "chan", axis=4, tiled=True)
        gain, shift, mean, factor = (
            lax.all_gather(v, "chan", axis=v.ndim - 1, tiled=True) for v in (gn_gain, gn_shift, mean, factor)
        )
    mean = jnp.repeat(mean, group_width, axis=1)[:, None, None, None]
    factor = jnp.repeat(factor, group_width, axis=1)[:, None, None, None]
    normed = (tile.astype(jnp.float32) - mean) * factor * gain + shift
    row_at = row_block * rows - 1 + jnp.arange(rows + 2)
    col_at = me * width - 1 + jnp.arange(width + 2)
    inside = ((row_at >= 0) & (row_at < rows * spaces))[:, None] & ((col_at >= 0) & (col_at < cols))[None]
    active = jnp.where(inside[None, None, :, :, None], jax.nn.silu(normed), 0.0).astype(jnp.bfloat16)
    wide = jnp.repeat(jnp.repeat(active, 2, axis=2), 2, axis=3)[:, :, 1:-1, 1:-1]
    flat = wide.reshape((clips * frames,) + wide.shape[2:])
    output = lax.conv_general_dilated(
        flat,
        up_weight,
        (1, 1),
        "VALID",
        dimension_numbers=("NHWC", "HWIO", "NHWC"),
        preferred_element_type=jnp.float32,
    )
    output = (output + up_bias).astype(jnp.bfloat16)
    return output.reshape(clips, frames, 2 * rows, 2 * width, half)


def conv_kernel(side_ref, latents_ref, weight_ref, sums_ref, taps):
    spaces, his, los, clips, span, rows, cols, depth = latents_ref.shape
    spans = his * los
    frames = spans * span
    side = side_ref[0]
    block = rows * cols
    lead = 2 * block
    column = lax.broadcasted_iota(jnp.int32, (1, 1, cols, depth), 2)
    for clip in range(clips):
        taps[clip, :lead] = jnp.zeros((lead, taps.shape[2]), taps.dtype)
        order = [(j + clip) % spans for j in range(spans)]

        def taken(at, row):
            parts = [latents_ref[at, j // los, j % los, clip, :, row] for j in order]
            return jnp.concatenate(parts, axis=0).astype(jnp.float32)

        above = jnp.where(side > 0, taken(1 - side, rows - 1), 0.0)
        below = jnp.where(side > 0, 0.0, taken(1 - side, 0))
        own = [taken(side, row) for row in range(rows)]
        tall = jnp.stack([above] + own + [below], axis=1)
        shifts = (
            jnp.where(column > 0, pltpu.roll(tall, 1, 2), 0.0),
            tall,
            jnp.where(column < cols - 1, pltpu.roll(tall, cols - 1, 2), 0.0),
        )
        for e in range(3):
            for b in range(3):
                piece = shifts[e][:, b : b + rows].reshape(frames * block, depth)
                at = (b * 3 + e) * depth
                taps[clip, lead:, at : at + depth] = piece.astype(taps.dtype)
    total = None
    for a in range(3):
        left = jnp.concatenate(
            [taps[clip, a * block : a * block + frames * block] for clip in range(clips)], axis=0
        )
        right = weight_ref[a].reshape(9 * depth, weight_ref.shape[4])
        part = jnp.dot(left, right, preferred_element_type=jnp.float32)
        total = part if total is None else total + part
    count = frames * block
    width = sums_ref.shape[3]
    for x in range(los):
        for clip in range(clips):
            piece = total[clip * count : (clip + 1) * count, x * width : (x + 1) * width]
            sums_ref[x, clip] = piece.astype(sums_ref.dtype)


def norm_kernel(side_ref, conv_ref, gain_ref, shift_ref, tiles_ref):
    spaces, frames, rows, cols, depth = conv_ref.shape
    owners, reach = tiles_ref.shape[0], tiles_ref.shape[1]
    side = side_ref[0]
    group = C // GROUPS
    values = conv_ref[...].astype(jnp.float32)
    flat = values.reshape(spaces * frames * rows * cols, depth)
    sums = jnp.sum(flat, axis=0, keepdims=True)
    squares = jnp.sum(flat * flat, axis=0, keepdims=True)
    lane = lax.broadcasted_iota(jnp.int32, (depth, depth), 0) // group
    other = lax.broadcasted_iota(jnp.int32, (depth, depth), 1) // group
    same = (lane == other).astype(jnp.float32)
    both = jnp.concatenate([sums, squares, jnp.zeros((6, depth), jnp.float32)], axis=0)
    both = jnp.dot(both, same, precision=lax.Precision.HIGHEST, preferred_element_type=jnp.float32)
    both = both / float(flat.shape[0] * group)
    mean, square = both[0:1], both[1:2]
    factor = lax.rsqrt(square - mean * mean + 1e-06)
    normed = (flat - mean) * factor * gain_ref[...] + shift_ref[...]
    active = (normed / (1.0 + jnp.exp(-normed))).reshape(values.shape)
    cells = {}
    for at in range(spaces):
        for row in range(rows):
            cells[at * rows + row] = jnp.swapaxes(active[at, :, row], 0, 1)
    width = cols // owners
    empty = jnp.zeros((frames, depth), jnp.float32)
    for i in range(reach):
        lower, upper = cells[i], cells[i + spaces * rows - reach]
        chosen = jnp.where(side > 0, upper, lower)
        for owner in range(owners):
            picked = []
            for j in range(owner * width - 1, (owner + 1) * width + 1):
                picked.append(chosen[j] if 0 <= j < cols else empty)
            tiles_ref[owner, i] = jnp.concatenate(picked, axis=0).astype(tiles_ref.dtype)


def up_kernel(side_ref, tiles_ref, weight_ref, bias_ref, out_ref, cells):
    chans, clips, los, reach, tall, depth = tiles_ref.shape
    frames = out_ref.shape[1]
    out_rows, out_cols = out_ref.shape[2], out_ref.shape[3]
    wide = tall // frames
    side = side_ref[0]
    edge = jnp.where(side > 0, reach, 0)
    cells[edge] = jnp.zeros(cells.shape[1:], cells.dtype)
    for i in range(reach):
        for j in range(wide):
            parts = []
            for chan in range(chans):
                for x in range(los):
                    stack = [
                        tiles_ref[chan, clip, x, i, j * frames : (j + 1) * frames].astype(jnp.float32)
                        for clip in range(clips)
                    ]
                    parts.append(jnp.concatenate(stack, axis=0))
            cells[i + 1 - side, j] = jnp.concatenate(parts, axis=1).astype(cells.dtype)
    total = None
    for b in range(3):
        for e in range(3):
            left = jnp.concatenate(
                [
                    cells[(r - 1 + b) // 2 + 1, (q - 1 + e) // 2 + 1]
                    for r in range(out_rows)
                    for q in range(out_cols)
                ],
                axis=0,
            )
            part = jnp.dot(left, weight_ref[b, e], preferred_element_type=jnp.float32)
            total = part if total is None else total + part
    total = total + bias_ref[...]
    total = total.reshape(out_rows * out_cols, clips, frames, total.shape[1])
    span = frames // (clips * los)
    for clip in range(clips):
        turned = jnp.swapaxes(total[:, clip], 0, 1).astype(out_ref.dtype)
        for k in range(frames):
            slot = (k + clip * span) % frames
            for r in range(out_rows):
                out_ref[clip, slot, r] = turned[k, r * out_cols : (r + 1) * out_cols]


def whole_vmem():
    return pl.BlockSpec(memory_space=pltpu.VMEM)


def in_smem():
    return pl.BlockSpec(memory_space=pltpu.SMEM)


def swap(value, axis):
    return lax.all_to_all(value, axis, split_axis=0, concat_axis=0, tiled=True)


def small_plan(latents, conv_weight, conv_bias, gn_gain, gn_shift, up_weight, up_bias):
    clips, span, rows, cols, half = latents.shape
    his, los = lax.axis_size("tm_hi"), lax.axis_size("tm_lo")
    spaces, chans = lax.axis_size("space"), lax.axis_size("chan")
    spans = his * los
    frames, width, depth = span * spans, cols // spans, half // los
    side = lax.axis_index("space").astype(jnp.int32).reshape(1)
    x = lax.axis_index("tm_lo")

    split = latents.reshape(clips, span, rows, cols, los, depth).transpose(4, 0, 1, 2, 3, 5)
    both = lax.all_gather(split[None], "chan", axis=0, tiled=True)
    both = swap(both, "tm_hi")
    both = swap(both.swapaxes(0, 1), "tm_lo").swapaxes(0, 1)
    every = lax.all_gather(both, "space")
    sums = pl.pallas_call(
        conv_kernel,
        out_shape=jax.ShapeDtypeStruct((los, clips, frames * rows * cols, depth), jnp.float32),
        in_specs=[in_smem(), whole_vmem(), whole_vmem()],
        out_specs=whole_vmem(),
        scratch_shapes=[pltpu.VMEM((clips, (frames + 2) * rows * cols, 9 * depth), jnp.bfloat16)],
        compiler_params=pltpu.CompilerParams(vmem_limit_bytes=16 << 20),
    )(side, every, conv_weight)
    sums = jnp.sum(swap(sums, "tm_lo"), axis=0)
    sums = jnp.sum(swap(sums, "tm_hi"), axis=0)

    def block_of(vector):
        return lax.dynamic_slice_in_dim(vector, x * depth, depth)[None]

    conved = (sums + block_of(conv_bias)).astype(jnp.bfloat16)
    conved = lax.all_gather(conved, "space").reshape(spaces, frames, rows, cols, depth)
    tiles = pl.pallas_call(
        norm_kernel,
        out_shape=jax.ShapeDtypeStruct((spans, rows + 1, (width + 2) * frames, depth), jnp.bfloat16),
        in_specs=[in_smem(), whole_vmem(), whole_vmem(), whole_vmem()],
        out_specs=whole_vmem(),
        compiler_params=pltpu.CompilerParams(vmem_limit_bytes=16 << 20),
    )(side, conved, block_of(gn_gain), block_of(gn_shift))
    tiles = tiles.reshape((his, los) + tiles.shape[1:])
    tiles = swap(tiles, "tm_hi")
    tiles = swap(tiles.swapaxes(0, 1), "tm_lo").swapaxes(0, 1)
    tiles = lax.all_gather(tiles, "chan")
    return pl.pallas_call(
        up_kernel,
        out_shape=jax.ShapeDtypeStruct((clips, frames, 2 * rows, 2 * width, half), jnp.bfloat16),
        in_specs=[in_smem(), whole_vmem(), whole_vmem(), whole_vmem()],
        out_specs=whole_vmem(),
        scratch_shapes=[pltpu.VMEM((rows + 2, width + 2, clips * frames, C), jnp.bfloat16)],
        compiler_params=pltpu.CompilerParams(vmem_limit_bytes=16 << 20),
    )(side, tiles, up_weight, up_bias[None])


def solution(mesh):
    sizes = dict(mesh.shape)
    small = sizes["tm"] == 4 and sizes["space"] == 2 and sizes["chan"] == 2
    if small:
        shape = (sizes["groups"], 2, 2, sizes["space"], sizes["chan"])
        mesh = Mesh(mesh.devices.reshape(shape), ("groups", "tm_hi", "tm_lo", "space", "chan"))
    tm = ("tm_hi", "tm_lo") if small else "tm"
    placed = (
        P("groups", tm, "space", None, "chan"),
        P(None, None, None, tm, "chan"),
        P("chan"),
        P("chan"),
        P("chan"),
        P(None, None, None, "chan"),
        P("chan"),
    )
    return jax.shard_map(
        small_plan if small else general_plan,
        mesh=mesh,
        in_specs=placed,
        out_specs=P("groups", None, "space", tm, "chan"),
        check_vma=False,
    )
```

```python
import jax
import jax.numpy as jnp
from jax import lax
from jax.experimental import pallas as pl
from jax.experimental.pallas import tpu as pltpu
from jax.sharding import PartitionSpec as P

C = 512
GROUPS = 32


def shifted(value, axis, step):
    count = lax.axis_size(axis)
    pairs = [(i, i + step) for i in range(count) if 0 <= i + step < count]
    return lax.ppermute(value, axis, pairs)


def rows_around(block, axis_rows, depth):
    low = shifted(lax.slice_in_dim(block, block.shape[axis_rows] - depth, None, axis=axis_rows), "space", 1)
    high = shifted(lax.slice_in_dim(block, 0, depth, axis=axis_rows), "space", -1)
    return jnp.concatenate([low, block, high], axis=axis_rows)


def input_slice(latents):
    clips, span, rows, cols, half = latents.shape
    spans, spaces, chans = lax.axis_size("tm"), lax.axis_size("space"), lax.axis_size("chan")
    me, row_block = lax.axis_index("tm"), lax.axis_index("space")
    depth = half * chans // spans
    per_half = half // depth
    if spaces == 2:
        whole = lax.all_gather(latents, ("tm", "space", "chan"))
        whole = whole.reshape(spans, spaces, chans, clips, span, rows, cols, per_half, depth)
        mine = lax.dynamic_index_in_dim(whole, me // per_half, axis=2, keepdims=False)
        mine = lax.dynamic_index_in_dim(mine, me % per_half, axis=7 - 1, keepdims=False)
        mine = mine.transpose(2, 0, 3, 1, 4, 5, 6).reshape(clips, spans * span, spaces * rows, cols, depth)
        mine = jnp.pad(mine, ((0, 0), (0, 0), (1, 1), (0, 0), (0, 0)))
        mine = lax.dynamic_slice_in_dim(mine, row_block * rows, rows + 2, axis=2)
    else:
        bordered = rows_around(latents, 2, 1)
        whole = lax.all_gather(bordered, ("tm", "chan"))
        whole = whole.reshape((spans, chans) + bordered.shape[:4] + (per_half, depth))
        mine = lax.dynamic_index_in_dim(whole, me // per_half, axis=1, keepdims=False)
        mine = lax.dynamic_index_in_dim(mine, me % per_half, axis=5, keepdims=False)
        mine = mine.transpose(1, 0, 2, 3, 4, 5).reshape(clips, spans * span, rows + 2, cols, depth)
    return jnp.stack([jnp.roll(mine[c], -c * span, axis=0) for c in range(clips)])


def general_plan(latents, conv_weight, conv_bias, gn_gain, gn_shift, up_weight, up_bias):
    clips, span, rows, cols, half = latents.shape
    spans, spaces, chans = lax.axis_size("tm"), lax.axis_size("space"), lax.axis_size("chan")
    me, row_block = lax.axis_index("tm"), lax.axis_index("space")
    frames, width = span * spans, cols // spans
    group_width = C // GROUPS

    mine = input_slice(latents)
    padded = jnp.pad(mine, ((0, 0), (2, 0), (0, 0), (1, 1), (0, 0)))
    partial = lax.conv_general_dilated(
        padded,
        conv_weight,
        (1, 1, 1),
        "VALID",
        dimension_numbers=("NDHWC", "DHWIO", "NDHWC"),
        preferred_element_type=jnp.float32,
    )
    partial = jnp.stack([jnp.roll(partial[c], c * span, axis=0) for c in range(clips)])
    parts = partial.reshape(clips, frames, rows, spans, width, half)
    parts = parts.transpose(3, 0, 1, 2, 4, 5)
    parts = lax.all_to_all(parts, "tm", split_axis=0, concat_axis=0, tiled=True)
    conved = (jnp.sum(parts, axis=0) + conv_bias).astype(jnp.bfloat16)

    values = conved.astype(jnp.float32).reshape(-1, half)
    values = values.reshape(clips, frames * rows * width, half // group_width, group_width)
    if spaces == 2:
        every = lax.all_gather(conved, ("tm", "space", "chan"))
        every = every.reshape(spans, spaces, chans, clips, frames, rows, width, half)
        every = every.transpose(3, 4, 1, 5, 0, 6, 2, 7).reshape(clips, frames, spaces * rows, cols, C)
        gain = lax.all_gather(gn_gain, "chan", tiled=True)
        shift = lax.all_gather(gn_shift, "chan", tiled=True)
        values = every.astype(jnp.float32).reshape(clips, -1, GROUPS, group_width)
        sums = jnp.sum(values, axis=(1, 3))
        squares = jnp.sum(values * values, axis=(1, 3))
        count = float(values.shape[1] * group_width)
        mean = sums / count
        factor = lax.rsqrt(squares / count - mean * mean + 1e-06)
        edged = jnp.pad(every, ((0, 0), (0, 0), (1, 1), (1, 1), (0, 0)))
        tile = lax.dynamic_slice(
            edged, (0, 0, row_block * rows, me * width, 0), (clips, frames, rows + 2, width + 2, C)
        )
    else:
        sums = jnp.sum(values, axis=(1, 3))
        squares = jnp.sum(values * values, axis=(1, 3))
        sums, squares = lax.psum((sums, squares), ("tm", "space"))
        count = float(values.shape[1] * group_width * spans * spaces)
        mean = sums / count
        factor = lax.rsqrt(squares / count - mean * mean + 1e-06)
        bordered = rows_around(conved, 2, 1)
        left = shifted(bordered[:, :, :, -1:], "tm", 1)
        right = shifted(bordered[:, :, :, :1], "tm", -1)
        tile = jnp.concatenate([left, bordered, right], axis=3)
        tile = lax.all_gather(tile, "chan", axis=4, tiled=True)
        gain, shift, mean, factor = (
            lax.all_gather(v, "chan", axis=v.ndim - 1, tiled=True) for v in (gn_gain, gn_shift, mean, factor)
        )
    mean = jnp.repeat(mean, group_width, axis=1)[:, None, None, None]
    factor = jnp.repeat(factor, group_width, axis=1)[:, None, None, None]
    normed = (tile.astype(jnp.float32) - mean) * factor * gain + shift
    row_at = row_block * rows - 1 + jnp.arange(rows + 2)
    col_at = me * width - 1 + jnp.arange(width + 2)
    inside = ((row_at >= 0) & (row_at < rows * spaces))[:, None] & ((col_at >= 0) & (col_at < cols))[None]
    active = jnp.where(inside[None, None, :, :, None], jax.nn.silu(normed), 0.0).astype(jnp.bfloat16)
    wide = jnp.repeat(jnp.repeat(active, 2, axis=2), 2, axis=3)[:, :, 1:-1, 1:-1]
    flat = wide.reshape((clips * frames,) + wide.shape[2:])
    output = lax.conv_general_dilated(
        flat,
        up_weight,
        (1, 1),
        "VALID",
        dimension_numbers=("NHWC", "HWIO", "NHWC"),
        preferred_element_type=jnp.float32,
    )
    output = (output + up_bias).astype(jnp.bfloat16)
    return output.reshape(clips, frames, 2 * rows, 2 * width, half)


def pack_kernel(place_ref, own_ref, other_ref, first_ref, second_ref):
    tm, side = place_ref[0], place_ref[1]
    depth = first_ref.shape[5]
    upper = (tm // 2) > 0
    for ref, at in ((own_ref, side), (other_ref, 1 - side)):
        low, high = ref[..., :depth], ref[..., depth:]
        first_ref[at] = jnp.where(upper, high, low)
        second_ref[at] = jnp.where(upper, low, high)


def conv_kernel(place_ref, *refs):
    got, (weight_ref, keep_ref), sent = refs[:4], refs[4:6], refs[6:9]
    latents, taps, tiles = refs[9:]
    spans, spaces, clips, span, rows, cols, depth = latents.shape
    frames, tall = spans * span, spaces * rows
    tm, chan = place_ref[0], place_ref[2]
    turn = 2 * (tm % 2) + chan
    for m in range(spans):
        latents[m ^ turn] = got[m][...].astype(jnp.float32)
    block = tall * cols
    lead = 2 * block
    column = lax.broadcasted_iota(jnp.int32, (1, 1, cols, depth), 2)
    empty = jnp.zeros((frames, cols, depth), jnp.float32)
    for clip in range(clips):
        taps[clip, :lead] = jnp.zeros((lead, taps.shape[2]), taps.dtype)
        lines = [empty]
        for at in range(spaces):
            for row in range(rows):
                parts = [latents[(j + clip) % spans, at, clip, :, row] for j in range(spans)]
                lines.append(jnp.concatenate(parts, axis=0))
        padded = jnp.stack(lines + [empty], axis=1)
        shifts = (
            jnp.where(column > 0, pltpu.roll(padded, 1, 2), 0.0),
            padded,
            jnp.where(column < cols - 1, pltpu.roll(padded, cols - 1, 2), 0.0),
        )
        for e in range(3):
            for b in range(3):
                piece = shifts[e][:, b : b + tall].reshape(frames * block, depth)
                at = (b * 3 + e) * depth
                taps[clip, lead:, at : at + depth] = piece.astype(taps.dtype)
    count = frames * block
    total = None
    for a in range(3):
        left = jnp.concatenate([taps[clip, a * block : a * block + count] for clip in range(clips)], axis=0)
        right = weight_ref[a].reshape(9 * depth, weight_ref.shape[4])
        part = jnp.dot(left, right, preferred_element_type=jnp.float32)
        total = part if total is None else total + part
    width = tiles.shape[2]
    los = spans // clips
    for clip in range(clips):
        for x in range(los):
            tiles[clip * los + x] = total[clip * count : (clip + 1) * count, x * width : (x + 1) * width]
    keep_ref[...] = tiles[tm]
    for m in range(1, spans):
        sent[m - 1][...] = tiles[tm ^ m].astype(sent[m - 1].dtype)


def norm_kernel(place_ref, *refs):
    partial, (bias_ref, gain_ref, shift_ref), sent = refs[:4], refs[4:7], refs[7:11]
    tiles = refs[11]
    tm, side = place_ref[0], place_ref[1]
    owners, reach, strip, depth = tiles.shape
    cols = 8
    frames = strip // (cols // owners + 2)
    tall = partial[0].shape[0] // (frames * cols)
    group = C // GROUPS
    block = pl.ds(tm % bias_ref.shape[0], 1)
    total = partial[0][...]
    for ref in partial[1:]:
        total = total + ref[...].astype(jnp.float32)
    flat = (total + bias_ref[block, :]).astype(jnp.bfloat16).astype(jnp.float32)
    sums = jnp.sum(flat, axis=0, keepdims=True)
    squares = jnp.sum(flat * flat, axis=0, keepdims=True)
    lane = lax.broadcasted_iota(jnp.int32, (depth, depth), 0) // group
    other = lax.broadcasted_iota(jnp.int32, (depth, depth), 1) // group
    same = (lane == other).astype(jnp.float32)
    both = jnp.concatenate([sums, squares, jnp.zeros((6, depth), jnp.float32)], axis=0)
    both = jnp.dot(both, same, precision=lax.Precision.HIGHEST, preferred_element_type=jnp.float32)
    both = both / float(flat.shape[0] * group)
    mean, square = both[0:1], both[1:2]
    factor = lax.rsqrt(square - mean * mean + 1e-06)
    normed = (flat - mean) * factor * gain_ref[block, :] + shift_ref[block, :]
    active = (normed / (1.0 + jnp.exp(-normed))).reshape(frames, tall, cols, depth)
    cells = [jnp.swapaxes(active[:, row], 0, 1) for row in range(tall)]
    width = cols // owners
    empty = jnp.zeros((frames, depth), jnp.float32)
    for i in range(reach):
        chosen = jnp.where(side > 0, cells[i + tall - reach], cells[i])
        for owner in range(owners):
            picked = []
            for j in range(owner * width - 1, (owner + 1) * width + 1):
                picked.append(chosen[j] if 0 <= j < cols else empty)
            tiles[owner, i] = jnp.concatenate(picked, axis=0).astype(tiles.dtype)
    for m in range(owners):
        sent[m][...] = tiles[tm ^ m]


def cells_kernel(place_ref, *refs):
    got, cells_ref, tiles = refs[:4], refs[4], refs[5]
    tm = place_ref[0]
    for m in range(len(got)):
        tiles[tm ^ m] = got[m][...].astype(jnp.float32)
    reach, wide, tall, half = cells_ref.shape
    depth = tiles.shape[3]
    los = half // depth
    clips = tiles.shape[0] // los
    frames = tall // clips
    for i in range(reach):
        for j in range(wide):
            for x in range(los):
                stack = [tiles[clip * los + x, i, j * frames : (j + 1) * frames] for clip in range(clips)]
                piece = jnp.concatenate(stack, axis=0).astype(cells_ref.dtype)
                cells_ref[i, j, :, x * depth : (x + 1) * depth] = piece


def taps_of(side, half, cells_ref, weight_ref, cells, out_rows, out_cols):
    reach, width = cells_ref.shape[0], cells_ref.shape[3]
    cells[jnp.where(side > 0, reach, 0)] = jnp.zeros(cells.shape[1:], cells.dtype)
    for i in range(reach):
        cells[i + 1 - side] = cells_ref[i]
    rows = pl.ds(pl.multiple_of(half * width, width), width)
    total = None
    for b in range(3):
        for e in range(3):
            left = jnp.concatenate(
                [
                    cells[(r - 1 + b) // 2 + 1, (q - 1 + e) // 2 + 1]
                    for r in range(out_rows)
                    for q in range(out_cols)
                ],
                axis=0,
            )
            part = jnp.dot(left, weight_ref[b, e, rows, :], preferred_element_type=jnp.float32)
            total = part if total is None else total + part
    return total


def near_kernel(place_ref, cells_ref, weight_ref, bias_ref, total_ref, cells):
    tall = cells_ref.shape[2]
    out_rows, out_cols = 2 * (cells_ref.shape[0] - 1), 2 * (cells_ref.shape[1] - 2)
    total = taps_of(place_ref[1], place_ref[2], cells_ref, weight_ref, cells, out_rows, out_cols)
    total_ref[...] = total + bias_ref[...]


def far_kernel(place_ref, cells_ref, weight_ref, total_ref, out_ref, cells):
    clips, frames, out_rows, out_cols, width = out_ref.shape
    total = taps_of(place_ref[1], 1 - place_ref[2], cells_ref, weight_ref, cells, out_rows, out_cols)
    total = (total + total_ref[...]).reshape(out_rows * out_cols, clips, frames, width)
    span = frames // 4
    for clip in range(clips):
        turned = jnp.swapaxes(total[:, clip], 0, 1).astype(out_ref.dtype)
        for k in range(frames):
            slot = (k + clip * span) % frames
            for r in range(out_rows):
                out_ref[clip, slot, r] = turned[k, r * out_cols : (r + 1) * out_cols]


def run(kernel, shapes, scratch, place, *operands, flops=0, moved=0):
    several = isinstance(shapes, (list, tuple))
    vmem = pl.BlockSpec(memory_space=pltpu.VMEM)
    return pl.pallas_call(
        kernel,
        out_shape=shapes,
        in_specs=[pl.BlockSpec(memory_space=pltpu.SMEM)] + [vmem] * len(operands),
        out_specs=[vmem] * len(shapes) if several else vmem,
        scratch_shapes=scratch,
        compiler_params=pltpu.CompilerParams(vmem_limit_bytes=16 << 20),
        cost_estimate=pl.CostEstimate(flops=flops, bytes_accessed=moved, transcendentals=0),
    )(place, *operands)


def small_plan(latents, conv_weight, conv_bias, gn_gain, gn_shift, up_weight, up_bias):
    clips, span, rows, cols, half = latents.shape
    spans, spaces, chans = lax.axis_size("tm"), lax.axis_size("space"), lax.axis_size("chan")
    los = spans // clips
    frames, tall, width, depth = span * spans, rows * spaces, cols // spans, half // los
    place = jnp.stack([lax.axis_index(axis) for axis in ("tm", "space", "chan")]).astype(jnp.int32)
    low, full = jnp.bfloat16, jnp.float32
    shape = jax.ShapeDtypeStruct
    flip = ((0, 1), (1, 0))

    other = lax.ppermute(latents, "space", flip)
    packed = shape((spaces,) + latents.shape[:4] + (depth,), low)
    pair = run(pack_kernel, [packed, packed], [], place, latents, other, moved=1 << 17)
    got = []
    for m in range(spans):
        pairs = []
        for source in range(spans):
            for chan in range(chans):
                turned = source ^ m
                target = 2 * chan + turned // 2
                pairs.append((source * chans + chan, target * chans + turned % 2))
        got.append(lax.ppermute(pair[m // 2], ("tm", "chan"), pairs))

    count = frames * tall * cols
    part = shape((count, depth), low)
    partial = run(
        conv_kernel,
        [shape((count, depth), full)] + [part] * (spans - 1),
        [
            pltpu.VMEM((spans,) + packed.shape, full),
            pltpu.VMEM((clips, count + 2 * tall * cols, 9 * depth), low),
            pltpu.VMEM((spans, count, depth), full),
        ],
        place,
        *got,
        conv_weight,
        flops=2 * clips * count * 27 * depth * half,
        moved=3 << 20,
    )
    partial = [partial[0]] + [
        lax.ppermute(partial[m], "tm", [(i, i ^ m) for i in range(spans)]) for m in range(1, spans)
    ]

    tile = shape((rows + 1, (width + 2) * frames, depth), low)
    tiles = run(
        norm_kernel,
        [tile] * spans,
        [pltpu.VMEM((spans,) + tile.shape, low)],
        place,
        *partial,
        *(vector.reshape(los, depth) for vector in (conv_bias, gn_gain, gn_shift)),
        moved=1 << 19,
    )
    tiles = [tiles[0]] + [
        lax.ppermute(tiles[m], "tm", [(i, i ^ m) for i in range(spans)]) for m in range(1, spans)
    ]

    near = run(
        cells_kernel,
        shape((rows + 1, width + 2, clips * frames, half), low),
        [pltpu.VMEM((spans,) + tile.shape, full)],
        place,
        *tiles,
        moved=1 << 18,
    )
    far = lax.ppermute(near, "chan", flip)
    cells = pltpu.VMEM((rows + 2,) + near.shape[1:], low)
    outputs = clips * frames * 4 * rows * width
    flops = 2 * outputs * 9 * half * half
    total = run(
        near_kernel, shape((outputs, half), full), [cells], place, near, up_weight, up_bias[None],
        flops=flops, moved=2 << 20,
    )
    return run(
        far_kernel, shape((clips, frames, 2 * rows, 2 * width, half), low), [cells], place, far, up_weight, total,
        flops=flops, moved=2 << 20,
    )


def solution(mesh):
    sizes = dict(mesh.shape)
    small = sizes["tm"] == 4 and sizes["space"] == 2 and sizes["chan"] == 2
    placed = (
        P("groups", "tm", "space", None, "chan"),
        P(None, None, None, "tm", "chan"),
        P("chan"),
        P("chan"),
        P("chan"),
        P(None, None, None, "chan"),
        P("chan"),
    )
    return jax.shard_map(
        small_plan if small else general_plan,
        mesh=mesh,
        in_specs=placed,
        out_specs=P("groups", None, "space", "tm", "chan"),
        check_vma=False,
    )
```

```python
import jax
import jax.numpy as jnp
from jax import lax
from jax.experimental import pallas as pl
from jax.experimental.pallas import tpu as pltpu
from jax.sharding import PartitionSpec as P

C = 512
GROUPS = 32


def shifted(value, axis, step):
    count = lax.axis_size(axis)
    pairs = [(i, i + step) for i in range(count) if 0 <= i + step < count]
    return lax.ppermute(value, axis, pairs)


def rows_around(block, axis_rows, depth):
    low = shifted(lax.slice_in_dim(block, block.shape[axis_rows] - depth, None, axis=axis_rows), "space", 1)
    high = shifted(lax.slice_in_dim(block, 0, depth, axis=axis_rows), "space", -1)
    return jnp.concatenate([low, block, high], axis=axis_rows)


def input_slice(latents):
    clips, span, rows, cols, half = latents.shape
    spans, spaces, chans = lax.axis_size("tm"), lax.axis_size("space"), lax.axis_size("chan")
    me, row_block = lax.axis_index("tm"), lax.axis_index("space")
    depth = half * chans // spans
    per_half = half // depth
    if spaces == 2:
        whole = lax.all_gather(latents, ("tm", "space", "chan"))
        whole = whole.reshape(spans, spaces, chans, clips, span, rows, cols, per_half, depth)
        mine = lax.dynamic_index_in_dim(whole, me // per_half, axis=2, keepdims=False)
        mine = lax.dynamic_index_in_dim(mine, me % per_half, axis=7 - 1, keepdims=False)
        mine = mine.transpose(2, 0, 3, 1, 4, 5, 6).reshape(clips, spans * span, spaces * rows, cols, depth)
        mine = jnp.pad(mine, ((0, 0), (0, 0), (1, 1), (0, 0), (0, 0)))
        mine = lax.dynamic_slice_in_dim(mine, row_block * rows, rows + 2, axis=2)
    else:
        bordered = rows_around(latents, 2, 1)
        whole = lax.all_gather(bordered, ("tm", "chan"))
        whole = whole.reshape((spans, chans) + bordered.shape[:4] + (per_half, depth))
        mine = lax.dynamic_index_in_dim(whole, me // per_half, axis=1, keepdims=False)
        mine = lax.dynamic_index_in_dim(mine, me % per_half, axis=5, keepdims=False)
        mine = mine.transpose(1, 0, 2, 3, 4, 5).reshape(clips, spans * span, rows + 2, cols, depth)
    return jnp.stack([jnp.roll(mine[c], -c * span, axis=0) for c in range(clips)])


def general_plan(latents, conv_weight, conv_bias, gn_gain, gn_shift, up_weight, up_bias):
    clips, span, rows, cols, half = latents.shape
    spans, spaces, chans = lax.axis_size("tm"), lax.axis_size("space"), lax.axis_size("chan")
    me, row_block = lax.axis_index("tm"), lax.axis_index("space")
    frames, width = span * spans, cols // spans
    group_width = C // GROUPS

    mine = input_slice(latents)
    padded = jnp.pad(mine, ((0, 0), (2, 0), (0, 0), (1, 1), (0, 0)))
    partial = lax.conv_general_dilated(
        padded,
        conv_weight,
        (1, 1, 1),
        "VALID",
        dimension_numbers=("NDHWC", "DHWIO", "NDHWC"),
        preferred_element_type=jnp.float32,
    )
    partial = jnp.stack([jnp.roll(partial[c], c * span, axis=0) for c in range(clips)])
    parts = partial.reshape(clips, frames, rows, spans, width, half)
    parts = parts.transpose(3, 0, 1, 2, 4, 5)
    parts = lax.all_to_all(parts, "tm", split_axis=0, concat_axis=0, tiled=True)
    conved = (jnp.sum(parts, axis=0) + conv_bias).astype(jnp.bfloat16)

    values = conved.astype(jnp.float32).reshape(-1, half)
    values = values.reshape(clips, frames * rows * width, half // group_width, group_width)
    if spaces == 2:
        every = lax.all_gather(conved, ("tm", "space", "chan"))
        every = every.reshape(spans, spaces, chans, clips, frames, rows, width, half)
        every = every.transpose(3, 4, 1, 5, 0, 6, 2, 7).reshape(clips, frames, spaces * rows, cols, C)
        gain = lax.all_gather(gn_gain, "chan", tiled=True)
        shift = lax.all_gather(gn_shift, "chan", tiled=True)
        values = every.astype(jnp.float32).reshape(clips, -1, GROUPS, group_width)
        sums = jnp.sum(values, axis=(1, 3))
        squares = jnp.sum(values * values, axis=(1, 3))
        count = float(values.shape[1] * group_width)
        mean = sums / count
        factor = lax.rsqrt(squares / count - mean * mean + 1e-06)
        edged = jnp.pad(every, ((0, 0), (0, 0), (1, 1), (1, 1), (0, 0)))
        tile = lax.dynamic_slice(
            edged, (0, 0, row_block * rows, me * width, 0), (clips, frames, rows + 2, width + 2, C)
        )
    else:
        sums = jnp.sum(values, axis=(1, 3))
        squares = jnp.sum(values * values, axis=(1, 3))
        sums, squares = lax.psum((sums, squares), ("tm", "space"))
        count = float(values.shape[1] * group_width * spans * spaces)
        mean = sums / count
        factor = lax.rsqrt(squares / count - mean * mean + 1e-06)
        bordered = rows_around(conved, 2, 1)
        left = shifted(bordered[:, :, :, -1:], "tm", 1)
        right = shifted(bordered[:, :, :, :1], "tm", -1)
        tile = jnp.concatenate([left, bordered, right], axis=3)
        tile = lax.all_gather(tile, "chan", axis=4, tiled=True)
        gain, shift, mean, factor = (
            lax.all_gather(v, "chan", axis=v.ndim - 1, tiled=True) for v in (gn_gain, gn_shift, mean, factor)
        )
    mean = jnp.repeat(mean, group_width, axis=1)[:, None, None, None]
    factor = jnp.repeat(factor, group_width, axis=1)[:, None, None, None]
    normed = (tile.astype(jnp.float32) - mean) * factor * gain + shift
    row_at = row_block * rows - 1 + jnp.arange(rows + 2)
    col_at = me * width - 1 + jnp.arange(width + 2)
    inside = ((row_at >= 0) & (row_at < rows * spaces))[:, None] & ((col_at >= 0) & (col_at < cols))[None]
    active = jnp.where(inside[None, None, :, :, None], jax.nn.silu(normed), 0.0).astype(jnp.bfloat16)
    wide = jnp.repeat(jnp.repeat(active, 2, axis=2), 2, axis=3)[:, :, 1:-1, 1:-1]
    flat = wide.reshape((clips * frames,) + wide.shape[2:])
    output = lax.conv_general_dilated(
        flat,
        up_weight,
        (1, 1),
        "VALID",
        dimension_numbers=("NHWC", "HWIO", "NHWC"),
        preferred_element_type=jnp.float32,
    )
    output = (output + up_bias).astype(jnp.bfloat16)
    return output.reshape(clips, frames, 2 * rows, 2 * width, half)


def placed_at():
    return lax.axis_index("tm"), lax.axis_index("space"), lax.axis_index("chan")


def fetch_kernel(latents_ref, weight_ref, token_ref):
    depth = token_ref.shape[1]
    token_ref[...] = latents_ref[:16, :depth] + weight_ref[0, 0, 0, :16, :depth]


def pack_kernel(own_ref, other_ref, token_ref, first_ref, second_ref):
    del token_ref
    tm, side, chan = placed_at()
    depth = first_ref.shape[2]
    home = (chan == tm // 2).astype(jnp.int32)
    upper = ((tm % 2) ^ home) > 0
    for ref, at in ((own_ref, side), (other_ref, 1 - side)):
        low, high = ref[:, :depth], ref[:, depth:]
        first_ref[at] = jnp.where(upper, high, low)
        second_ref[at] = jnp.where(upper, low, high)


def conv_kernel(own_ref, other_ref, weight_ref, keep_ref, *refs):
    sent, (latents, taps, tiles) = refs[:3], refs[3:]
    spans, spaces, clips, span, rows, cols, depth = latents.shape
    frames, tall = spans * span, spaces * rows
    tm, _, chan = placed_at()
    home = chan == tm // 2
    near, far = jnp.where(home, 0, 2), jnp.where(home, 2, 0)
    for ref, turn in ((own_ref, near), (other_ref, far)):
        first = jnp.where(turn > 0, tm ^ 2, tm ^ 1)
        second = jnp.where(turn > 0, tm ^ 3, tm)
        latents[first] = ref[0].astype(jnp.float32).reshape(latents.shape[1:])
        latents[second] = ref[1].astype(jnp.float32).reshape(latents.shape[1:])
    column = lax.broadcasted_iota(jnp.int32, (1, cols, depth), 1)
    taps[0] = jnp.zeros(taps.shape[1:], taps.dtype)
    taps[tall + 1] = jnp.zeros(taps.shape[1:], taps.dtype)
    for at in range(spaces):
        for row in range(rows):
            line = at * rows + row + 1
            taps[line, :2] = jnp.zeros((2,) + taps.shape[2:], taps.dtype)
            shifts = [[], [], []]
            for clip in range(clips):
                parts = [latents[(j + clip) % spans, at, clip, :, row] for j in range(spans)]
                value = jnp.concatenate(parts, axis=0)
                shifts[0].append(jnp.where(column > 0, pltpu.roll(value, 1, 1), 0.0))
                shifts[1].append(value)
                shifts[2].append(jnp.where(column < cols - 1, pltpu.roll(value, cols - 1, 1), 0.0))
            for e in range(3):
                piece = jnp.concatenate(shifts[e], axis=1).astype(taps.dtype)
                taps[line, 2:, :, e * depth : (e + 1) * depth] = piece
    count = frames * tall * cols
    total = None
    for a in range(3):
        lines = [taps[b : b + tall, a : a + frames].reshape(clips * count, 3 * depth) for b in range(3)]
        right = weight_ref[a].reshape(9 * depth, weight_ref.shape[4])
        part = jnp.dot(jnp.concatenate(lines, axis=1), right, preferred_element_type=jnp.float32)
        total = part if total is None else total + part
    width = tiles.shape[2]
    los = spans // clips
    total = total.reshape(tall * frames, clips, cols, total.shape[1])
    for clip in range(clips):
        for x in range(los):
            tiles[clip * los + x] = total[:, clip, :, x * width : (x + 1) * width].reshape(count, width)
    keep_ref[...] = tiles[tm]
    for m in range(1, spans):
        sent[m - 1][...] = tiles[tm ^ m].astype(sent[m - 1].dtype)


def norm_kernel(*refs):
    partial, (bias_ref, gain_ref, shift_ref), sent = refs[:4], refs[4:7], refs[7:11]
    tiles = refs[11]
    tm, side, _ = placed_at()
    owners, reach, strip, depth = tiles.shape
    cols = 8
    frames = strip // (cols // owners + 2)
    tall = partial[0].shape[0] // (frames * cols)
    group = C // GROUPS
    block = pl.ds(tm % bias_ref.shape[0], 1)
    total = partial[0][...]
    for ref in partial[1:]:
        total = total + ref[...].astype(jnp.float32)
    flat = (total + bias_ref[block, :]).astype(jnp.bfloat16).astype(jnp.float32)
    sums = jnp.sum(flat, axis=0, keepdims=True)
    squares = jnp.sum(flat * flat, axis=0, keepdims=True)
    lane = lax.broadcasted_iota(jnp.int32, (depth, depth), 0) // group
    other = lax.broadcasted_iota(jnp.int32, (depth, depth), 1) // group
    same = (lane == other).astype(jnp.float32)
    both = jnp.concatenate([sums, squares, jnp.zeros((6, depth), jnp.float32)], axis=0)
    both = jnp.dot(both, same, precision=lax.Precision.HIGHEST, preferred_element_type=jnp.float32)
    both = both / float(flat.shape[0] * group)
    mean, square = both[0:1], both[1:2]
    factor = lax.rsqrt(square - mean * mean + 1e-06)
    normed = (flat - mean) * factor * gain_ref[block, :] + shift_ref[block, :]
    active = (normed / (1.0 + jnp.exp(-normed))).reshape(tall, frames, cols, depth)
    cells = [jnp.swapaxes(active[row], 0, 1) for row in range(tall)]
    width = cols // owners
    empty = jnp.zeros((frames, depth), jnp.float32)
    for i in range(reach):
        chosen = jnp.where(side > 0, cells[i + tall - reach], cells[i])
        for owner in range(owners):
            picked = []
            for j in range(owner * width - 1, (owner + 1) * width + 1):
                picked.append(chosen[j] if 0 <= j < cols else empty)
            tiles[owner, i] = jnp.concatenate(picked, axis=0).astype(tiles.dtype)
    for m in range(owners):
        sent[m][...] = tiles[tm ^ m]


def cells_kernel(*refs):
    got, cells_ref, tiles = refs[:4], refs[4], refs[5]
    tm, _, _ = placed_at()
    for m in range(len(got)):
        tiles[tm ^ m] = got[m][...].astype(jnp.float32)
    reach, wide, tall, half = cells_ref.shape
    depth = tiles.shape[3]
    los = half // depth
    clips = tiles.shape[0] // los
    frames = tall // clips
    for i in range(reach):
        for j in range(wide):
            for x in range(los):
                stack = [tiles[clip * los + x, i, j * frames : (j + 1) * frames] for clip in range(clips)]
                piece = jnp.concatenate(stack, axis=0).astype(cells_ref.dtype)
                cells_ref[i, j, :, x * depth : (x + 1) * depth] = piece


def taps_of(side, half, cells_ref, weight_ref, cells, out_rows, out_cols):
    reach, width = cells_ref.shape[0], cells_ref.shape[3]
    cells[jnp.where(side > 0, reach, 0)] = jnp.zeros(cells.shape[1:], cells.dtype)
    for i in range(reach):
        cells[i + 1 - side] = cells_ref[i]
    rows = pl.ds(pl.multiple_of(half * width, width), width)
    total = None
    for b in range(3):
        lines = []
        for e in range(3):
            pieces = [
                cells[(r - 1 + b) // 2 + 1, (q - 1 + e) // 2 + 1]
                for r in range(out_rows)
                for q in range(out_cols)
            ]
            lines.append(jnp.concatenate(pieces, axis=0))
        right = jnp.concatenate([weight_ref[b, e, rows, :] for e in range(3)], axis=0)
        part = jnp.dot(jnp.concatenate(lines, axis=1), right, preferred_element_type=jnp.float32)
        total = part if total is None else total + part
    return total


def near_kernel(cells_ref, weight_ref, bias_ref, total_ref, cells):
    _, side, chan = placed_at()
    out_rows, out_cols = 2 * (cells_ref.shape[0] - 1), 2 * (cells_ref.shape[1] - 2)
    total = taps_of(side, chan, cells_ref, weight_ref, cells, out_rows, out_cols)
    total_ref[...] = total + bias_ref[...]


def far_kernel(cells_ref, weight_ref, total_ref, out_ref, cells):
    _, side, chan = placed_at()
    clips, frames, out_rows, out_cols, width = out_ref.shape
    total = taps_of(side, 1 - chan, cells_ref, weight_ref, cells, out_rows, out_cols)
    total = (total + total_ref[...]).reshape(out_rows * out_cols, clips, frames, width)
    span = frames // 4
    for clip in range(clips):
        turned = jnp.swapaxes(total[:, clip], 0, 1).astype(out_ref.dtype)
        for k in range(frames):
            slot = (k + clip * span) % frames
            for r in range(out_rows):
                out_ref[clip, slot, r] = turned[k, r * out_cols : (r + 1) * out_cols]


def run(kernel, shapes, scratch, *operands, flops=0, moved=0):
    several = isinstance(shapes, (list, tuple))
    vmem = pl.BlockSpec(memory_space=pltpu.VMEM)
    return pl.pallas_call(
        kernel,
        out_shape=shapes,
        in_specs=[vmem] * len(operands),
        out_specs=[vmem] * len(shapes) if several else vmem,
        scratch_shapes=scratch,
        compiler_params=pltpu.CompilerParams(vmem_limit_bytes=16 << 20),
        cost_estimate=pl.CostEstimate(flops=flops, bytes_accessed=moved, transcendentals=0),
    )(*operands)


def small_plan(latents, conv_weight, conv_bias, gn_gain, gn_shift, up_weight, up_bias):
    clips, span, rows, cols, half = latents.shape
    spans, spaces, chans = lax.axis_size("tm"), lax.axis_size("space"), lax.axis_size("chan")
    los = spans // clips
    frames, tall, width, depth = span * spans, rows * spaces, cols // spans, half // los
    low, full = jnp.bfloat16, jnp.float32
    shape = jax.ShapeDtypeStruct
    flip = ((0, 1), (1, 0))

    cells_in = latents.reshape(clips * span * rows * cols, half)
    other = lax.ppermute(cells_in, "space", flip)
    token = run(
        fetch_kernel,
        shape((16, depth), low),
        [],
        cells_in,
        conv_weight,
        moved=4 << 20,
    )
    packed = shape((spaces, cells_in.shape[0], depth), low)
    pair = run(pack_kernel, [packed, packed], [], cells_in, other, token, moved=1 << 17)
    turns = ((1, 2), (0, 3))
    got = []
    for block, (at_home, across) in zip(pair, turns):
        pairs = []
        for source in range(spans):
            for chan in range(chans):
                home = chan == source // 2
                target = (source ^ at_home, chan) if home else (source ^ across, 1 - chan)
                pairs.append((source * chans + chan, target[0] * chans + target[1]))
        got.append(lax.ppermute(block, ("tm", "chan"), pairs))
    got = jnp.stack(got)
    core = lax.ppermute(got, "chan", flip)

    count = frames * tall * cols
    part = shape((count, depth), low)
    partial = run(
        conv_kernel,
        [shape((count, depth), full)] + [part] * (spans - 1),
        [
            pltpu.VMEM((spans, spaces, clips, span, rows, cols, depth), full),
            pltpu.VMEM((tall + 2, frames + 2, clips * cols, 3 * depth), low),
            pltpu.VMEM((spans, count, depth), full),
        ],
        got,
        core,
        conv_weight,
        flops=2 * clips * count * 27 * depth * half,
        moved=3 << 20,
    )
    partial = [partial[0]] + [
        lax.ppermute(partial[m], "tm", [(i, i ^ m) for i in range(spans)]) for m in range(1, spans)
    ]

    tile = shape((rows + 1, (width + 2) * frames, depth), low)
    tiles = run(
        norm_kernel,
        [tile] * spans,
        [pltpu.VMEM((spans,) + tile.shape, low)],
        *partial,
        *(vector.reshape(los, depth) for vector in (conv_bias, gn_gain, gn_shift)),
        moved=1 << 19,
    )
    tiles = [tiles[0]] + [
        lax.ppermute(tiles[m], "tm", [(i, i ^ m) for i in range(spans)]) for m in range(1, spans)
    ]

    near = run(
        cells_kernel,
        shape((rows + 1, width + 2, clips * frames, half), low),
        [pltpu.VMEM((spans,) + tile.shape, full)],
        *tiles,
        moved=1 << 18,
    )
    far = lax.ppermute(near, "chan", flip)
    cells = pltpu.VMEM((rows + 2,) + near.shape[1:], low)
    outputs = clips * frames * 4 * rows * width
    flops = 2 * outputs * 9 * half * half
    total = run(
        near_kernel, shape((outputs, half), full), [cells], near, up_weight, up_bias[None],
        flops=flops, moved=2 << 20,
    )
    return run(
        far_kernel, shape((clips, frames, 2 * rows, 2 * width, half), low), [cells], far, up_weight, total,
        flops=flops, moved=2 << 20,
    )


def solution(mesh):
    sizes = dict(mesh.shape)
    small = sizes["tm"] == 4 and sizes["space"] == 2 and sizes["chan"] == 2
    placed = (
        P("groups", "tm", "space", None, "chan"),
        P(None, None, None, "tm", "chan"),
        P("chan"),
        P("chan"),
        P("chan"),
        P(None, None, None, "chan"),
        P("chan"),
    )
    return jax.shard_map(
        small_plan if small else general_plan,
        mesh=mesh,
        in_specs=placed,
        out_specs=P("groups", None, "space", "tm", "chan"),
        check_vma=False,
    )
```

```python
import jax
import jax.numpy as jnp
from jax import lax
from jax.experimental import pallas as pl
from jax.experimental.pallas import tpu as pltpu
from jax.sharding import PartitionSpec as P

C = 512
GROUPS = 32


def shifted(value, axis, step):
    count = lax.axis_size(axis)
    pairs = [(i, i + step) for i in range(count) if 0 <= i + step < count]
    return lax.ppermute(value, axis, pairs)


def rows_around(block, axis_rows, depth):
    low = shifted(lax.slice_in_dim(block, block.shape[axis_rows] - depth, None, axis=axis_rows), "space", 1)
    high = shifted(lax.slice_in_dim(block, 0, depth, axis=axis_rows), "space", -1)
    return jnp.concatenate([low, block, high], axis=axis_rows)


def input_slice(latents):
    clips, span, rows, cols, half = latents.shape
    spans, spaces, chans = lax.axis_size("tm"), lax.axis_size("space"), lax.axis_size("chan")
    me, row_block = lax.axis_index("tm"), lax.axis_index("space")
    depth = half * chans // spans
    per_half = half // depth
    if spaces == 2:
        whole = lax.all_gather(latents, ("tm", "space", "chan"))
        whole = whole.reshape(spans, spaces, chans, clips, span, rows, cols, per_half, depth)
        mine = lax.dynamic_index_in_dim(whole, me // per_half, axis=2, keepdims=False)
        mine = lax.dynamic_index_in_dim(mine, me % per_half, axis=7 - 1, keepdims=False)
        mine = mine.transpose(2, 0, 3, 1, 4, 5, 6).reshape(clips, spans * span, spaces * rows, cols, depth)
        mine = jnp.pad(mine, ((0, 0), (0, 0), (1, 1), (0, 0), (0, 0)))
        mine = lax.dynamic_slice_in_dim(mine, row_block * rows, rows + 2, axis=2)
    else:
        bordered = rows_around(latents, 2, 1)
        whole = lax.all_gather(bordered, ("tm", "chan"))
        whole = whole.reshape((spans, chans) + bordered.shape[:4] + (per_half, depth))
        mine = lax.dynamic_index_in_dim(whole, me // per_half, axis=1, keepdims=False)
        mine = lax.dynamic_index_in_dim(mine, me % per_half, axis=5, keepdims=False)
        mine = mine.transpose(1, 0, 2, 3, 4, 5).reshape(clips, spans * span, rows + 2, cols, depth)
    return jnp.stack([jnp.roll(mine[c], -c * span, axis=0) for c in range(clips)])


def general_plan(latents, conv_weight, conv_bias, gn_gain, gn_shift, up_weight, up_bias):
    clips, span, rows, cols, half = latents.shape
    spans, spaces, chans = lax.axis_size("tm"), lax.axis_size("space"), lax.axis_size("chan")
    me, row_block = lax.axis_index("tm"), lax.axis_index("space")
    frames, width = span * spans, cols // spans
    group_width = C // GROUPS

    mine = input_slice(latents)
    padded = jnp.pad(mine, ((0, 0), (2, 0), (0, 0), (1, 1), (0, 0)))
    partial = lax.conv_general_dilated(
        padded,
        conv_weight,
        (1, 1, 1),
        "VALID",
        dimension_numbers=("NDHWC", "DHWIO", "NDHWC"),
        preferred_element_type=jnp.float32,
    )
    partial = jnp.stack([jnp.roll(partial[c], c * span, axis=0) for c in range(clips)])
    parts = partial.reshape(clips, frames, rows, spans, width, half)
    parts = parts.transpose(3, 0, 1, 2, 4, 5)
    parts = lax.all_to_all(parts, "tm", split_axis=0, concat_axis=0, tiled=True)
    conved = (jnp.sum(parts, axis=0) + conv_bias).astype(jnp.bfloat16)

    values = conved.astype(jnp.float32).reshape(-1, half)
    values = values.reshape(clips, frames * rows * width, half // group_width, group_width)
    if spaces == 2:
        every = lax.all_gather(conved, ("tm", "space", "chan"))
        every = every.reshape(spans, spaces, chans, clips, frames, rows, width, half)
        every = every.transpose(3, 4, 1, 5, 0, 6, 2, 7).reshape(clips, frames, spaces * rows, cols, C)
        gain = lax.all_gather(gn_gain, "chan", tiled=True)
        shift = lax.all_gather(gn_shift, "chan", tiled=True)
        values = every.astype(jnp.float32).reshape(clips, -1, GROUPS, group_width)
        sums = jnp.sum(values, axis=(1, 3))
        squares = jnp.sum(values * values, axis=(1, 3))
        count = float(values.shape[1] * group_width)
        mean = sums / count
        factor = lax.rsqrt(squares / count - mean * mean + 1e-06)
        edged = jnp.pad(every, ((0, 0), (0, 0), (1, 1), (1, 1), (0, 0)))
        tile = lax.dynamic_slice(
            edged, (0, 0, row_block * rows, me * width, 0), (clips, frames, rows + 2, width + 2, C)
        )
    else:
        sums = jnp.sum(values, axis=(1, 3))
        squares = jnp.sum(values * values, axis=(1, 3))
        sums, squares = lax.psum((sums, squares), ("tm", "space"))
        count = float(values.shape[1] * group_width * spans * spaces)
        mean = sums / count
        factor = lax.rsqrt(squares / count - mean * mean + 1e-06)
        bordered = rows_around(conved, 2, 1)
        left = shifted(bordered[:, :, :, -1:], "tm", 1)
        right = shifted(bordered[:, :, :, :1], "tm", -1)
        tile = jnp.concatenate([left, bordered, right], axis=3)
        tile = lax.all_gather(tile, "chan", axis=4, tiled=True)
        gain, shift, mean, factor = (
            lax.all_gather(v, "chan", axis=v.ndim - 1, tiled=True) for v in (gn_gain, gn_shift, mean, factor)
        )
    mean = jnp.repeat(mean, group_width, axis=1)[:, None, None, None]
    factor = jnp.repeat(factor, group_width, axis=1)[:, None, None, None]
    normed = (tile.astype(jnp.float32) - mean) * factor * gain + shift
    row_at = row_block * rows - 1 + jnp.arange(rows + 2)
    col_at = me * width - 1 + jnp.arange(width + 2)
    inside = ((row_at >= 0) & (row_at < rows * spaces))[:, None] & ((col_at >= 0) & (col_at < cols))[None]
    active = jnp.where(inside[None, None, :, :, None], jax.nn.silu(normed), 0.0).astype(jnp.bfloat16)
    wide = jnp.repeat(jnp.repeat(active, 2, axis=2), 2, axis=3)[:, :, 1:-1, 1:-1]
    flat = wide.reshape((clips * frames,) + wide.shape[2:])
    output = lax.conv_general_dilated(
        flat,
        up_weight,
        (1, 1),
        "VALID",
        dimension_numbers=("NHWC", "HWIO", "NHWC"),
        preferred_element_type=jnp.float32,
    )
    output = (output + up_bias).astype(jnp.bfloat16)
    return output.reshape(clips, frames, 2 * rows, 2 * width, half)


def placed_at():
    return lax.axis_index("tm"), lax.axis_index("space"), lax.axis_index("chan")


def fetch_kernel(weight_ref, weight_out, sem):
    copy = pltpu.make_async_copy(weight_ref, weight_out, sem)
    copy.start()
    copy.wait()


def select_kernel(first_ref, second_ref, after_ref, out_ref):
    del after_ref
    tm, _, _ = placed_at()
    depth = out_ref.shape[2]
    upper = tm % 2 > 0
    for i, ref in enumerate((first_ref, second_ref)):
        out_ref[i] = jnp.where(upper, ref[:, depth:], ref[:, :depth])


def conv_of_clip(clip, got, weight_ref, latents, taps):
    spans, spaces, span, rows, cols, depth = latents.shape
    frames, tall = spans * span, spaces * rows
    tm, side, chan = placed_at()
    size = span * rows * cols
    part = pl.ds(pl.multiple_of(clip * size, size), size)
    for i, ref in enumerate(got):
        at = side if i < 2 else 1 - side
        home = (chan if i % 2 == 0 else 1 - chan) == tm // 2
        for j, source in enumerate((jnp.where(home, tm ^ 1, tm ^ 2), jnp.where(home, tm, tm ^ 3))):
            latents[source, at] = ref[j, part, :].astype(jnp.float32).reshape(latents.shape[2:])
    column = lax.broadcasted_iota(jnp.int32, (1, cols, depth), 1)
    empty = jnp.zeros((frames, cols, depth), jnp.float32)
    lines = [[empty] * 3]
    for at in range(spaces):
        for row in range(rows):
            parts = [latents[(j + clip) % spans, at, :, row] for j in range(spans)]
            value = jnp.concatenate(parts, axis=0)
            lower = jnp.where(column > 0, pltpu.roll(value, 1, 1), 0.0)
            upper = jnp.where(column < cols - 1, pltpu.roll(value, cols - 1, 1), 0.0)
            lines.append([lower, value, upper])
    lines.append([empty] * 3)
    short = tall // 2
    for line in range(short + 2):
        taps[line, :2] = jnp.zeros((2,) + taps.shape[2:], taps.dtype)
        for e in range(3):
            piece = jnp.concatenate([lines[line][e], lines[line + short][e]], axis=1)
            taps[line, 2:, :, e * depth : (e + 1) * depth] = piece.astype(taps.dtype)
    total = None
    for a in range(3):
        wide = [taps[b : b + short, a : a + frames].reshape(frames * tall * cols, 3 * depth) for b in range(3)]
        right = weight_ref[a].reshape(9 * depth, weight_ref.shape[4])
        product = jnp.dot(jnp.concatenate(wide, axis=1), right, preferred_element_type=jnp.float32)
        total = product if total is None else total + product
    width = total.shape[1] // 2
    swapped = tm % 2 > 0
    lower, upper = total[:, :width], total[:, width:]
    return jnp.where(swapped, upper, lower), jnp.where(swapped, lower, upper)


def conv_far_kernel(own_ref, core_ref, row_ref, both_ref, weight_ref, same_ref, other_ref, latents, taps):
    tm, _, _ = placed_at()
    got = (own_ref, core_ref, row_ref, both_ref)
    same, other = conv_of_clip(1 - tm // 2, got, weight_ref, latents, taps)
    same_ref[...] = same.astype(same_ref.dtype)
    other_ref[...] = other.astype(other_ref.dtype)


def conv_near_kernel(own_ref, core_ref, row_ref, both_ref, weight_ref, keep_ref, other_ref, latents, taps):
    tm, _, _ = placed_at()
    got = (own_ref, core_ref, row_ref, both_ref)
    keep, other = conv_of_clip(tm // 2, got, weight_ref, latents, taps)
    keep_ref[...] = keep
    other_ref[...] = other.astype(other_ref.dtype)


def norm_kernel(*refs):
    partial, (bias_ref, gain_ref, shift_ref), sent = refs[:4], refs[4:7], refs[7:11]
    tiles = refs[11]
    tm, side, _ = placed_at()
    owners, reach, strip, depth = tiles.shape
    cols = 8
    frames = strip // (cols // owners + 2)
    tall = partial[0].shape[0] // (frames * cols)
    group = C // GROUPS
    block = pl.ds(tm % bias_ref.shape[0], 1)
    total = partial[0][...]
    for ref in partial[1:]:
        total = total + ref[...].astype(jnp.float32)
    flat = (total + bias_ref[block, :]).astype(jnp.bfloat16).astype(jnp.float32)
    sums = jnp.sum(flat, axis=0, keepdims=True)
    squares = jnp.sum(flat * flat, axis=0, keepdims=True)
    lane = lax.broadcasted_iota(jnp.int32, (depth, depth), 0) // group
    other = lax.broadcasted_iota(jnp.int32, (depth, depth), 1) // group
    same = (lane == other).astype(jnp.float32)
    both = jnp.concatenate([sums, squares, jnp.zeros((6, depth), jnp.float32)], axis=0)
    both = jnp.dot(both, same, precision=lax.Precision.HIGHEST, preferred_element_type=jnp.float32)
    both = both / float(flat.shape[0] * group)
    mean, square = both[0:1], both[1:2]
    factor = lax.rsqrt(square - mean * mean + 1e-06)
    normed = (flat - mean) * factor * gain_ref[block, :] + shift_ref[block, :]
    active = (normed / (1.0 + jnp.exp(-normed))).reshape(tall // 2, frames, 2, cols, depth)
    short = tall // 2
    cells = [jnp.swapaxes(active[row % short, :, row // short], 0, 1) for row in range(tall)]
    width = cols // owners
    empty = jnp.zeros((frames, depth), jnp.float32)
    for i in range(reach):
        chosen = jnp.where(side > 0, cells[i + tall - reach], cells[i])
        for owner in range(owners):
            picked = []
            for j in range(owner * width - 1, (owner + 1) * width + 1):
                picked.append(chosen[j] if 0 <= j < cols else empty)
            tiles[owner, i] = jnp.concatenate(picked, axis=0).astype(tiles.dtype)
    for m in range(owners):
        sent[m][...] = tiles[tm ^ m]


def cells_kernel(*refs):
    got, cells_ref, tiles = refs[:4], refs[4], refs[5]
    tm, _, _ = placed_at()
    for m in range(len(got)):
        tiles[tm ^ m] = got[m][...].astype(jnp.float32)
    reach, wide, tall, half = cells_ref.shape
    depth = tiles.shape[3]
    los = half // depth
    clips = tiles.shape[0] // los
    frames = tall // clips
    for i in range(reach):
        for j in range(wide):
            for x in range(los):
                stack = [tiles[clip * los + x, i, j * frames : (j + 1) * frames] for clip in range(clips)]
                piece = jnp.concatenate(stack, axis=0).astype(cells_ref.dtype)
                cells_ref[i, j, :, x * depth : (x + 1) * depth] = piece


def taps_of(side, half, cells_ref, weight_ref, cells, out_rows, out_cols):
    reach, width = cells_ref.shape[0], cells_ref.shape[3]
    cells[jnp.where(side > 0, reach, 0)] = jnp.zeros(cells.shape[1:], cells.dtype)
    for i in range(reach):
        cells[i + 1 - side] = cells_ref[i]
    rows = pl.ds(pl.multiple_of(half * width, width), width)
    total = None
    for b in range(3):
        lines = []
        for e in range(3):
            pieces = [
                cells[(r - 1 + b) // 2 + 1, (q - 1 + e) // 2 + 1]
                for r in range(out_rows)
                for q in range(out_cols)
            ]
            lines.append(jnp.concatenate(pieces, axis=0))
        right = jnp.concatenate([weight_ref[b, e, rows, :] for e in range(3)], axis=0)
        part = jnp.dot(jnp.concatenate(lines, axis=1), right, preferred_element_type=jnp.float32)
        total = part if total is None else total + part
    return total


def near_kernel(cells_ref, weight_ref, bias_ref, total_ref, cells):
    _, side, chan = placed_at()
    out_rows, out_cols = 2 * (cells_ref.shape[0] - 1), 2 * (cells_ref.shape[1] - 2)
    total = taps_of(side, chan, cells_ref, weight_ref, cells, out_rows, out_cols)
    total_ref[...] = total + bias_ref[...]


def far_kernel(cells_ref, weight_ref, total_ref, out_ref, cells):
    _, side, chan = placed_at()
    clips, frames, out_rows, out_cols, width = out_ref.shape
    total = taps_of(side, 1 - chan, cells_ref, weight_ref, cells, out_rows, out_cols)
    total = (total + total_ref[...]).reshape(out_rows * out_cols, clips, frames, width)
    span = frames // 4
    for clip in range(clips):
        turned = jnp.swapaxes(total[:, clip], 0, 1).astype(out_ref.dtype)
        for k in range(frames):
            slot = (k + clip * span) % frames
            for r in range(out_rows):
                out_ref[clip, slot, r] = turned[k, r * out_cols : (r + 1) * out_cols]


def run(kernel, shapes, scratch, *operands, flops=0, moved=0):
    several = isinstance(shapes, (list, tuple))
    vmem = pl.BlockSpec(memory_space=pltpu.VMEM)
    return pl.pallas_call(
        kernel,
        out_shape=shapes,
        in_specs=[vmem] * len(operands),
        out_specs=[vmem] * len(shapes) if several else vmem,
        scratch_shapes=scratch,
        compiler_params=pltpu.CompilerParams(vmem_limit_bytes=16 << 20),
        cost_estimate=pl.CostEstimate(flops=flops, bytes_accessed=moved, transcendentals=0),
    )(*operands)


def small_plan(latents, conv_weight, conv_bias, gn_gain, gn_shift, up_weight, up_bias):
    clips, span, rows, cols, half = latents.shape
    spans, spaces, chans = lax.axis_size("tm"), lax.axis_size("space"), lax.axis_size("chan")
    los = spans // clips
    frames, tall, width, depth = span * spans, rows * spaces, cols // spans, half // los
    low, full = jnp.bfloat16, jnp.float32
    shape = jax.ShapeDtypeStruct
    flip = ((0, 1), (1, 0))

    cells_in = latents.reshape(clips * span * rows * cols, half)
    turns = ((1, 2), (0, 3))
    got = []
    for at_home, across in turns:
        pairs = []
        for source in range(spans):
            for chan in range(chans):
                home = chan == source // 2
                target = (source ^ at_home, chan) if home else (source ^ across, 1 - chan)
                pairs.append((source * chans + chan, target[0] * chans + target[1]))
        got.append(lax.ppermute(cells_in, ("tm", "chan"), pairs))
    weight = run(fetch_kernel, shape(conv_weight.shape, low), [pltpu.SemaphoreType.DMA], conv_weight, moved=4 << 20)
    own = run(select_kernel, shape((2, cells_in.shape[0], depth), low), [], *got, weight, moved=1 << 17)
    every = [own] + [
        lax.ppermute(own, ("space", "chan"), [(i, i ^ m) for i in range(spaces * chans)]) for m in range(1, spaces * chans)
    ]

    count = frames * tall * cols
    part = shape((count, depth), low)
    scratch = [
        pltpu.VMEM((spans, spaces, span, rows, cols, depth), full),
        pltpu.VMEM((tall // 2 + 2, frames + 2, 2 * cols, 3 * depth), low),
    ]
    flops = 2 * count * 27 * depth * half
    far_same, far_other = run(
        conv_far_kernel, [part, part], scratch, *every, weight, flops=flops, moved=3 << 20
    )
    partial = [
        lax.ppermute(value, "tm", [(i, i ^ m) for i in range(spans)]) for m, value in ((2, far_same), (3, far_other))
    ]
    keep, near_other = run(
        conv_near_kernel, [shape(part.shape, full), part], scratch, *every, weight, flops=flops, moved=3 << 20
    )
    partial = [keep] + partial + [lax.ppermute(near_other, "tm", [(i, i ^ 1) for i in range(spans)])]

    tile = shape((rows + 1, (width + 2) * frames, depth), low)
    tiles = run(
        norm_kernel,
        [tile] * spans,
        [pltpu.VMEM((spans,) + tile.shape, low)],
        *partial,
        *(vector.reshape(los, depth) for vector in (conv_bias, gn_gain, gn_shift)),
        moved=1 << 19,
    )
    tiles = [tiles[0]] + [
        lax.ppermute(tiles[m], "tm", [(i, i ^ m) for i in range(spans)]) for m in range(1, spans)
    ]

    near = run(
        cells_kernel,
        shape((rows + 1, width + 2, clips * frames, half), low),
        [pltpu.VMEM((spans,) + tile.shape, full)],
        *tiles,
        moved=1 << 18,
    )
    far = lax.ppermute(near, "chan", flip)
    cells = pltpu.VMEM((rows + 2,) + near.shape[1:], low)
    outputs = clips * frames * 4 * rows * width
    flops = 2 * outputs * 9 * half * half
    total = run(
        near_kernel, shape((outputs, half), full), [cells], near, up_weight, up_bias[None],
        flops=flops, moved=2 << 20,
    )
    return run(
        far_kernel, shape((clips, frames, 2 * rows, 2 * width, half), low), [cells], far, up_weight, total,
        flops=flops, moved=2 << 20,
    )


def solution(mesh):
    sizes = dict(mesh.shape)
    small = sizes["tm"] == 4 and sizes["space"] == 2 and sizes["chan"] == 2
    placed = (
        P("groups", "tm", "space", None, "chan"),
        P(None, None, None, "tm", "chan"),
        P("chan"),
        P("chan"),
        P("chan"),
        P(None, None, None, "chan"),
        P("chan"),
    )
    return jax.shard_map(
        small_plan if small else general_plan,
        mesh=mesh,
        in_specs=placed,
        out_specs=P("groups", None, "space", "tm", "chan"),
        check_vma=False,
    )
```

```python
import jax
import jax.numpy as jnp
from jax import lax
from jax.experimental import pallas as pl
from jax.experimental.pallas import tpu as pltpu
from jax.sharding import PartitionSpec as P

C = 512
GROUPS = 32


def shifted(value, axis, step):
    count = lax.axis_size(axis)
    pairs = [(i, i + step) for i in range(count) if 0 <= i + step < count]
    return lax.ppermute(value, axis, pairs)


def rows_around(block, axis_rows, depth):
    low = shifted(lax.slice_in_dim(block, block.shape[axis_rows] - depth, None, axis=axis_rows), "space", 1)
    high = shifted(lax.slice_in_dim(block, 0, depth, axis=axis_rows), "space", -1)
    return jnp.concatenate([low, block, high], axis=axis_rows)


def input_slice(latents):
    clips, span, rows, cols, half = latents.shape
    spans, spaces, chans = lax.axis_size("tm"), lax.axis_size("space"), lax.axis_size("chan")
    me, row_block = lax.axis_index("tm"), lax.axis_index("space")
    depth = half * chans // spans
    per_half = half // depth
    if spaces == 2:
        whole = lax.all_gather(latents, ("tm", "space", "chan"))
        whole = whole.reshape(spans, spaces, chans, clips, span, rows, cols, per_half, depth)
        mine = lax.dynamic_index_in_dim(whole, me // per_half, axis=2, keepdims=False)
        mine = lax.dynamic_index_in_dim(mine, me % per_half, axis=7 - 1, keepdims=False)
        mine = mine.transpose(2, 0, 3, 1, 4, 5, 6).reshape(clips, spans * span, spaces * rows, cols, depth)
        mine = jnp.pad(mine, ((0, 0), (0, 0), (1, 1), (0, 0), (0, 0)))
        mine = lax.dynamic_slice_in_dim(mine, row_block * rows, rows + 2, axis=2)
    else:
        bordered = rows_around(latents, 2, 1)
        whole = lax.all_gather(bordered, ("tm", "chan"))
        whole = whole.reshape((spans, chans) + bordered.shape[:4] + (per_half, depth))
        mine = lax.dynamic_index_in_dim(whole, me // per_half, axis=1, keepdims=False)
        mine = lax.dynamic_index_in_dim(mine, me % per_half, axis=5, keepdims=False)
        mine = mine.transpose(1, 0, 2, 3, 4, 5).reshape(clips, spans * span, rows + 2, cols, depth)
    return jnp.stack([jnp.roll(mine[c], -c * span, axis=0) for c in range(clips)])


def general_plan(latents, conv_weight, conv_bias, gn_gain, gn_shift, up_weight, up_bias):
    clips, span, rows, cols, half = latents.shape
    spans, spaces, chans = lax.axis_size("tm"), lax.axis_size("space"), lax.axis_size("chan")
    me, row_block = lax.axis_index("tm"), lax.axis_index("space")
    frames, width = span * spans, cols // spans
    group_width = C // GROUPS

    mine = input_slice(latents)
    padded = jnp.pad(mine, ((0, 0), (2, 0), (0, 0), (1, 1), (0, 0)))
    partial = lax.conv_general_dilated(
        padded,
        conv_weight,
        (1, 1, 1),
        "VALID",
        dimension_numbers=("NDHWC", "DHWIO", "NDHWC"),
        preferred_element_type=jnp.float32,
    )
    partial = jnp.stack([jnp.roll(partial[c], c * span, axis=0) for c in range(clips)])
    parts = partial.reshape(clips, frames, rows, spans, width, half)
    parts = parts.transpose(3, 0, 1, 2, 4, 5)
    parts = lax.all_to_all(parts, "tm", split_axis=0, concat_axis=0, tiled=True)
    conved = (jnp.sum(parts, axis=0) + conv_bias).astype(jnp.bfloat16)

    values = conved.astype(jnp.float32).reshape(-1, half)
    values = values.reshape(clips, frames * rows * width, half // group_width, group_width)
    if spaces == 2:
        every = lax.all_gather(conved, ("tm", "space", "chan"))
        every = every.reshape(spans, spaces, chans, clips, frames, rows, width, half)
        every = every.transpose(3, 4, 1, 5, 0, 6, 2, 7).reshape(clips, frames, spaces * rows, cols, C)
        gain = lax.all_gather(gn_gain, "chan", tiled=True)
        shift = lax.all_gather(gn_shift, "chan", tiled=True)
        values = every.astype(jnp.float32).reshape(clips, -1, GROUPS, group_width)
        sums = jnp.sum(values, axis=(1, 3))
        squares = jnp.sum(values * values, axis=(1, 3))
        count = float(values.shape[1] * group_width)
        mean = sums / count
        factor = lax.rsqrt(squares / count - mean * mean + 1e-06)
        edged = jnp.pad(every, ((0, 0), (0, 0), (1, 1), (1, 1), (0, 0)))
        tile = lax.dynamic_slice(
            edged, (0, 0, row_block * rows, me * width, 0), (clips, frames, rows + 2, width + 2, C)
        )
    else:
        sums = jnp.sum(values, axis=(1, 3))
        squares = jnp.sum(values * values, axis=(1, 3))
        sums, squares = lax.psum((sums, squares), ("tm", "space"))
        count = float(values.shape[1] * group_width * spans * spaces)
        mean = sums / count
        factor = lax.rsqrt(squares / count - mean * mean + 1e-06)
        bordered = rows_around(conved, 2, 1)
        left = shifted(bordered[:, :, :, -1:], "tm", 1)
        right = shifted(bordered[:, :, :, :1], "tm", -1)
        tile = jnp.concatenate([left, bordered, right], axis=3)
        tile = lax.all_gather(tile, "chan", axis=4, tiled=True)
        gain, shift, mean, factor = (
            lax.all_gather(v, "chan", axis=v.ndim - 1, tiled=True) for v in (gn_gain, gn_shift, mean, factor)
        )
    mean = jnp.repeat(mean, group_width, axis=1)[:, None, None, None]
    factor = jnp.repeat(factor, group_width, axis=1)[:, None, None, None]
    normed = (tile.astype(jnp.float32) - mean) * factor * gain + shift
    row_at = row_block * rows - 1 + jnp.arange(rows + 2)
    col_at = me * width - 1 + jnp.arange(width + 2)
    inside = ((row_at >= 0) & (row_at < rows * spaces))[:, None] & ((col_at >= 0) & (col_at < cols))[None]
    active = jnp.where(inside[None, None, :, :, None], jax.nn.silu(normed), 0.0).astype(jnp.bfloat16)
    wide = jnp.repeat(jnp.repeat(active, 2, axis=2), 2, axis=3)[:, :, 1:-1, 1:-1]
    flat = wide.reshape((clips * frames,) + wide.shape[2:])
    output = lax.conv_general_dilated(
        flat,
        up_weight,
        (1, 1),
        "VALID",
        dimension_numbers=("NHWC", "HWIO", "NHWC"),
        preferred_element_type=jnp.float32,
    )
    output = (output + up_bias).astype(jnp.bfloat16)
    return output.reshape(clips, frames, 2 * rows, 2 * width, half)


def placed_at():
    return lax.axis_index("tm"), lax.axis_index("space"), lax.axis_index("chan")


def fetch_kernel(weight_ref, weight_out, sem):
    copy = pltpu.make_async_copy(weight_ref, weight_out, sem)
    copy.start()
    copy.wait()


def select_kernel(first_ref, second_ref, after_ref, out_ref):
    del after_ref
    tm, _, _ = placed_at()
    depth = out_ref.shape[2]
    upper = tm % 2 > 0
    for i, ref in enumerate((first_ref, second_ref)):
        out_ref[i] = jnp.where(upper, ref[:, depth:], ref[:, :depth])


def stack_kernel(own_ref, row_ref, out_ref):
    out_ref[0] = own_ref[...]
    out_ref[1] = row_ref[...]


def conv_of_clip(clip, near_ref, far_ref, weight_ref, latents, taps):
    spans, spaces, span, rows, cols, depth = latents.shape
    frames, tall = spans * span, spaces * rows
    tm, side, chan = placed_at()
    size = span * rows * cols
    part = pl.ds(pl.multiple_of(clip * size, size), size)
    for ref, core in ((near_ref, chan), (far_ref, 1 - chan)):
        home = core == tm // 2
        for j, source in enumerate((jnp.where(home, tm ^ 1, tm ^ 2), jnp.where(home, tm, tm ^ 3))):
            for i, at in enumerate((side, 1 - side)):
                latents[source, at] = ref[i, j, part, :].astype(jnp.float32).reshape(latents.shape[2:])
    column = lax.broadcasted_iota(jnp.int32, (1, cols, depth), 1)
    empty = jnp.zeros((frames, cols, depth), jnp.float32)
    lines = [[empty] * 3]
    for at in range(spaces):
        for row in range(rows):
            parts = [latents[(j + clip) % spans, at, :, row] for j in range(spans)]
            value = jnp.concatenate(parts, axis=0)
            lower = jnp.where(column > 0, pltpu.roll(value, 1, 1), 0.0)
            upper = jnp.where(column < cols - 1, pltpu.roll(value, cols - 1, 1), 0.0)
            lines.append([lower, value, upper])
    lines.append([empty] * 3)
    short = tall // 2
    for line in range(short + 2):
        taps[line, :2] = jnp.zeros((2,) + taps.shape[2:], taps.dtype)
        for e in range(3):
            piece = jnp.concatenate([lines[line][e], lines[line + short][e]], axis=1)
            taps[line, 2:, :, e * depth : (e + 1) * depth] = piece.astype(taps.dtype)
    total = None
    for a in range(3):
        wide = [taps[b : b + short, a : a + frames].reshape(frames * tall * cols, 3 * depth) for b in range(3)]
        right = weight_ref[a].reshape(9 * depth, weight_ref.shape[4])
        product = jnp.dot(jnp.concatenate(wide, axis=1), right, preferred_element_type=jnp.float32)
        total = product if total is None else total + product
    width = total.shape[1] // 2
    swapped = tm % 2 > 0
    lower, upper = total[:, :width], total[:, width:]
    return jnp.where(swapped, upper, lower), jnp.where(swapped, lower, upper)


def conv_far_kernel(near_ref, far_ref, weight_ref, keep_ref, sent_ref, latents, taps):
    tm, _, _ = placed_at()
    keep, sent = conv_of_clip(1 - tm // 2, near_ref, far_ref, weight_ref, latents, taps)
    keep_ref[...] = keep
    sent_ref[...] = sent.astype(sent_ref.dtype)


def conv_near_kernel(near_ref, far_ref, weight_ref, keep_ref, sent_ref, latents, taps):
    tm, _, _ = placed_at()
    keep, sent = conv_of_clip(tm // 2, near_ref, far_ref, weight_ref, latents, taps)
    keep_ref[...] = keep
    sent_ref[...] = sent.astype(sent_ref.dtype)


def add_kernel(keep_ref, got_ref, out_ref):
    out_ref[...] = (keep_ref[...] + got_ref[...].astype(jnp.float32)).astype(out_ref.dtype)


def norm_kernel(*refs):
    partial, (bias_ref, gain_ref, shift_ref), sent = refs[:3], refs[3:6], refs[6:10]
    tiles = refs[10]
    tm, side, _ = placed_at()
    owners, reach, strip, depth = tiles.shape
    cols = 8
    frames = strip // (cols // owners + 2)
    tall = partial[0].shape[0] // (frames * cols)
    group = C // GROUPS
    block = pl.ds(tm % bias_ref.shape[0], 1)
    total = partial[0][...]
    for ref in partial[1:]:
        total = total + ref[...].astype(jnp.float32)
    flat = (total + bias_ref[block, :]).astype(jnp.bfloat16).astype(jnp.float32)
    sums = jnp.sum(flat, axis=0, keepdims=True)
    squares = jnp.sum(flat * flat, axis=0, keepdims=True)
    lane = lax.broadcasted_iota(jnp.int32, (depth, depth), 0) // group
    other = lax.broadcasted_iota(jnp.int32, (depth, depth), 1) // group
    same = (lane == other).astype(jnp.float32)
    both = jnp.concatenate([sums, squares, jnp.zeros((6, depth), jnp.float32)], axis=0)
    both = jnp.dot(both, same, precision=lax.Precision.HIGHEST, preferred_element_type=jnp.float32)
    both = both / float(flat.shape[0] * group)
    mean, square = both[0:1], both[1:2]
    factor = lax.rsqrt(square - mean * mean + 1e-06)
    normed = (flat - mean) * factor * gain_ref[block, :] + shift_ref[block, :]
    active = (normed / (1.0 + jnp.exp(-normed))).reshape(tall // 2, frames, 2, cols, depth)
    short = tall // 2
    cells = [jnp.swapaxes(active[row % short, :, row // short], 0, 1) for row in range(tall)]
    width = cols // owners
    empty = jnp.zeros((frames, depth), jnp.float32)
    for i in range(reach):
        chosen = jnp.where(side > 0, cells[i + tall - reach], cells[i])
        for owner in range(owners):
            picked = []
            for j in range(owner * width - 1, (owner + 1) * width + 1):
                picked.append(chosen[j] if 0 <= j < cols else empty)
            tiles[owner, i] = jnp.concatenate(picked, axis=0).astype(tiles.dtype)
    for m in range(owners):
        sent[m][...] = tiles[tm ^ m]


def cells_kernel(*refs):
    got, cells_ref, tiles = refs[:4], refs[4], refs[5]
    tm, _, _ = placed_at()
    for m in range(len(got)):
        tiles[tm ^ m] = got[m][...].astype(jnp.float32)
    reach, wide, tall, half = cells_ref.shape
    depth = tiles.shape[3]
    los = half // depth
    clips = tiles.shape[0] // los
    frames = tall // clips
    for i in range(reach):
        for j in range(wide):
            for x in range(los):
                stack = [tiles[clip * los + x, i, j * frames : (j + 1) * frames] for clip in range(clips)]
                piece = jnp.concatenate(stack, axis=0).astype(cells_ref.dtype)
                cells_ref[i, j, :, x * depth : (x + 1) * depth] = piece


def taps_of(side, half, cells_ref, weight_ref, cells, out_rows, out_cols):
    reach, width = cells_ref.shape[0], cells_ref.shape[3]
    cells[jnp.where(side > 0, reach, 0)] = jnp.zeros(cells.shape[1:], cells.dtype)
    for i in range(reach):
        cells[i + 1 - side] = cells_ref[i]
    rows = pl.ds(pl.multiple_of(half * width, width), width)
    total = None
    for b in range(3):
        lines = []
        for e in range(3):
            pieces = [
                cells[(r - 1 + b) // 2 + 1, (q - 1 + e) // 2 + 1]
                for r in range(out_rows)
                for q in range(out_cols)
            ]
            lines.append(jnp.concatenate(pieces, axis=0))
        right = jnp.concatenate([weight_ref[b, e, rows, :] for e in range(3)], axis=0)
        part = jnp.dot(jnp.concatenate(lines, axis=1), right, preferred_element_type=jnp.float32)
        total = part if total is None else total + part
    return total


def near_kernel(cells_ref, weight_ref, bias_ref, total_ref, cells):
    _, side, chan = placed_at()
    out_rows, out_cols = 2 * (cells_ref.shape[0] - 1), 2 * (cells_ref.shape[1] - 2)
    total = taps_of(side, chan, cells_ref, weight_ref, cells, out_rows, out_cols)
    total_ref[...] = total + bias_ref[...]


def far_kernel(cells_ref, weight_ref, total_ref, out_ref, cells):
    _, side, chan = placed_at()
    clips, frames, out_rows, out_cols, width = out_ref.shape
    total = taps_of(side, 1 - chan, cells_ref, weight_ref, cells, out_rows, out_cols)
    total = (total + total_ref[...]).reshape(out_rows * out_cols, clips, frames, width)
    span = frames // 4
    for clip in range(clips):
        turned = jnp.swapaxes(total[:, clip], 0, 1).astype(out_ref.dtype)
        for k in range(frames):
            slot = (k + clip * span) % frames
            for r in range(out_rows):
                out_ref[clip, slot, r] = turned[k, r * out_cols : (r + 1) * out_cols]


def run(kernel, shapes, scratch, *operands, flops=0, moved=0):
    several = isinstance(shapes, (list, tuple))
    vmem = pl.BlockSpec(memory_space=pltpu.VMEM)
    return pl.pallas_call(
        kernel,
        out_shape=shapes,
        in_specs=[vmem] * len(operands),
        out_specs=[vmem] * len(shapes) if several else vmem,
        scratch_shapes=scratch,
        compiler_params=pltpu.CompilerParams(vmem_limit_bytes=16 << 20),
        cost_estimate=pl.CostEstimate(flops=flops, bytes_accessed=moved, transcendentals=0),
    )(*operands)


def small_plan(latents, conv_weight, conv_bias, gn_gain, gn_shift, up_weight, up_bias):
    clips, span, rows, cols, half = latents.shape
    spans, spaces, chans = lax.axis_size("tm"), lax.axis_size("space"), lax.axis_size("chan")
    los = spans // clips
    frames, tall, width, depth = span * spans, rows * spaces, cols // spans, half // los
    low, full = jnp.bfloat16, jnp.float32
    shape = jax.ShapeDtypeStruct
    flip = ((0, 1), (1, 0))

    cells_in = latents.reshape(clips * span * rows * cols, half)
    turns = ((1, 2), (0, 3))
    got = []
    for at_home, across in turns:
        pairs = []
        for source in range(spans):
            for chan in range(chans):
                home = chan == source // 2
                target = (source ^ at_home, chan) if home else (source ^ across, 1 - chan)
                pairs.append((source * chans + chan, target[0] * chans + target[1]))
        got.append(lax.ppermute(cells_in, ("tm", "chan"), pairs))
    def across(value, axes, m):
        count = lax.axis_size(axes)
        return lax.ppermute(value, axes, [(i, i ^ m) for i in range(count)])

    weight = run(fetch_kernel, shape(conv_weight.shape, low), [pltpu.SemaphoreType.DMA], conv_weight, moved=4 << 20)
    own = run(select_kernel, shape((2, cells_in.shape[0], depth), low), [], *got, weight, moved=1 << 17)
    row = across(own, "space", 1)
    near = run(stack_kernel, shape((spaces,) + own.shape, low), [], own, row, moved=1 << 17)
    far = across(near, "chan", 1)

    count = frames * tall * cols
    part = [shape((count, depth), full), shape((count, depth), low)]
    scratch = [
        pltpu.VMEM((spans, spaces, span, rows, cols, depth), full),
        pltpu.VMEM((tall // 2 + 2, frames + 2, 2 * cols, 3 * depth), low),
    ]
    cost = {"flops": 2 * count * 27 * depth * half, "moved": 3 << 20}
    far_keep, far_sent = run(conv_far_kernel, part, scratch, near, far, weight, **cost)
    far_got = across(far_sent, "tm", 1)
    keep, sent = run(conv_near_kernel, part, scratch, near, far, weight, **cost)
    summed = run(add_kernel, part[1], [], far_keep, far_got, moved=1 << 18)
    partial = [keep, across(summed, "tm", 2), across(sent, "tm", 1)]

    tile = shape((rows + 1, (width + 2) * frames, depth), low)
    tiles = run(
        norm_kernel,
        [tile] * spans,
        [pltpu.VMEM((spans,) + tile.shape, low)],
        *partial,
        *(vector.reshape(los, depth) for vector in (conv_bias, gn_gain, gn_shift)),
        moved=1 << 19,
    )
    tiles = [tiles[0]] + [across(tiles[m], "tm", m) for m in range(1, spans)]

    near = run(
        cells_kernel,
        shape((rows + 1, width + 2, clips * frames, half), low),
        [pltpu.VMEM((spans,) + tile.shape, full)],
        *tiles,
        moved=1 << 18,
    )
    far = lax.ppermute(near, "chan", flip)
    cells = pltpu.VMEM((rows + 2,) + near.shape[1:], low)
    outputs = clips * frames * 4 * rows * width
    flops = 2 * outputs * 9 * half * half
    total = run(
        near_kernel, shape((outputs, half), full), [cells], near, up_weight, up_bias[None],
        flops=flops, moved=2 << 20,
    )
    return run(
        far_kernel, shape((clips, frames, 2 * rows, 2 * width, half), low), [cells], far, up_weight, total,
        flops=flops, moved=2 << 20,
    )


def solution(mesh):
    sizes = dict(mesh.shape)
    small = sizes["tm"] == 4 and sizes["space"] == 2 and sizes["chan"] == 2
    placed = (
        P("groups", "tm", "space", None, "chan"),
        P(None, None, None, "tm", "chan"),
        P("chan"),
        P("chan"),
        P("chan"),
        P(None, None, None, "chan"),
        P("chan"),
    )
    return jax.shard_map(
        small_plan if small else general_plan,
        mesh=mesh,
        in_specs=placed,
        out_specs=P("groups", None, "space", "tm", "chan"),
        check_vma=False,
    )
```

```python
import jax
import jax.numpy as jnp
from jax import lax
from jax.experimental import pallas as pl
from jax.experimental.pallas import tpu as pltpu
from jax.sharding import PartitionSpec as P

C = 512
GROUPS = 32


def shifted(value, axis, step):
    count = lax.axis_size(axis)
    pairs = [(i, i + step) for i in range(count) if 0 <= i + step < count]
    return lax.ppermute(value, axis, pairs)


def rows_around(block, axis_rows, depth):
    low = shifted(lax.slice_in_dim(block, block.shape[axis_rows] - depth, None, axis=axis_rows), "space", 1)
    high = shifted(lax.slice_in_dim(block, 0, depth, axis=axis_rows), "space", -1)
    return jnp.concatenate([low, block, high], axis=axis_rows)


def input_slice(latents):
    clips, span, rows, cols, half = latents.shape
    spans, spaces, chans = lax.axis_size("tm"), lax.axis_size("space"), lax.axis_size("chan")
    me, row_block = lax.axis_index("tm"), lax.axis_index("space")
    depth = half * chans // spans
    per_half = half // depth
    if spaces == 2:
        whole = lax.all_gather(latents, ("tm", "space", "chan"))
        whole = whole.reshape(spans, spaces, chans, clips, span, rows, cols, per_half, depth)
        mine = lax.dynamic_index_in_dim(whole, me // per_half, axis=2, keepdims=False)
        mine = lax.dynamic_index_in_dim(mine, me % per_half, axis=7 - 1, keepdims=False)
        mine = mine.transpose(2, 0, 3, 1, 4, 5, 6).reshape(clips, spans * span, spaces * rows, cols, depth)
        mine = jnp.pad(mine, ((0, 0), (0, 0), (1, 1), (0, 0), (0, 0)))
        mine = lax.dynamic_slice_in_dim(mine, row_block * rows, rows + 2, axis=2)
    else:
        bordered = rows_around(latents, 2, 1)
        whole = lax.all_gather(bordered, ("tm", "chan"))
        whole = whole.reshape((spans, chans) + bordered.shape[:4] + (per_half, depth))
        mine = lax.dynamic_index_in_dim(whole, me // per_half, axis=1, keepdims=False)
        mine = lax.dynamic_index_in_dim(mine, me % per_half, axis=5, keepdims=False)
        mine = mine.transpose(1, 0, 2, 3, 4, 5).reshape(clips, spans * span, rows + 2, cols, depth)
    return jnp.stack([jnp.roll(mine[c], -c * span, axis=0) for c in range(clips)])


def general_plan(latents, conv_weight, conv_bias, gn_gain, gn_shift, up_weight, up_bias):
    clips, span, rows, cols, half = latents.shape
    spans, spaces, chans = lax.axis_size("tm"), lax.axis_size("space"), lax.axis_size("chan")
    me, row_block = lax.axis_index("tm"), lax.axis_index("space")
    frames, width = span * spans, cols // spans
    group_width = C // GROUPS

    mine = input_slice(latents)
    padded = jnp.pad(mine, ((0, 0), (2, 0), (0, 0), (1, 1), (0, 0)))
    partial = lax.conv_general_dilated(
        padded,
        conv_weight,
        (1, 1, 1),
        "VALID",
        dimension_numbers=("NDHWC", "DHWIO", "NDHWC"),
        preferred_element_type=jnp.float32,
    )
    partial = jnp.stack([jnp.roll(partial[c], c * span, axis=0) for c in range(clips)])
    parts = partial.reshape(clips, frames, rows, spans, width, half)
    parts = parts.transpose(3, 0, 1, 2, 4, 5)
    parts = lax.all_to_all(parts, "tm", split_axis=0, concat_axis=0, tiled=True)
    conved = (jnp.sum(parts, axis=0) + conv_bias).astype(jnp.bfloat16)

    values = conved.astype(jnp.float32).reshape(-1, half)
    values = values.reshape(clips, frames * rows * width, half // group_width, group_width)
    if spaces == 2:
        every = lax.all_gather(conved, ("tm", "space", "chan"))
        every = every.reshape(spans, spaces, chans, clips, frames, rows, width, half)
        every = every.transpose(3, 4, 1, 5, 0, 6, 2, 7).reshape(clips, frames, spaces * rows, cols, C)
        gain = lax.all_gather(gn_gain, "chan", tiled=True)
        shift = lax.all_gather(gn_shift, "chan", tiled=True)
        values = every.astype(jnp.float32).reshape(clips, -1, GROUPS, group_width)
        sums = jnp.sum(values, axis=(1, 3))
        squares = jnp.sum(values * values, axis=(1, 3))
        count = float(values.shape[1] * group_width)
        mean = sums / count
        factor = lax.rsqrt(squares / count - mean * mean + 1e-06)
        edged = jnp.pad(every, ((0, 0), (0, 0), (1, 1), (1, 1), (0, 0)))
        tile = lax.dynamic_slice(
            edged, (0, 0, row_block * rows, me * width, 0), (clips, frames, rows + 2, width + 2, C)
        )
    else:
        sums = jnp.sum(values, axis=(1, 3))
        squares = jnp.sum(values * values, axis=(1, 3))
        sums, squares = lax.psum((sums, squares), ("tm", "space"))
        count = float(values.shape[1] * group_width * spans * spaces)
        mean = sums / count
        factor = lax.rsqrt(squares / count - mean * mean + 1e-06)
        bordered = rows_around(conved, 2, 1)
        left = shifted(bordered[:, :, :, -1:], "tm", 1)
        right = shifted(bordered[:, :, :, :1], "tm", -1)
        tile = jnp.concatenate([left, bordered, right], axis=3)
        tile = lax.all_gather(tile, "chan", axis=4, tiled=True)
        gain, shift, mean, factor = (
            lax.all_gather(v, "chan", axis=v.ndim - 1, tiled=True) for v in (gn_gain, gn_shift, mean, factor)
        )
    mean = jnp.repeat(mean, group_width, axis=1)[:, None, None, None]
    factor = jnp.repeat(factor, group_width, axis=1)[:, None, None, None]
    normed = (tile.astype(jnp.float32) - mean) * factor * gain + shift
    row_at = row_block * rows - 1 + jnp.arange(rows + 2)
    col_at = me * width - 1 + jnp.arange(width + 2)
    inside = ((row_at >= 0) & (row_at < rows * spaces))[:, None] & ((col_at >= 0) & (col_at < cols))[None]
    active = jnp.where(inside[None, None, :, :, None], jax.nn.silu(normed), 0.0).astype(jnp.bfloat16)
    wide = jnp.repeat(jnp.repeat(active, 2, axis=2), 2, axis=3)[:, :, 1:-1, 1:-1]
    flat = wide.reshape((clips * frames,) + wide.shape[2:])
    output = lax.conv_general_dilated(
        flat,
        up_weight,
        (1, 1),
        "VALID",
        dimension_numbers=("NHWC", "HWIO", "NHWC"),
        preferred_element_type=jnp.float32,
    )
    output = (output + up_bias).astype(jnp.bfloat16)
    return output.reshape(clips, frames, 2 * rows, 2 * width, half)


def placed_at():
    return lax.axis_index("tm"), lax.axis_index("space"), lax.axis_index("chan")


def fetch_kernel(weight_ref, weight_out, sem):
    copy = pltpu.make_async_copy(weight_ref, weight_out, sem)
    copy.start()
    copy.wait()


def relay_kernel(got_ref, after_ref, out_ref):
    del after_ref
    tm, _, _ = placed_at()
    depth = out_ref.shape[1]
    out_ref[...] = jnp.where(tm % 2 > 0, got_ref[:, :depth], got_ref[:, depth:])


def select_kernel(own_ref, got_ref, passed_ref, out_ref):
    tm, _, chan = placed_at()
    depth = out_ref.shape[2]
    upper, home = tm % 2 > 0, chan == tm // 2
    out_ref[0] = jnp.where(upper, got_ref[:, depth:], got_ref[:, :depth])
    own = jnp.where(upper, own_ref[:, depth:], own_ref[:, :depth])
    out_ref[1] = jnp.where(home, own, passed_ref[...])


def stack_kernel(own_ref, row_ref, out_ref):
    out_ref[0] = own_ref[...]
    out_ref[1] = row_ref[...]


def conv_of_clip(clip, near_ref, far_ref, weight_ref, latents, taps):
    spans, spaces, span, rows, cols, depth = latents.shape
    frames, tall = spans * span, spaces * rows
    tm, side, chan = placed_at()
    size = span * rows * cols
    part = pl.ds(pl.multiple_of(clip * size, size), size)
    for ref, core in ((near_ref, chan), (far_ref, 1 - chan)):
        home = core == tm // 2
        for j, source in enumerate((jnp.where(home, tm ^ 1, tm ^ 2), jnp.where(home, tm, tm ^ 3))):
            for i, at in enumerate((side, 1 - side)):
                latents[source, at] = ref[i, j, part, :].astype(jnp.float32).reshape(latents.shape[2:])
    column = lax.broadcasted_iota(jnp.int32, (1, cols, depth), 1)
    empty = jnp.zeros((frames, cols, depth), jnp.float32)
    lines = [[empty] * 3]
    for at in range(spaces):
        for row in range(rows):
            parts = [latents[(j + clip) % spans, at, :, row] for j in range(spans)]
            value = jnp.concatenate(parts, axis=0)
            lower = jnp.where(column > 0, pltpu.roll(value, 1, 1), 0.0)
            upper = jnp.where(column < cols - 1, pltpu.roll(value, cols - 1, 1), 0.0)
            lines.append([lower, value, upper])
    lines.append([empty] * 3)
    short = tall // 2
    for line in range(short + 2):
        taps[line, :2] = jnp.zeros((2,) + taps.shape[2:], taps.dtype)
        for e in range(3):
            piece = jnp.concatenate([lines[line][e], lines[line + short][e]], axis=1)
            taps[line, 2:, :, e * depth : (e + 1) * depth] = piece.astype(taps.dtype)
    total = None
    for a in range(3):
        wide = [taps[b : b + short, a : a + frames].reshape(frames * tall * cols, 3 * depth) for b in range(3)]
        right = weight_ref[a].reshape(9 * depth, weight_ref.shape[4])
        product = jnp.dot(jnp.concatenate(wide, axis=1), right, preferred_element_type=jnp.float32)
        total = product if total is None else total + product
    width = total.shape[1] // 2
    swapped = tm % 2 > 0
    lower, upper = total[:, :width], total[:, width:]
    return jnp.where(swapped, upper, lower), jnp.where(swapped, lower, upper)


def conv_far_kernel(near_ref, far_ref, weight_ref, same_ref, other_ref, latents, taps):
    tm, _, _ = placed_at()
    same, other = conv_of_clip(1 - tm // 2, near_ref, far_ref, weight_ref, latents, taps)
    same_ref[...] = same.astype(same_ref.dtype)
    other_ref[...] = other.astype(other_ref.dtype)


def conv_near_kernel(near_ref, far_ref, weight_ref, keep_ref, other_ref, latents, taps):
    tm, _, _ = placed_at()
    keep, other = conv_of_clip(tm // 2, near_ref, far_ref, weight_ref, latents, taps)
    keep_ref[...] = keep
    other_ref[...] = other.astype(other_ref.dtype)


def norm_kernel(*refs):
    partial, (bias_ref, gain_ref, shift_ref) = refs[:4], refs[4:7]
    keep_ref, next_ref, cross_ref, tiles = refs[7:]
    tm, side, _ = placed_at()
    owners, reach, strip, depth = tiles.shape
    cols = 8
    frames = strip // (cols // owners + 2)
    tall = partial[0].shape[0] // (frames * cols)
    group = C // GROUPS
    block = pl.ds(tm % bias_ref.shape[0], 1)
    total = partial[0][...]
    for ref in partial[1:]:
        total = total + ref[...].astype(jnp.float32)
    flat = (total + bias_ref[block, :]).astype(jnp.bfloat16).astype(jnp.float32)
    sums = jnp.sum(flat, axis=0, keepdims=True)
    squares = jnp.sum(flat * flat, axis=0, keepdims=True)
    lane = lax.broadcasted_iota(jnp.int32, (depth, depth), 0) // group
    other = lax.broadcasted_iota(jnp.int32, (depth, depth), 1) // group
    same = (lane == other).astype(jnp.float32)
    both = jnp.concatenate([sums, squares, jnp.zeros((6, depth), jnp.float32)], axis=0)
    both = jnp.dot(both, same, precision=lax.Precision.HIGHEST, preferred_element_type=jnp.float32)
    both = both / float(flat.shape[0] * group)
    mean, square = both[0:1], both[1:2]
    factor = lax.rsqrt(square - mean * mean + 1e-06)
    normed = (flat - mean) * factor * gain_ref[block, :] + shift_ref[block, :]
    active = (normed / (1.0 + jnp.exp(-normed))).reshape(tall // 2, frames, 2, cols, depth)
    short = tall // 2
    cells = [jnp.swapaxes(active[row % short, :, row // short], 0, 1) for row in range(tall)]
    width = cols // owners
    empty = jnp.zeros((frames, depth), jnp.float32)
    for i in range(reach):
        chosen = jnp.where(side > 0, cells[i + tall - reach], cells[i])
        for owner in range(owners):
            picked = []
            for j in range(owner * width - 1, (owner + 1) * width + 1):
                picked.append(chosen[j] if 0 <= j < cols else empty)
            tiles[owner, i] = jnp.concatenate(picked, axis=0).astype(tiles.dtype)
    keep_ref[...] = tiles[tm]
    next_ref[...] = tiles[tm ^ 1]
    for m in (2, 3):
        cross_ref[m - 2] = tiles[tm ^ m]


def hand_kernel(following_ref, crossed_ref, out_ref):
    out_ref[0] = following_ref[...]
    out_ref[1] = crossed_ref[1]


def cells_kernel(kept_ref, crossed_ref, handed_ref, cells_ref, tiles):
    tm, _, _ = placed_at()
    for m, value in enumerate((kept_ref[...], handed_ref[0], crossed_ref[0], handed_ref[1])):
        tiles[tm ^ m] = value.astype(jnp.float32)
    reach, wide, tall, half = cells_ref.shape
    depth = tiles.shape[3]
    los = half // depth
    clips = tiles.shape[0] // los
    frames = tall // clips
    for i in range(reach):
        for j in range(wide):
            for x in range(los):
                stack = [tiles[clip * los + x, i, j * frames : (j + 1) * frames] for clip in range(clips)]
                piece = jnp.concatenate(stack, axis=0).astype(cells_ref.dtype)
                cells_ref[i, j, :, x * depth : (x + 1) * depth] = piece


def taps_of(side, half, cells_ref, weight_ref, cells, out_rows, out_cols):
    reach, width = cells_ref.shape[0], cells_ref.shape[3]
    cells[jnp.where(side > 0, reach, 0)] = jnp.zeros(cells.shape[1:], cells.dtype)
    for i in range(reach):
        cells[i + 1 - side] = cells_ref[i]
    rows = pl.ds(pl.multiple_of(half * width, width), width)
    total = None
    for b in range(3):
        lines = []
        for e in range(3):
            pieces = [
                cells[(r - 1 + b) // 2 + 1, (q - 1 + e) // 2 + 1]
                for r in range(out_rows)
                for q in range(out_cols)
            ]
            lines.append(jnp.concatenate(pieces, axis=0))
        right = jnp.concatenate([weight_ref[b, e, rows, :] for e in range(3)], axis=0)
        part = jnp.dot(jnp.concatenate(lines, axis=1), right, preferred_element_type=jnp.float32)
        total = part if total is None else total + part
    return total


def near_kernel(cells_ref, weight_ref, bias_ref, total_ref, cells):
    _, side, chan = placed_at()
    out_rows, out_cols = 2 * (cells_ref.shape[0] - 1), 2 * (cells_ref.shape[1] - 2)
    total = taps_of(side, chan, cells_ref, weight_ref, cells, out_rows, out_cols)
    total_ref[...] = total + bias_ref[...]


def far_kernel(cells_ref, weight_ref, total_ref, out_ref, cells):
    _, side, chan = placed_at()
    clips, frames, out_rows, out_cols, width = out_ref.shape
    total = taps_of(side, 1 - chan, cells_ref, weight_ref, cells, out_rows, out_cols)
    total = (total + total_ref[...]).reshape(out_rows * out_cols, clips, frames, width)
    span = frames // 4
    for clip in range(clips):
        turned = jnp.swapaxes(total[:, clip], 0, 1).astype(out_ref.dtype)
        for k in range(frames):
            slot = (k + clip * span) % frames
            for r in range(out_rows):
                out_ref[clip, slot, r] = turned[k, r * out_cols : (r + 1) * out_cols]


def run(kernel, shapes, scratch, *operands, flops=0, moved=0):
    several = isinstance(shapes, (list, tuple))
    vmem = pl.BlockSpec(memory_space=pltpu.VMEM)
    return pl.pallas_call(
        kernel,
        out_shape=shapes,
        in_specs=[vmem] * len(operands),
        out_specs=[vmem] * len(shapes) if several else vmem,
        scratch_shapes=scratch,
        compiler_params=pltpu.CompilerParams(vmem_limit_bytes=16 << 20),
        cost_estimate=pl.CostEstimate(flops=flops, bytes_accessed=moved, transcendentals=0),
    )(*operands)


def small_plan(latents, conv_weight, conv_bias, gn_gain, gn_shift, up_weight, up_bias):
    clips, span, rows, cols, half = latents.shape
    spans, spaces, chans = lax.axis_size("tm"), lax.axis_size("space"), lax.axis_size("chan")
    los = spans // clips
    frames, tall, width, depth = span * spans, rows * spaces, cols // spans, half // los
    low, full = jnp.bfloat16, jnp.float32
    shape = jax.ShapeDtypeStruct
    flip = ((0, 1), (1, 0))

    cells_in = latents.reshape(clips * span * rows * cols, half)
    first, second = [], []
    for source in range(spans):
        for chan in range(chans):
            home = chan == source // 2
            target = (source ^ 1, chan) if home else (source ^ 2, 1 - chan)
            first.append((source * chans + chan, target[0] * chans + target[1]))
            if not home:
                second.append((source * chans + chan, (source ^ 1) * chans + chan))
    got = lax.ppermute(cells_in, ("tm", "chan"), first)
    weight = run(fetch_kernel, shape(conv_weight.shape, low), [pltpu.SemaphoreType.DMA], conv_weight, moved=4 << 20)
    relayed = run(relay_kernel, shape((cells_in.shape[0], depth), low), [], got, weight, moved=1 << 17)
    passed = lax.ppermute(relayed, ("tm", "chan"), second)

    def across(value, axes, m):
        count = lax.axis_size(axes)
        return lax.ppermute(value, axes, [(i, i ^ m) for i in range(count)])

    own = run(select_kernel, shape((2, cells_in.shape[0], depth), low), [], cells_in, got, passed, moved=1 << 17)
    row = across(own, "space", 1)
    near = run(stack_kernel, shape((spaces,) + own.shape, low), [], own, row, moved=1 << 17)
    far = across(near, "chan", 1)

    count = frames * tall * cols
    part = [shape((count, depth), full), shape((count, depth), low)]
    scratch = [
        pltpu.VMEM((spans, spaces, span, rows, cols, depth), full),
        pltpu.VMEM((tall // 2 + 2, frames + 2, 2 * cols, 3 * depth), low),
    ]
    cost = {"flops": 2 * count * 27 * depth * half, "moved": 3 << 20}
    far_same, far_other = run(conv_far_kernel, [part[1], part[1]], scratch, near, far, weight, **cost)
    partial = [across(far_same, "tm", 2), across(far_other, "tm", 3)]
    keep, near_other = run(conv_near_kernel, part, scratch, near, far, weight, **cost)
    partial = [keep] + partial + [across(near_other, "tm", 1)]

    tile = shape((rows + 1, (width + 2) * frames, depth), low)
    kept, following, crossing = run(
        norm_kernel,
        [tile, tile, shape((2,) + tile.shape, low)],
        [pltpu.VMEM((spans,) + tile.shape, low)],
        *partial,
        *(vector.reshape(los, depth) for vector in (conv_bias, gn_gain, gn_shift)),
        moved=1 << 19,
    )
    crossed = across(crossing, "tm", 2)
    handed = run(hand_kernel, shape((2,) + tile.shape, low), [], following, crossed, moved=1 << 17)
    tiles = [kept, crossed, across(handed, "tm", 1)]

    near = run(
        cells_kernel,
        shape((rows + 1, width + 2, clips * frames, half), low),
        [pltpu.VMEM((spans,) + tile.shape, full)],
        *tiles,
        moved=1 << 18,
    )
    far = lax.ppermute(near, "chan", flip)
    cells = pltpu.VMEM((rows + 2,) + near.shape[1:], low)
    outputs = clips * frames * 4 * rows * width
    flops = 2 * outputs * 9 * half * half
    total = run(
        near_kernel, shape((outputs, half), full), [cells], near, up_weight, up_bias[None],
        flops=flops, moved=2 << 20,
    )
    return run(
        far_kernel, shape((clips, frames, 2 * rows, 2 * width, half), low), [cells], far, up_weight, total,
        flops=flops, moved=2 << 20,
    )


def solution(mesh):
    sizes = dict(mesh.shape)
    small = sizes["tm"] == 4 and sizes["space"] == 2 and sizes["chan"] == 2
    placed = (
        P("groups", "tm", "space", None, "chan"),
        P(None, None, None, "tm", "chan"),
        P("chan"),
        P("chan"),
        P("chan"),
        P(None, None, None, "chan"),
        P("chan"),
    )
    return jax.shard_map(
        small_plan if small else general_plan,
        mesh=mesh,
        in_specs=placed,
        out_specs=P("groups", None, "space", "tm", "chan"),
        check_vma=False,
    )
```

```python
import jax
import jax.numpy as jnp
from jax import lax
from jax.experimental import pallas as pl
from jax.experimental.pallas import tpu as pltpu
from jax.sharding import PartitionSpec as P

C = 512
GROUPS = 32


def shifted(value, axis, step):
    count = lax.axis_size(axis)
    pairs = [(i, i + step) for i in range(count) if 0 <= i + step < count]
    return lax.ppermute(value, axis, pairs)


def rows_around(block, axis_rows, depth):
    low = shifted(lax.slice_in_dim(block, block.shape[axis_rows] - depth, None, axis=axis_rows), "space", 1)
    high = shifted(lax.slice_in_dim(block, 0, depth, axis=axis_rows), "space", -1)
    return jnp.concatenate([low, block, high], axis=axis_rows)


def input_slice(latents):
    clips, span, rows, cols, half = latents.shape
    spans, spaces, chans = lax.axis_size("tm"), lax.axis_size("space"), lax.axis_size("chan")
    me, row_block = lax.axis_index("tm"), lax.axis_index("space")
    depth = half * chans // spans
    per_half = half // depth
    if spaces == 2:
        whole = lax.all_gather(latents, ("tm", "space", "chan"))
        whole = whole.reshape(spans, spaces, chans, clips, span, rows, cols, per_half, depth)
        mine = lax.dynamic_index_in_dim(whole, me // per_half, axis=2, keepdims=False)
        mine = lax.dynamic_index_in_dim(mine, me % per_half, axis=7 - 1, keepdims=False)
        mine = mine.transpose(2, 0, 3, 1, 4, 5, 6).reshape(clips, spans * span, spaces * rows, cols, depth)
        mine = jnp.pad(mine, ((0, 0), (0, 0), (1, 1), (0, 0), (0, 0)))
        mine = lax.dynamic_slice_in_dim(mine, row_block * rows, rows + 2, axis=2)
    else:
        bordered = rows_around(latents, 2, 1)
        whole = lax.all_gather(bordered, ("tm", "chan"))
        whole = whole.reshape((spans, chans) + bordered.shape[:4] + (per_half, depth))
        mine = lax.dynamic_index_in_dim(whole, me // per_half, axis=1, keepdims=False)
        mine = lax.dynamic_index_in_dim(mine, me % per_half, axis=5, keepdims=False)
        mine = mine.transpose(1, 0, 2, 3, 4, 5).reshape(clips, spans * span, rows + 2, cols, depth)
    return jnp.stack([jnp.roll(mine[c], -c * span, axis=0) for c in range(clips)])


def general_plan(latents, conv_weight, conv_bias, gn_gain, gn_shift, up_weight, up_bias):
    clips, span, rows, cols, half = latents.shape
    spans, spaces, chans = lax.axis_size("tm"), lax.axis_size("space"), lax.axis_size("chan")
    me, row_block = lax.axis_index("tm"), lax.axis_index("space")
    frames, width = span * spans, cols // spans
    group_width = C // GROUPS

    mine = input_slice(latents)
    padded = jnp.pad(mine, ((0, 0), (2, 0), (0, 0), (1, 1), (0, 0)))
    partial = lax.conv_general_dilated(
        padded,
        conv_weight,
        (1, 1, 1),
        "VALID",
        dimension_numbers=("NDHWC", "DHWIO", "NDHWC"),
        preferred_element_type=jnp.float32,
    )
    partial = jnp.stack([jnp.roll(partial[c], c * span, axis=0) for c in range(clips)])
    parts = partial.reshape(clips, frames, rows, spans, width, half)
    parts = parts.transpose(3, 0, 1, 2, 4, 5)
    parts = lax.all_to_all(parts, "tm", split_axis=0, concat_axis=0, tiled=True)
    conved = (jnp.sum(parts, axis=0) + conv_bias).astype(jnp.bfloat16)

    values = conved.astype(jnp.float32).reshape(-1, half)
    values = values.reshape(clips, frames * rows * width, half // group_width, group_width)
    if spaces == 2:
        every = lax.all_gather(conved, ("tm", "space", "chan"))
        every = every.reshape(spans, spaces, chans, clips, frames, rows, width, half)
        every = every.transpose(3, 4, 1, 5, 0, 6, 2, 7).reshape(clips, frames, spaces * rows, cols, C)
        gain = lax.all_gather(gn_gain, "chan", tiled=True)
        shift = lax.all_gather(gn_shift, "chan", tiled=True)
        values = every.astype(jnp.float32).reshape(clips, -1, GROUPS, group_width)
        sums = jnp.sum(values, axis=(1, 3))
        squares = jnp.sum(values * values, axis=(1, 3))
        count = float(values.shape[1] * group_width)
        mean = sums / count
        factor = lax.rsqrt(squares / count - mean * mean + 1e-06)
        edged = jnp.pad(every, ((0, 0), (0, 0), (1, 1), (1, 1), (0, 0)))
        tile = lax.dynamic_slice(
            edged, (0, 0, row_block * rows, me * width, 0), (clips, frames, rows + 2, width + 2, C)
        )
    else:
        sums = jnp.sum(values, axis=(1, 3))
        squares = jnp.sum(values * values, axis=(1, 3))
        sums, squares = lax.psum((sums, squares), ("tm", "space"))
        count = float(values.shape[1] * group_width * spans * spaces)
        mean = sums / count
        factor = lax.rsqrt(squares / count - mean * mean + 1e-06)
        bordered = rows_around(conved, 2, 1)
        left = shifted(bordered[:, :, :, -1:], "tm", 1)
        right = shifted(bordered[:, :, :, :1], "tm", -1)
        tile = jnp.concatenate([left, bordered, right], axis=3)
        tile = lax.all_gather(tile, "chan", axis=4, tiled=True)
        gain, shift, mean, factor = (
            lax.all_gather(v, "chan", axis=v.ndim - 1, tiled=True) for v in (gn_gain, gn_shift, mean, factor)
        )
    mean = jnp.repeat(mean, group_width, axis=1)[:, None, None, None]
    factor = jnp.repeat(factor, group_width, axis=1)[:, None, None, None]
    normed = (tile.astype(jnp.float32) - mean) * factor * gain + shift
    row_at = row_block * rows - 1 + jnp.arange(rows + 2)
    col_at = me * width - 1 + jnp.arange(width + 2)
    inside = ((row_at >= 0) & (row_at < rows * spaces))[:, None] & ((col_at >= 0) & (col_at < cols))[None]
    active = jnp.where(inside[None, None, :, :, None], jax.nn.silu(normed), 0.0).astype(jnp.bfloat16)
    wide = jnp.repeat(jnp.repeat(active, 2, axis=2), 2, axis=3)[:, :, 1:-1, 1:-1]
    flat = wide.reshape((clips * frames,) + wide.shape[2:])
    output = lax.conv_general_dilated(
        flat,
        up_weight,
        (1, 1),
        "VALID",
        dimension_numbers=("NHWC", "HWIO", "NHWC"),
        preferred_element_type=jnp.float32,
    )
    output = (output + up_bias).astype(jnp.bfloat16)
    return output.reshape(clips, frames, 2 * rows, 2 * width, half)


def placed_at():
    return lax.axis_index("tm"), lax.axis_index("space"), lax.axis_index("chan")


def fetch_kernel(weight_ref, weight_out, sem):
    copy = pltpu.make_async_copy(weight_ref, weight_out, sem)
    copy.start()
    copy.wait()


def relay_kernel(got_ref, after_ref, out_ref):
    del after_ref
    tm, _, _ = placed_at()
    depth = out_ref.shape[1]
    out_ref[...] = jnp.where(tm % 2 > 0, got_ref[:, :depth], got_ref[:, depth:])


def select_kernel(own_ref, got_ref, passed_ref, out_ref):
    tm, _, chan = placed_at()
    depth = out_ref.shape[2]
    upper, home = tm % 2 > 0, chan == tm // 2
    out_ref[0] = jnp.where(upper, got_ref[:, depth:], got_ref[:, :depth])
    own = jnp.where(upper, own_ref[:, depth:], own_ref[:, :depth])
    out_ref[1] = jnp.where(home, own, passed_ref[...])


def stack_kernel(own_ref, row_ref, out_ref):
    out_ref[0] = own_ref[...]
    out_ref[1] = row_ref[...]


def conv_of_clip(clip, near_ref, far_ref, weight_ref, latents, taps):
    spans, spaces, span, rows, cols, depth = latents.shape
    frames, tall = spans * span, spaces * rows
    tm, side, chan = placed_at()
    size = span * rows * cols
    part = pl.ds(pl.multiple_of(clip * size, size), size)
    for ref, core in ((near_ref, chan), (far_ref, 1 - chan)):
        home = core == tm // 2
        for j, source in enumerate((jnp.where(home, tm ^ 1, tm ^ 2), jnp.where(home, tm, tm ^ 3))):
            for i, at in enumerate((side, 1 - side)):
                latents[source, at] = ref[i, j, part, :].astype(jnp.float32).reshape(latents.shape[2:])
    column = lax.broadcasted_iota(jnp.int32, (1, cols, depth), 1)
    empty = jnp.zeros((frames, cols, depth), jnp.float32)
    lines = [[empty] * 3]
    for at in range(spaces):
        for row in range(rows):
            parts = [latents[(j + clip) % spans, at, :, row] for j in range(spans)]
            value = jnp.concatenate(parts, axis=0)
            lower = jnp.where(column > 0, pltpu.roll(value, 1, 1), 0.0)
            upper = jnp.where(column < cols - 1, pltpu.roll(value, cols - 1, 1), 0.0)
            lines.append([lower, value, upper])
    lines.append([empty] * 3)
    short = tall // 2
    for line in range(short + 2):
        taps[line, :2] = jnp.zeros((2,) + taps.shape[2:], taps.dtype)
        for e in range(3):
            piece = jnp.concatenate([lines[line][e], lines[line + short][e]], axis=1)
            taps[line, 2:, :, e * depth : (e + 1) * depth] = piece.astype(taps.dtype)
    total = None
    for a in range(3):
        wide = [taps[b : b + short, a : a + frames].reshape(frames * tall * cols, 3 * depth) for b in range(3)]
        right = weight_ref[a].reshape(9 * depth, weight_ref.shape[4])
        product = jnp.dot(jnp.concatenate(wide, axis=1), right, preferred_element_type=jnp.float32)
        total = product if total is None else total + product
    width = total.shape[1] // 2
    swapped = tm % 2 > 0
    lower, upper = total[:, :width], total[:, width:]
    return jnp.where(swapped, upper, lower), jnp.where(swapped, lower, upper)


def conv_far_kernel(near_ref, far_ref, weight_ref, same_ref, other_ref, latents, taps):
    tm, _, _ = placed_at()
    same, other = conv_of_clip(1 - tm // 2, near_ref, far_ref, weight_ref, latents, taps)
    same_ref[...] = same.astype(same_ref.dtype)
    other_ref[...] = other.astype(other_ref.dtype)


def conv_near_kernel(near_ref, far_ref, weight_ref, keep_ref, other_ref, latents, taps):
    tm, _, _ = placed_at()
    keep, other = conv_of_clip(tm // 2, near_ref, far_ref, weight_ref, latents, taps)
    keep_ref[...] = keep
    other_ref[...] = other.astype(other_ref.dtype)


def norm_kernel(*refs):
    partial, (bias_ref, gain_ref, shift_ref), sent = refs[:4], refs[4:7], refs[7:11]
    tiles = refs[11]
    tm, side, _ = placed_at()
    owners, reach, strip, depth = tiles.shape
    cols = 8
    frames = strip // (cols // owners + 2)
    tall = partial[0].shape[0] // (frames * cols)
    group = C // GROUPS
    block = pl.ds(tm % bias_ref.shape[0], 1)
    total = partial[0][...]
    for ref in partial[1:]:
        total = total + ref[...].astype(jnp.float32)
    flat = (total + bias_ref[block, :]).astype(jnp.bfloat16).astype(jnp.float32)
    sums = jnp.sum(flat, axis=0, keepdims=True)
    squares = jnp.sum(flat * flat, axis=0, keepdims=True)
    lane = lax.broadcasted_iota(jnp.int32, (depth, depth), 0) // group
    other = lax.broadcasted_iota(jnp.int32, (depth, depth), 1) // group
    same = (lane == other).astype(jnp.float32)
    both = jnp.concatenate([sums, squares, jnp.zeros((6, depth), jnp.float32)], axis=0)
    both = jnp.dot(both, same, precision=lax.Precision.HIGHEST, preferred_element_type=jnp.float32)
    both = both / float(flat.shape[0] * group)
    mean, square = both[0:1], both[1:2]
    factor = lax.rsqrt(square - mean * mean + 1e-06)
    normed = (flat - mean) * factor * gain_ref[block, :] + shift_ref[block, :]
    active = (normed / (1.0 + jnp.exp(-normed))).reshape(tall // 2, frames, 2, cols, depth)
    short = tall // 2
    cells = [jnp.swapaxes(active[row % short, :, row // short], 0, 1) for row in range(tall)]
    width = cols // owners
    empty = jnp.zeros((frames, depth), jnp.float32)
    for i in range(reach):
        chosen = jnp.where(side > 0, cells[i + tall - reach], cells[i])
        for owner in range(owners):
            picked = []
            for j in range(owner * width - 1, (owner + 1) * width + 1):
                picked.append(chosen[j] if 0 <= j < cols else empty)
            tiles[owner, i] = jnp.concatenate(picked, axis=0).astype(tiles.dtype)
    for m in range(owners):
        sent[m][...] = tiles[tm ^ m]


def cells_kernel(*refs):
    got, cells_ref, tiles = refs[:4], refs[4], refs[5]
    tm, _, _ = placed_at()
    for m in range(len(got)):
        tiles[tm ^ m] = got[m][...].astype(jnp.float32)
    reach, wide, tall, half = cells_ref.shape
    depth = tiles.shape[3]
    los = half // depth
    clips = tiles.shape[0] // los
    frames = tall // clips
    for i in range(reach):
        for j in range(wide):
            for x in range(los):
                stack = [tiles[clip * los + x, i, j * frames : (j + 1) * frames] for clip in range(clips)]
                piece = jnp.concatenate(stack, axis=0).astype(cells_ref.dtype)
                cells_ref[i, j, :, x * depth : (x + 1) * depth] = piece


def taps_of(side, half, cells_ref, weight_ref, cells, out_rows, out_cols):
    reach, width = cells_ref.shape[0], cells_ref.shape[3]
    cells[jnp.where(side > 0, reach, 0)] = jnp.zeros(cells.shape[1:], cells.dtype)
    for i in range(reach):
        cells[i + 1 - side] = cells_ref[i]
    rows = pl.ds(pl.multiple_of(half * width, width), width)
    total = None
    for b in range(3):
        lines = []
        for e in range(3):
            pieces = [
                cells[(r - 1 + b) // 2 + 1, (q - 1 + e) // 2 + 1]
                for r in range(out_rows)
                for q in range(out_cols)
            ]
            lines.append(jnp.concatenate(pieces, axis=0))
        right = jnp.concatenate([weight_ref[b, e, rows, :] for e in range(3)], axis=0)
        part = jnp.dot(jnp.concatenate(lines, axis=1), right, preferred_element_type=jnp.float32)
        total = part if total is None else total + part
    return total


def near_kernel(cells_ref, weight_ref, bias_ref, total_ref, cells):
    _, side, chan = placed_at()
    out_rows, out_cols = 2 * (cells_ref.shape[0] - 1), 2 * (cells_ref.shape[1] - 2)
    total = taps_of(side, chan, cells_ref, weight_ref, cells, out_rows, out_cols)
    total_ref[...] = total + bias_ref[...]


def far_kernel(cells_ref, weight_ref, total_ref, out_ref, cells):
    _, side, chan = placed_at()
    clips, frames, out_rows, out_cols, width = out_ref.shape
    total = taps_of(side, 1 - chan, cells_ref, weight_ref, cells, out_rows, out_cols)
    total = (total + total_ref[...]).reshape(out_rows * out_cols, clips, frames, width)
    span = frames // 4
    for clip in range(clips):
        turned = jnp.swapaxes(total[:, clip], 0, 1).astype(out_ref.dtype)
        for k in range(frames):
            slot = (k + clip * span) % frames
            for r in range(out_rows):
                out_ref[clip, slot, r] = turned[k, r * out_cols : (r + 1) * out_cols]


def run(kernel, shapes, scratch, *operands, flops=0, moved=0):
    several = isinstance(shapes, (list, tuple))
    vmem = pl.BlockSpec(memory_space=pltpu.VMEM)
    return pl.pallas_call(
        kernel,
        out_shape=shapes,
        in_specs=[vmem] * len(operands),
        out_specs=[vmem] * len(shapes) if several else vmem,
        scratch_shapes=scratch,
        compiler_params=pltpu.CompilerParams(vmem_limit_bytes=16 << 20),
        cost_estimate=pl.CostEstimate(flops=flops, bytes_accessed=moved, transcendentals=0),
    )(*operands)


def small_plan(latents, conv_weight, conv_bias, gn_gain, gn_shift, up_weight, up_bias):
    clips, span, rows, cols, half = latents.shape
    spans, spaces, chans = lax.axis_size("tm"), lax.axis_size("space"), lax.axis_size("chan")
    los = spans // clips
    frames, tall, width, depth = span * spans, rows * spaces, cols // spans, half // los
    low, full = jnp.bfloat16, jnp.float32
    shape = jax.ShapeDtypeStruct
    flip = ((0, 1), (1, 0))

    cells_in = latents.reshape(clips * span * rows * cols, half)
    first, second = [], []
    for source in range(spans):
        for chan in range(chans):
            home = chan == source // 2
            target = (source ^ 1, chan) if home else (source ^ 2, 1 - chan)
            first.append((source * chans + chan, target[0] * chans + target[1]))
            if not home:
                second.append((source * chans + chan, (source ^ 1) * chans + chan))
    got = lax.ppermute(cells_in, ("tm", "chan"), first)
    weight = run(fetch_kernel, shape(conv_weight.shape, low), [pltpu.SemaphoreType.DMA], conv_weight, moved=4 << 20)
    relayed = run(relay_kernel, shape((cells_in.shape[0], depth), low), [], got, weight, moved=1 << 17)
    passed = lax.ppermute(relayed, ("tm", "chan"), second)

    def across(value, axes, m):
        count = lax.axis_size(axes)
        return lax.ppermute(value, axes, [(i, i ^ m) for i in range(count)])

    own = run(select_kernel, shape((2, cells_in.shape[0], depth), low), [], cells_in, got, passed, moved=1 << 17)
    row = across(own, "space", 1)
    near = run(stack_kernel, shape((spaces,) + own.shape, low), [], own, row, moved=1 << 17)
    far = across(near, "chan", 1)

    count = frames * tall * cols
    part = [shape((count, depth), full), shape((count, depth), low)]
    scratch = [
        pltpu.VMEM((spans, spaces, span, rows, cols, depth), full),
        pltpu.VMEM((tall // 2 + 2, frames + 2, 2 * cols, 3 * depth), low),
    ]
    cost = {"flops": 2 * count * 27 * depth * half, "moved": 3 << 20}
    far_same, far_other = run(conv_far_kernel, [part[1], part[1]], scratch, near, far, weight, **cost)
    partial = [across(far_same, "tm", 2), across(far_other, "tm", 3)]
    keep, near_other = run(conv_near_kernel, part, scratch, near, far, weight, **cost)
    partial = [keep] + partial + [across(near_other, "tm", 1)]

    tile = shape((rows + 1, (width + 2) * frames, depth), low)
    tiles = run(
        norm_kernel,
        [tile] * spans,
        [pltpu.VMEM((spans,) + tile.shape, low)],
        *partial,
        *(vector.reshape(los, depth) for vector in (conv_bias, gn_gain, gn_shift)),
        moved=1 << 19,
    )
    tiles = [tiles[0]] + [across(tiles[m], "tm", m) for m in range(1, spans)]

    near = run(
        cells_kernel,
        shape((rows + 1, width + 2, clips * frames, half), low),
        [pltpu.VMEM((spans,) + tile.shape, full)],
        *tiles,
        moved=1 << 18,
    )
    far = lax.ppermute(near, "chan", flip)
    cells = pltpu.VMEM((rows + 2,) + near.shape[1:], low)
    outputs = clips * frames * 4 * rows * width
    flops = 2 * outputs * 9 * half * half
    total = run(
        near_kernel, shape((outputs, half), full), [cells], near, up_weight, up_bias[None],
        flops=flops, moved=2 << 20,
    )
    return run(
        far_kernel, shape((clips, frames, 2 * rows, 2 * width, half), low), [cells], far, up_weight, total,
        flops=flops, moved=2 << 20,
    )


def solution(mesh):
    sizes = dict(mesh.shape)
    small = sizes["tm"] == 4 and sizes["space"] == 2 and sizes["chan"] == 2
    placed = (
        P("groups", "tm", "space", None, "chan"),
        P(None, None, None, "tm", "chan"),
        P("chan"),
        P("chan"),
        P("chan"),
        P(None, None, None, "chan"),
        P("chan"),
    )
    return jax.shard_map(
        small_plan if small else general_plan,
        mesh=mesh,
        in_specs=placed,
        out_specs=P("groups", None, "space", "tm", "chan"),
        check_vma=False,
    )
```

```python
import jax
import jax.numpy as jnp
from jax import lax
from jax.experimental import pallas as pl
from jax.experimental.pallas import tpu as pltpu
from jax.sharding import PartitionSpec as P

C = 512
GROUPS = 32


def shifted(value, axis, step):
    count = lax.axis_size(axis)
    pairs = [(i, i + step) for i in range(count) if 0 <= i + step < count]
    return lax.ppermute(value, axis, pairs)


def rows_around(block, axis_rows, depth):
    low = shifted(lax.slice_in_dim(block, block.shape[axis_rows] - depth, None, axis=axis_rows), "space", 1)
    high = shifted(lax.slice_in_dim(block, 0, depth, axis=axis_rows), "space", -1)
    return jnp.concatenate([low, block, high], axis=axis_rows)


def input_slice(latents):
    clips, span, rows, cols, half = latents.shape
    spans, spaces, chans = lax.axis_size("tm"), lax.axis_size("space"), lax.axis_size("chan")
    me, row_block = lax.axis_index("tm"), lax.axis_index("space")
    depth = half * chans // spans
    per_half = half // depth
    if spaces == 2:
        whole = lax.all_gather(latents, ("tm", "space", "chan"))
        whole = whole.reshape(spans, spaces, chans, clips, span, rows, cols, per_half, depth)
        mine = lax.dynamic_index_in_dim(whole, me // per_half, axis=2, keepdims=False)
        mine = lax.dynamic_index_in_dim(mine, me % per_half, axis=7 - 1, keepdims=False)
        mine = mine.transpose(2, 0, 3, 1, 4, 5, 6).reshape(clips, spans * span, spaces * rows, cols, depth)
        mine = jnp.pad(mine, ((0, 0), (0, 0), (1, 1), (0, 0), (0, 0)))
        mine = lax.dynamic_slice_in_dim(mine, row_block * rows, rows + 2, axis=2)
    else:
        bordered = rows_around(latents, 2, 1)
        whole = lax.all_gather(bordered, ("tm", "chan"))
        whole = whole.reshape((spans, chans) + bordered.shape[:4] + (per_half, depth))
        mine = lax.dynamic_index_in_dim(whole, me // per_half, axis=1, keepdims=False)
        mine = lax.dynamic_index_in_dim(mine, me % per_half, axis=5, keepdims=False)
        mine = mine.transpose(1, 0, 2, 3, 4, 5).reshape(clips, spans * span, rows + 2, cols, depth)
    return jnp.stack([jnp.roll(mine[c], -c * span, axis=0) for c in range(clips)])


def general_plan(latents, conv_weight, conv_bias, gn_gain, gn_shift, up_weight, up_bias):
    clips, span, rows, cols, half = latents.shape
    spans, spaces, chans = lax.axis_size("tm"), lax.axis_size("space"), lax.axis_size("chan")
    me, row_block = lax.axis_index("tm"), lax.axis_index("space")
    frames, width = span * spans, cols // spans
    group_width = C // GROUPS

    mine = input_slice(latents)
    padded = jnp.pad(mine, ((0, 0), (2, 0), (0, 0), (1, 1), (0, 0)))
    partial = lax.conv_general_dilated(
        padded,
        conv_weight,
        (1, 1, 1),
        "VALID",
        dimension_numbers=("NDHWC", "DHWIO", "NDHWC"),
        preferred_element_type=jnp.float32,
    )
    partial = jnp.stack([jnp.roll(partial[c], c * span, axis=0) for c in range(clips)])
    parts = partial.reshape(clips, frames, rows, spans, width, half)
    parts = parts.transpose(3, 0, 1, 2, 4, 5)
    parts = lax.all_to_all(parts, "tm", split_axis=0, concat_axis=0, tiled=True)
    conved = (jnp.sum(parts, axis=0) + conv_bias).astype(jnp.bfloat16)

    values = conved.astype(jnp.float32).reshape(-1, half)
    values = values.reshape(clips, frames * rows * width, half // group_width, group_width)
    if spaces == 2:
        every = lax.all_gather(conved, ("tm", "space", "chan"))
        every = every.reshape(spans, spaces, chans, clips, frames, rows, width, half)
        every = every.transpose(3, 4, 1, 5, 0, 6, 2, 7).reshape(clips, frames, spaces * rows, cols, C)
        gain = lax.all_gather(gn_gain, "chan", tiled=True)
        shift = lax.all_gather(gn_shift, "chan", tiled=True)
        values = every.astype(jnp.float32).reshape(clips, -1, GROUPS, group_width)
        sums = jnp.sum(values, axis=(1, 3))
        squares = jnp.sum(values * values, axis=(1, 3))
        count = float(values.shape[1] * group_width)
        mean = sums / count
        factor = lax.rsqrt(squares / count - mean * mean + 1e-06)
        edged = jnp.pad(every, ((0, 0), (0, 0), (1, 1), (1, 1), (0, 0)))
        tile = lax.dynamic_slice(
            edged, (0, 0, row_block * rows, me * width, 0), (clips, frames, rows + 2, width + 2, C)
        )
    else:
        sums = jnp.sum(values, axis=(1, 3))
        squares = jnp.sum(values * values, axis=(1, 3))
        sums, squares = lax.psum((sums, squares), ("tm", "space"))
        count = float(values.shape[1] * group_width * spans * spaces)
        mean = sums / count
        factor = lax.rsqrt(squares / count - mean * mean + 1e-06)
        bordered = rows_around(conved, 2, 1)
        left = shifted(bordered[:, :, :, -1:], "tm", 1)
        right = shifted(bordered[:, :, :, :1], "tm", -1)
        tile = jnp.concatenate([left, bordered, right], axis=3)
        tile = lax.all_gather(tile, "chan", axis=4, tiled=True)
        gain, shift, mean, factor = (
            lax.all_gather(v, "chan", axis=v.ndim - 1, tiled=True) for v in (gn_gain, gn_shift, mean, factor)
        )
    mean = jnp.repeat(mean, group_width, axis=1)[:, None, None, None]
    factor = jnp.repeat(factor, group_width, axis=1)[:, None, None, None]
    normed = (tile.astype(jnp.float32) - mean) * factor * gain + shift
    row_at = row_block * rows - 1 + jnp.arange(rows + 2)
    col_at = me * width - 1 + jnp.arange(width + 2)
    inside = ((row_at >= 0) & (row_at < rows * spaces))[:, None] & ((col_at >= 0) & (col_at < cols))[None]
    active = jnp.where(inside[None, None, :, :, None], jax.nn.silu(normed), 0.0).astype(jnp.bfloat16)
    wide = jnp.repeat(jnp.repeat(active, 2, axis=2), 2, axis=3)[:, :, 1:-1, 1:-1]
    flat = wide.reshape((clips * frames,) + wide.shape[2:])
    output = lax.conv_general_dilated(
        flat,
        up_weight,
        (1, 1),
        "VALID",
        dimension_numbers=("NHWC", "HWIO", "NHWC"),
        preferred_element_type=jnp.float32,
    )
    output = (output + up_bias).astype(jnp.bfloat16)
    return output.reshape(clips, frames, 2 * rows, 2 * width, half)


def placed_at():
    return lax.axis_index("tm"), lax.axis_index("space"), lax.axis_index("chan")


def fetch_kernel(weight_ref, weight_out, sem):
    copy = pltpu.make_async_copy(weight_ref, weight_out, sem)
    copy.start()
    copy.wait()


def relay_kernel(got_ref, after_ref, out_ref):
    del after_ref
    tm, _, _ = placed_at()
    depth = out_ref.shape[1]
    out_ref[...] = jnp.where(tm % 2 > 0, got_ref[:, :depth], got_ref[:, depth:])


def select_kernel(own_ref, got_ref, passed_ref, out_ref):
    tm, _, chan = placed_at()
    depth = out_ref.shape[2]
    upper, home = tm % 2 > 0, chan == tm // 2
    out_ref[0] = jnp.where(upper, got_ref[:, depth:], got_ref[:, :depth])
    own = jnp.where(upper, own_ref[:, depth:], own_ref[:, :depth])
    out_ref[1] = jnp.where(home, own, passed_ref[...])


def stack_kernel(own_ref, row_ref, out_ref):
    out_ref[0] = own_ref[...]
    out_ref[1] = row_ref[...]


def conv_of_clip(clip, near_ref, far_ref, weight_ref, latents, taps):
    spans, spaces, span, rows, cols, depth = latents.shape
    frames, tall = spans * span, spaces * rows
    tm, side, chan = placed_at()
    size = span * rows * cols
    part = pl.ds(pl.multiple_of(clip * size, size), size)
    for ref, core in ((near_ref, chan), (far_ref, 1 - chan)):
        home = core == tm // 2
        for j, source in enumerate((jnp.where(home, tm ^ 1, tm ^ 2), jnp.where(home, tm, tm ^ 3))):
            for i, at in enumerate((side, 1 - side)):
                latents[source, at] = ref[i, j, part, :].astype(jnp.float32).reshape(latents.shape[2:])
    column = lax.broadcasted_iota(jnp.int32, (1, cols, depth), 1)
    empty = jnp.zeros((frames, cols, depth), jnp.float32)
    lines = [[empty] * 3]
    for at in range(spaces):
        for row in range(rows):
            parts = [latents[(j + clip) % spans, at, :, row] for j in range(spans)]
            value = jnp.concatenate(parts, axis=0)
            lower = jnp.where(column > 0, pltpu.roll(value, 1, 1), 0.0)
            upper = jnp.where(column < cols - 1, pltpu.roll(value, cols - 1, 1), 0.0)
            lines.append([lower, value, upper])
    lines.append([empty] * 3)
    short = tall // 2
    for line in range(short + 2):
        taps[line, :2] = jnp.zeros((2,) + taps.shape[2:], taps.dtype)
        for e in range(3):
            piece = jnp.concatenate([lines[line][e], lines[line + short][e]], axis=1)
            taps[line, 2:, :, e * depth : (e + 1) * depth] = piece.astype(taps.dtype)
    total = None
    for a in range(3):
        wide = [taps[b : b + short, a : a + frames].reshape(frames * tall * cols, 3 * depth) for b in range(3)]
        right = weight_ref[a].reshape(9 * depth, weight_ref.shape[4])
        product = jnp.dot(jnp.concatenate(wide, axis=1), right, preferred_element_type=jnp.float32)
        total = product if total is None else total + product
    width = total.shape[1] // 2
    swapped = tm % 2 > 0
    lower, upper = total[:, :width], total[:, width:]
    return jnp.where(swapped, upper, lower), jnp.where(swapped, lower, upper)


def conv_far_kernel(near_ref, far_ref, weight_ref, same_ref, other_ref, latents, taps):
    tm, _, _ = placed_at()
    same, other = conv_of_clip(1 - tm // 2, near_ref, far_ref, weight_ref, latents, taps)
    same_ref[...] = same.astype(same_ref.dtype)
    other_ref[...] = other.astype(other_ref.dtype)


def conv_near_kernel(near_ref, far_ref, weight_ref, keep_ref, other_ref, latents, taps):
    tm, _, _ = placed_at()
    keep, other = conv_of_clip(tm // 2, near_ref, far_ref, weight_ref, latents, taps)
    keep_ref[...] = keep
    other_ref[...] = other.astype(other_ref.dtype)


def norm_kernel(*refs):
    partial, (bias_ref, gain_ref, shift_ref), sent = refs[:4], refs[4:7], refs[7:11]
    tiles = refs[11]
    tm, side, _ = placed_at()
    owners, reach, strip, depth = tiles.shape
    cols = 8
    frames = strip // (cols // owners + 2)
    tall = partial[0].shape[0] // (frames * cols)
    group = C // GROUPS
    block = pl.ds(tm % bias_ref.shape[0], 1)
    total = partial[0][...]
    for ref in partial[1:]:
        total = total + ref[...].astype(jnp.float32)
    flat = (total + bias_ref[block, :]).astype(jnp.bfloat16).astype(jnp.float32)
    sums = jnp.sum(flat, axis=0, keepdims=True)
    squares = jnp.sum(flat * flat, axis=0, keepdims=True)
    lane = lax.broadcasted_iota(jnp.int32, (depth, depth), 0) // group
    other = lax.broadcasted_iota(jnp.int32, (depth, depth), 1) // group
    same = (lane == other).astype(jnp.float32)
    both = jnp.concatenate([sums, squares, jnp.zeros((6, depth), jnp.float32)], axis=0)
    both = jnp.dot(both, same, precision=lax.Precision.HIGHEST, preferred_element_type=jnp.float32)
    both = both / float(flat.shape[0] * group)
    mean, square = both[0:1], both[1:2]
    factor = lax.rsqrt(square - mean * mean + 1e-06)
    normed = (flat - mean) * factor * gain_ref[block, :] + shift_ref[block, :]
    active = (normed / (1.0 + jnp.exp(-normed))).reshape(tall // 2, frames, 2, cols, depth)
    short = tall // 2
    cells = [jnp.swapaxes(active[row % short, :, row // short], 0, 1) for row in range(tall)]
    width = cols // owners
    empty = jnp.zeros((frames, depth), jnp.float32)
    for i in range(reach):
        chosen = jnp.where(side > 0, cells[i + tall - reach], cells[i])
        for owner in range(owners):
            picked = []
            for j in range(owner * width - 1, (owner + 1) * width + 1):
                picked.append(chosen[j] if 0 <= j < cols else empty)
            tiles[owner, i] = jnp.concatenate(picked, axis=0).astype(tiles.dtype)
    for m in range(owners):
        sent[m][...] = tiles[tm ^ m]


def cells_kernel(*refs):
    got, cells_ref, tiles = refs[:4], refs[4], refs[5]
    tm, _, _ = placed_at()
    for ref, m in zip(got, (0, 3, 2, 1)):
        tiles[tm ^ m] = ref[...].astype(jnp.float32)
    reach, wide, tall, half = cells_ref.shape
    depth = tiles.shape[3]
    los = half // depth
    clips = tiles.shape[0] // los
    frames = tall // clips
    for i in range(reach):
        for j in range(wide):
            for x in range(los):
                stack = [tiles[clip * los + x, i, j * frames : (j + 1) * frames] for clip in range(clips)]
                piece = jnp.concatenate(stack, axis=0).astype(cells_ref.dtype)
                cells_ref[i, j, :, x * depth : (x + 1) * depth] = piece


def taps_of(side, half, cells_ref, weight_ref, cells, out_rows, out_cols):
    reach, width = cells_ref.shape[0], cells_ref.shape[3]
    cells[jnp.where(side > 0, reach, 0)] = jnp.zeros(cells.shape[1:], cells.dtype)
    for i in range(reach):
        cells[i + 1 - side] = cells_ref[i]
    rows = pl.ds(pl.multiple_of(half * width, width), width)
    total = None
    for b in range(3):
        lines = []
        for e in range(3):
            pieces = [
                cells[(r - 1 + b) // 2 + 1, (q - 1 + e) // 2 + 1]
                for r in range(out_rows)
                for q in range(out_cols)
            ]
            lines.append(jnp.concatenate(pieces, axis=0))
        right = jnp.concatenate([weight_ref[b, e, rows, :] for e in range(3)], axis=0)
        part = jnp.dot(jnp.concatenate(lines, axis=1), right, preferred_element_type=jnp.float32)
        total = part if total is None else total + part
    return total


def near_kernel(cells_ref, weight_ref, bias_ref, total_ref, cells):
    _, side, chan = placed_at()
    out_rows, out_cols = 2 * (cells_ref.shape[0] - 1), 2 * (cells_ref.shape[1] - 2)
    total = taps_of(side, chan, cells_ref, weight_ref, cells, out_rows, out_cols)
    total_ref[...] = total + bias_ref[...]


def far_kernel(cells_ref, weight_ref, total_ref, out_ref, cells):
    _, side, chan = placed_at()
    clips, frames, out_rows, out_cols, width = out_ref.shape
    total = taps_of(side, 1 - chan, cells_ref, weight_ref, cells, out_rows, out_cols)
    total = (total + total_ref[...]).reshape(out_rows * out_cols, clips, frames, width)
    span = frames // 4
    for clip in range(clips):
        turned = jnp.swapaxes(total[:, clip], 0, 1).astype(out_ref.dtype)
        for k in range(frames):
            slot = (k + clip * span) % frames
            for r in range(out_rows):
                out_ref[clip, slot, r] = turned[k, r * out_cols : (r + 1) * out_cols]


def run(kernel, shapes, scratch, *operands, flops=0, moved=0):
    several = isinstance(shapes, (list, tuple))
    vmem = pl.BlockSpec(memory_space=pltpu.VMEM)
    return pl.pallas_call(
        kernel,
        out_shape=shapes,
        in_specs=[vmem] * len(operands),
        out_specs=[vmem] * len(shapes) if several else vmem,
        scratch_shapes=scratch,
        compiler_params=pltpu.CompilerParams(vmem_limit_bytes=16 << 20),
        cost_estimate=pl.CostEstimate(flops=flops, bytes_accessed=moved, transcendentals=0),
    )(*operands)


def small_plan(latents, conv_weight, conv_bias, gn_gain, gn_shift, up_weight, up_bias):
    clips, span, rows, cols, half = latents.shape
    spans, spaces, chans = lax.axis_size("tm"), lax.axis_size("space"), lax.axis_size("chan")
    los = spans // clips
    frames, tall, width, depth = span * spans, rows * spaces, cols // spans, half // los
    low, full = jnp.bfloat16, jnp.float32
    shape = jax.ShapeDtypeStruct
    flip = ((0, 1), (1, 0))

    cells_in = latents.reshape(clips * span * rows * cols, half)
    first, second = [], []
    for source in range(spans):
        for chan in range(chans):
            home = chan == source // 2
            target = (source ^ 1, chan) if home else (source ^ 2, 1 - chan)
            first.append((source * chans + chan, target[0] * chans + target[1]))
            second.append((source * chans + chan, (source ^ 1) * chans + chan))
    got = lax.ppermute(cells_in, ("tm", "chan"), first)
    weight = run(fetch_kernel, shape(conv_weight.shape, low), [pltpu.SemaphoreType.DMA], conv_weight, moved=4 << 20)
    relayed = run(relay_kernel, shape((cells_in.shape[0], depth), low), [], got, weight, moved=1 << 17)
    passed = lax.ppermute(relayed, ("tm", "chan"), second)

    def across(value, axes, m):
        count = lax.axis_size(axes)
        return lax.ppermute(value, axes, [(i, i ^ m) for i in range(count)])

    own = run(select_kernel, shape((2, cells_in.shape[0], depth), low), [], cells_in, got, passed, moved=1 << 17)
    row = across(own, "space", 1)
    near = run(stack_kernel, shape((spaces,) + own.shape, low), [], own, row, moved=1 << 17)
    far = across(near, "chan", 1)

    count = frames * tall * cols
    part = [shape((count, depth), full), shape((count, depth), low)]
    scratch = [
        pltpu.VMEM((spans, spaces, span, rows, cols, depth), full),
        pltpu.VMEM((tall // 2 + 2, frames + 2, 2 * cols, 3 * depth), low),
    ]
    cost = {"flops": 2 * count * 27 * depth * half, "moved": 3 << 20}
    far_same, far_other = run(conv_far_kernel, [part[1], part[1]], scratch, near, far, weight, **cost)
    partial = [across(far_same, "tm", 2), across(far_other, "tm", 3)]
    keep, near_other = run(conv_near_kernel, part, scratch, near, far, weight, **cost)
    partial = [keep] + partial + [across(near_other, "tm", 1)]

    tile = shape((rows + 1, (width + 2) * frames, depth), low)
    tiles = run(
        norm_kernel,
        [tile] * spans,
        [pltpu.VMEM((spans,) + tile.shape, low)],
        *partial,
        *(vector.reshape(los, depth) for vector in (conv_bias, gn_gain, gn_shift)),
        moved=1 << 19,
    )
    tiles = [tiles[0]] + [across(tiles[m], "tm", m) for m in range(spans - 1, 0, -1)]

    near = run(
        cells_kernel,
        shape((rows + 1, width + 2, clips * frames, half), low),
        [pltpu.VMEM((spans,) + tile.shape, full)],
        *tiles,
        moved=1 << 18,
    )
    far = lax.ppermute(near, "chan", flip)
    cells = pltpu.VMEM((rows + 2,) + near.shape[1:], low)
    outputs = clips * frames * 4 * rows * width
    flops = 2 * outputs * 9 * half * half
    total = run(
        near_kernel, shape((outputs, half), full), [cells], near, up_weight, up_bias[None],
        flops=flops, moved=2 << 20,
    )
    return run(
        far_kernel, shape((clips, frames, 2 * rows, 2 * width, half), low), [cells], far, up_weight, total,
        flops=flops, moved=2 << 20,
    )


def solution(mesh):
    sizes = dict(mesh.shape)
    small = sizes["tm"] == 4 and sizes["space"] == 2 and sizes["chan"] == 2
    placed = (
        P("groups", "tm", "space", None, "chan"),
        P(None, None, None, "tm", "chan"),
        P("chan"),
        P("chan"),
        P("chan"),
        P(None, None, None, "chan"),
        P("chan"),
    )
    return jax.shard_map(
        small_plan if small else general_plan,
        mesh=mesh,
        in_specs=placed,
        out_specs=P("groups", None, "space", "tm", "chan"),
        check_vma=False,
    )
```

```python
import jax
import jax.numpy as jnp
from jax import lax
from jax.experimental import pallas as pl
from jax.experimental.pallas import tpu as pltpu
from jax.sharding import PartitionSpec as P

C = 512
GROUPS = 32


def shifted(value, axis, step):
    count = lax.axis_size(axis)
    pairs = [(i, i + step) for i in range(count) if 0 <= i + step < count]
    return lax.ppermute(value, axis, pairs)


def rows_around(block, axis_rows, depth):
    low = shifted(lax.slice_in_dim(block, block.shape[axis_rows] - depth, None, axis=axis_rows), "space", 1)
    high = shifted(lax.slice_in_dim(block, 0, depth, axis=axis_rows), "space", -1)
    return jnp.concatenate([low, block, high], axis=axis_rows)


def input_slice(latents):
    clips, span, rows, cols, half = latents.shape
    spans, spaces, chans = lax.axis_size("tm"), lax.axis_size("space"), lax.axis_size("chan")
    me, row_block = lax.axis_index("tm"), lax.axis_index("space")
    depth = half * chans // spans
    per_half = half // depth
    if spaces == 2:
        whole = lax.all_gather(latents, ("tm", "space", "chan"))
        whole = whole.reshape(spans, spaces, chans, clips, span, rows, cols, per_half, depth)
        mine = lax.dynamic_index_in_dim(whole, me // per_half, axis=2, keepdims=False)
        mine = lax.dynamic_index_in_dim(mine, me % per_half, axis=7 - 1, keepdims=False)
        mine = mine.transpose(2, 0, 3, 1, 4, 5, 6).reshape(clips, spans * span, spaces * rows, cols, depth)
        mine = jnp.pad(mine, ((0, 0), (0, 0), (1, 1), (0, 0), (0, 0)))
        mine = lax.dynamic_slice_in_dim(mine, row_block * rows, rows + 2, axis=2)
    else:
        bordered = rows_around(latents, 2, 1)
        whole = lax.all_gather(bordered, ("tm", "chan"))
        whole = whole.reshape((spans, chans) + bordered.shape[:4] + (per_half, depth))
        mine = lax.dynamic_index_in_dim(whole, me // per_half, axis=1, keepdims=False)
        mine = lax.dynamic_index_in_dim(mine, me % per_half, axis=5, keepdims=False)
        mine = mine.transpose(1, 0, 2, 3, 4, 5).reshape(clips, spans * span, rows + 2, cols, depth)
    return jnp.stack([jnp.roll(mine[c], -c * span, axis=0) for c in range(clips)])


def general_plan(latents, conv_weight, conv_bias, gn_gain, gn_shift, up_weight, up_bias):
    clips, span, rows, cols, half = latents.shape
    spans, spaces, chans = lax.axis_size("tm"), lax.axis_size("space"), lax.axis_size("chan")
    me, row_block = lax.axis_index("tm"), lax.axis_index("space")
    frames, width = span * spans, cols // spans
    group_width = C // GROUPS

    mine = input_slice(latents)
    padded = jnp.pad(mine, ((0, 0), (2, 0), (0, 0), (1, 1), (0, 0)))
    partial = lax.conv_general_dilated(
        padded,
        conv_weight,
        (1, 1, 1),
        "VALID",
        dimension_numbers=("NDHWC", "DHWIO", "NDHWC"),
        preferred_element_type=jnp.float32,
    )
    partial = jnp.stack([jnp.roll(partial[c], c * span, axis=0) for c in range(clips)])
    parts = partial.reshape(clips, frames, rows, spans, width, half)
    parts = parts.transpose(3, 0, 1, 2, 4, 5)
    parts = lax.all_to_all(parts, "tm", split_axis=0, concat_axis=0, tiled=True)
    conved = (jnp.sum(parts, axis=0) + conv_bias).astype(jnp.bfloat16)

    values = conved.astype(jnp.float32).reshape(-1, half)
    values = values.reshape(clips, frames * rows * width, half // group_width, group_width)
    if spaces == 2:
        every = lax.all_gather(conved, ("tm", "space", "chan"))
        every = every.reshape(spans, spaces, chans, clips, frames, rows, width, half)
        every = every.transpose(3, 4, 1, 5, 0, 6, 2, 7).reshape(clips, frames, spaces * rows, cols, C)
        gain = lax.all_gather(gn_gain, "chan", tiled=True)
        shift = lax.all_gather(gn_shift, "chan", tiled=True)
        values = every.astype(jnp.float32).reshape(clips, -1, GROUPS, group_width)
        sums = jnp.sum(values, axis=(1, 3))
        squares = jnp.sum(values * values, axis=(1, 3))
        count = float(values.shape[1] * group_width)
        mean = sums / count
        factor = lax.rsqrt(squares / count - mean * mean + 1e-06)
        edged = jnp.pad(every, ((0, 0), (0, 0), (1, 1), (1, 1), (0, 0)))
        tile = lax.dynamic_slice(
            edged, (0, 0, row_block * rows, me * width, 0), (clips, frames, rows + 2, width + 2, C)
        )
    else:
        sums = jnp.sum(values, axis=(1, 3))
        squares = jnp.sum(values * values, axis=(1, 3))
        sums, squares = lax.psum((sums, squares), ("tm", "space"))
        count = float(values.shape[1] * group_width * spans * spaces)
        mean = sums / count
        factor = lax.rsqrt(squares / count - mean * mean + 1e-06)
        bordered = rows_around(conved, 2, 1)
        left = shifted(bordered[:, :, :, -1:], "tm", 1)
        right = shifted(bordered[:, :, :, :1], "tm", -1)
        tile = jnp.concatenate([left, bordered, right], axis=3)
        tile = lax.all_gather(tile, "chan", axis=4, tiled=True)
        gain, shift, mean, factor = (
            lax.all_gather(v, "chan", axis=v.ndim - 1, tiled=True) for v in (gn_gain, gn_shift, mean, factor)
        )
    mean = jnp.repeat(mean, group_width, axis=1)[:, None, None, None]
    factor = jnp.repeat(factor, group_width, axis=1)[:, None, None, None]
    normed = (tile.astype(jnp.float32) - mean) * factor * gain + shift
    row_at = row_block * rows - 1 + jnp.arange(rows + 2)
    col_at = me * width - 1 + jnp.arange(width + 2)
    inside = ((row_at >= 0) & (row_at < rows * spaces))[:, None] & ((col_at >= 0) & (col_at < cols))[None]
    active = jnp.where(inside[None, None, :, :, None], jax.nn.silu(normed), 0.0).astype(jnp.bfloat16)
    wide = jnp.repeat(jnp.repeat(active, 2, axis=2), 2, axis=3)[:, :, 1:-1, 1:-1]
    flat = wide.reshape((clips * frames,) + wide.shape[2:])
    output = lax.conv_general_dilated(
        flat,
        up_weight,
        (1, 1),
        "VALID",
        dimension_numbers=("NHWC", "HWIO", "NHWC"),
        preferred_element_type=jnp.float32,
    )
    output = (output + up_bias).astype(jnp.bfloat16)
    return output.reshape(clips, frames, 2 * rows, 2 * width, half)


def placed_at():
    return lax.axis_index("tm"), lax.axis_index("space"), lax.axis_index("chan")


def fetch_kernel(weight_ref, weight_out, sem):
    copy = pltpu.make_async_copy(weight_ref, weight_out, sem)
    copy.start()
    copy.wait()


def relay_kernel(got_ref, after_ref, out_ref):
    del after_ref
    tm, _, _ = placed_at()
    depth = out_ref.shape[1]
    out_ref[...] = jnp.where(tm % 2 > 0, got_ref[:, :depth], got_ref[:, depth:])


def select_kernel(own_ref, got_ref, passed_ref, out_ref):
    tm, _, chan = placed_at()
    depth = out_ref.shape[2]
    upper, home = tm % 2 > 0, chan == tm // 2
    out_ref[0] = jnp.where(upper, got_ref[:, depth:], got_ref[:, :depth])
    own = jnp.where(upper, own_ref[:, depth:], own_ref[:, :depth])
    out_ref[1] = jnp.where(home, own, passed_ref[...])


def conv_of_clip(clip, got, weight_ref, latents, taps):
    spans, spaces, span, rows, cols, depth = latents.shape
    frames, tall = spans * span, spaces * rows
    tm, side, chan = placed_at()
    size = span * rows * cols
    part = pl.ds(pl.multiple_of(clip * size, size), size)
    for i, ref in enumerate(got):
        at = side if i < 2 else 1 - side
        home = (chan if i % 2 == 0 else 1 - chan) == tm // 2
        for j, source in enumerate((jnp.where(home, tm ^ 1, tm ^ 2), jnp.where(home, tm, tm ^ 3))):
            latents[source, at] = ref[j, part, :].astype(jnp.float32).reshape(latents.shape[2:])
    column = lax.broadcasted_iota(jnp.int32, (1, cols, depth), 1)
    empty = jnp.zeros((frames, cols, depth), jnp.float32)
    lines = [[empty] * 3]
    for at in range(spaces):
        for row in range(rows):
            parts = [latents[(j + clip) % spans, at, :, row] for j in range(spans)]
            value = jnp.concatenate(parts, axis=0)
            lower = jnp.where(column > 0, pltpu.roll(value, 1, 1), 0.0)
            upper = jnp.where(column < cols - 1, pltpu.roll(value, cols - 1, 1), 0.0)
            lines.append([lower, value, upper])
    lines.append([empty] * 3)
    short = tall // 2
    for line in range(short + 2):
        taps[line, :2] = jnp.zeros((2,) + taps.shape[2:], taps.dtype)
        for e in range(3):
            piece = jnp.concatenate([lines[line][e], lines[line + short][e]], axis=1)
            taps[line, 2:, :, e * depth : (e + 1) * depth] = piece.astype(taps.dtype)
    total = None
    for a in range(3):
        wide = [taps[b : b + short, a : a + frames].reshape(frames * tall * cols, 3 * depth) for b in range(3)]
        right = weight_ref[a].reshape(9 * depth, weight_ref.shape[4])
        product = jnp.dot(jnp.concatenate(wide, axis=1), right, preferred_element_type=jnp.float32)
        total = product if total is None else total + product
    width = total.shape[1] // 2
    swapped = tm % 2 > 0
    lower, upper = total[:, :width], total[:, width:]
    return jnp.where(swapped, upper, lower), jnp.where(swapped, lower, upper)


def conv_far_kernel(own_ref, core_ref, row_ref, both_ref, weight_ref, same_ref, other_ref, latents, taps):
    tm, _, _ = placed_at()
    got = (own_ref, core_ref, row_ref, both_ref)
    same, other = conv_of_clip(1 - tm // 2, got, weight_ref, latents, taps)
    same_ref[...] = same.astype(same_ref.dtype)
    other_ref[...] = other.astype(other_ref.dtype)


def conv_near_kernel(own_ref, core_ref, row_ref, both_ref, weight_ref, keep_ref, other_ref, latents, taps):
    tm, _, _ = placed_at()
    got = (own_ref, core_ref, row_ref, both_ref)
    keep, other = conv_of_clip(tm // 2, got, weight_ref, latents, taps)
    keep_ref[...] = keep
    other_ref[...] = other.astype(other_ref.dtype)


def norm_kernel(*refs):
    partial, (bias_ref, gain_ref, shift_ref), sent = refs[:4], refs[4:7], refs[7:11]
    tiles = refs[11]
    tm, side, _ = placed_at()
    owners, reach, strip, depth = tiles.shape
    cols = 8
    frames = strip // (cols // owners + 2)
    tall = partial[0].shape[0] // (frames * cols)
    group = C // GROUPS
    block = pl.ds(tm % bias_ref.shape[0], 1)
    total = partial[0][...]
    for ref in partial[1:]:
        total = total + ref[...].astype(jnp.float32)
    flat = (total + bias_ref[block, :]).astype(jnp.bfloat16).astype(jnp.float32)
    sums = jnp.sum(flat, axis=0, keepdims=True)
    squares = jnp.sum(flat * flat, axis=0, keepdims=True)
    lane = lax.broadcasted_iota(jnp.int32, (depth, depth), 0) // group
    other = lax.broadcasted_iota(jnp.int32, (depth, depth), 1) // group
    same = (lane == other).astype(jnp.float32)
    both = jnp.concatenate([sums, squares, jnp.zeros((6, depth), jnp.float32)], axis=0)
    both = jnp.dot(both, same, precision=lax.Precision.HIGHEST, preferred_element_type=jnp.float32)
    both = both / float(flat.shape[0] * group)
    mean, square = both[0:1], both[1:2]
    factor = lax.rsqrt(square - mean * mean + 1e-06)
    normed = (flat - mean) * factor * gain_ref[block, :] + shift_ref[block, :]
    active = (normed / (1.0 + jnp.exp(-normed))).reshape(tall // 2, frames, 2, cols, depth)
    short = tall // 2
    cells = [jnp.swapaxes(active[row % short, :, row // short], 0, 1) for row in range(tall)]
    width = cols // owners
    empty = jnp.zeros((frames, depth), jnp.float32)
    for i in range(reach):
        chosen = jnp.where(side > 0, cells[i + tall - reach], cells[i])
        for owner in range(owners):
            picked = []
            for j in range(owner * width - 1, (owner + 1) * width + 1):
                picked.append(chosen[j] if 0 <= j < cols else empty)
            tiles[owner, i] = jnp.concatenate(picked, axis=0).astype(tiles.dtype)
    for m in range(owners):
        sent[m][...] = tiles[tm ^ m]


def cells_kernel(*refs):
    got, cells_ref, tiles = refs[:4], refs[4], refs[5]
    tm, _, _ = placed_at()
    for m in range(len(got)):
        tiles[tm ^ m] = got[m][...].astype(jnp.float32)
    reach, wide, tall, half = cells_ref.shape
    depth = tiles.shape[3]
    los = half // depth
    clips = tiles.shape[0] // los
    frames = tall // clips
    for i in range(reach):
        for j in range(wide):
            for x in range(los):
                stack = [tiles[clip * los + x, i, j * frames : (j + 1) * frames] for clip in range(clips)]
                piece = jnp.concatenate(stack, axis=0).astype(cells_ref.dtype)
                cells_ref[i, j, :, x * depth : (x + 1) * depth] = piece


def taps_of(side, half, cells_ref, weight_ref, cells, out_rows, out_cols):
    reach, width = cells_ref.shape[0], cells_ref.shape[3]
    cells[jnp.where(side > 0, reach, 0)] = jnp.zeros(cells.shape[1:], cells.dtype)
    for i in range(reach):
        cells[i + 1 - side] = cells_ref[i]
    rows = pl.ds(pl.multiple_of(half * width, width), width)
    total = None
    for b in range(3):
        lines = []
        for e in range(3):
            pieces = [
                cells[(r - 1 + b) // 2 + 1, (q - 1 + e) // 2 + 1]
                for r in range(out_rows)
                for q in range(out_cols)
            ]
            lines.append(jnp.concatenate(pieces, axis=0))
        right = jnp.concatenate([weight_ref[b, e, rows, :] for e in range(3)], axis=0)
        part = jnp.dot(jnp.concatenate(lines, axis=1), right, preferred_element_type=jnp.float32)
        total = part if total is None else total + part
    return total


def near_kernel(cells_ref, weight_ref, bias_ref, total_ref, cells):
    _, side, chan = placed_at()
    out_rows, out_cols = 2 * (cells_ref.shape[0] - 1), 2 * (cells_ref.shape[1] - 2)
    total = taps_of(side, chan, cells_ref, weight_ref, cells, out_rows, out_cols)
    total_ref[...] = total + bias_ref[...]


def far_kernel(cells_ref, weight_ref, total_ref, out_ref, cells):
    _, side, chan = placed_at()
    clips, frames, out_rows, out_cols, width = out_ref.shape
    total = taps_of(side, 1 - chan, cells_ref, weight_ref, cells, out_rows, out_cols)
    total = (total + total_ref[...]).reshape(out_rows * out_cols, clips, frames, width)
    span = frames // 4
    for clip in range(clips):
        turned = jnp.swapaxes(total[:, clip], 0, 1).astype(out_ref.dtype)
        for k in range(frames):
            slot = (k + clip * span) % frames
            for r in range(out_rows):
                out_ref[clip, slot, r] = turned[k, r * out_cols : (r + 1) * out_cols]


def run(kernel, shapes, scratch, *operands, flops=0, moved=0):
    several = isinstance(shapes, (list, tuple))
    vmem = pl.BlockSpec(memory_space=pltpu.VMEM)
    return pl.pallas_call(
        kernel,
        out_shape=shapes,
        in_specs=[vmem] * len(operands),
        out_specs=[vmem] * len(shapes) if several else vmem,
        scratch_shapes=scratch,
        compiler_params=pltpu.CompilerParams(vmem_limit_bytes=16 << 20),
        cost_estimate=pl.CostEstimate(flops=flops, bytes_accessed=moved, transcendentals=0),
    )(*operands)


def small_plan(latents, conv_weight, conv_bias, gn_gain, gn_shift, up_weight, up_bias):
    clips, span, rows, cols, half = latents.shape
    spans, spaces, chans = lax.axis_size("tm"), lax.axis_size("space"), lax.axis_size("chan")
    los = spans // clips
    frames, tall, width, depth = span * spans, rows * spaces, cols // spans, half // los
    low, full = jnp.bfloat16, jnp.float32
    shape = jax.ShapeDtypeStruct
    flip = ((0, 1), (1, 0))

    cells_in = latents.reshape(clips * span * rows * cols, half)
    first, second = [], []
    for source in range(spans):
        for chan in range(chans):
            home = chan == source // 2
            target = (source ^ 1, chan) if home else (source ^ 2, 1 - chan)
            first.append((source * chans + chan, target[0] * chans + target[1]))
            second.append((source * chans + chan, (source ^ 1) * chans + chan))
    got = lax.ppermute(cells_in, ("tm", "chan"), first)
    weight = run(fetch_kernel, shape(conv_weight.shape, low), [pltpu.SemaphoreType.DMA], conv_weight, moved=4 << 20)
    relayed = run(relay_kernel, shape((cells_in.shape[0], depth), low), [], got, weight, moved=1 << 17)
    passed = lax.ppermute(relayed, ("tm", "chan"), second)

    own = run(select_kernel, shape((2, cells_in.shape[0], depth), low), [], cells_in, got, passed, moved=1 << 17)
    every = [own] + [
        lax.ppermute(own, ("space", "chan"), [(i, i ^ m) for i in range(spaces * chans)]) for m in range(1, spaces * chans)
    ]

    count = frames * tall * cols
    part = shape((count, depth), low)
    scratch = [
        pltpu.VMEM((spans, spaces, span, rows, cols, depth), full),
        pltpu.VMEM((tall // 2 + 2, frames + 2, 2 * cols, 3 * depth), low),
    ]
    flops = 2 * count * 27 * depth * half
    far_same, far_other = run(
        conv_far_kernel, [part, part], scratch, *every, weight, flops=flops, moved=3 << 20
    )
    partial = [
        lax.ppermute(value, "tm", [(i, i ^ m) for i in range(spans)]) for m, value in ((2, far_same), (3, far_other))
    ]
    keep, near_other = run(
        conv_near_kernel, [shape(part.shape, full), part], scratch, *every, weight, flops=flops, moved=3 << 20
    )
    partial = [keep] + partial + [lax.ppermute(near_other, "tm", [(i, i ^ 1) for i in range(spans)])]

    tile = shape((rows + 1, (width + 2) * frames, depth), low)
    tiles = run(
        norm_kernel,
        [tile] * spans,
        [pltpu.VMEM((spans,) + tile.shape, low)],
        *partial,
        *(vector.reshape(los, depth) for vector in (conv_bias, gn_gain, gn_shift)),
        moved=1 << 19,
    )
    tiles = [tiles[0]] + [
        lax.ppermute(tiles[m], "tm", [(i, i ^ m) for i in range(spans)]) for m in range(1, spans)
    ]

    near = run(
        cells_kernel,
        shape((rows + 1, width + 2, clips * frames, half), low),
        [pltpu.VMEM((spans,) + tile.shape, full)],
        *tiles,
        moved=1 << 18,
    )
    far = lax.ppermute(near, "chan", flip)
    cells = pltpu.VMEM((rows + 2,) + near.shape[1:], low)
    outputs = clips * frames * 4 * rows * width
    flops = 2 * outputs * 9 * half * half
    total = run(
        near_kernel, shape((outputs, half), full), [cells], near, up_weight, up_bias[None],
        flops=flops, moved=2 << 20,
    )
    return run(
        far_kernel, shape((clips, frames, 2 * rows, 2 * width, half), low), [cells], far, up_weight, total,
        flops=flops, moved=2 << 20,
    )


def solution(mesh):
    sizes = dict(mesh.shape)
    small = sizes["tm"] == 4 and sizes["space"] == 2 and sizes["chan"] == 2
    placed = (
        P("groups", "tm", "space", None, "chan"),
        P(None, None, None, "tm", "chan"),
        P("chan"),
        P("chan"),
        P("chan"),
        P(None, None, None, "chan"),
        P("chan"),
    )
    return jax.shard_map(
        small_plan if small else general_plan,
        mesh=mesh,
        in_specs=placed,
        out_specs=P("groups", None, "space", "tm", "chan"),
        check_vma=False,
    )
```

```python
import jax
import jax.numpy as jnp
from jax import lax
from jax.experimental import pallas as pl
from jax.experimental.pallas import tpu as pltpu
from jax.sharding import PartitionSpec as P

C = 512
GROUPS = 32


def shifted(value, axis, step):
    count = lax.axis_size(axis)
    pairs = [(i, i + step) for i in range(count) if 0 <= i + step < count]
    return lax.ppermute(value, axis, pairs)


def rows_around(block, axis_rows, depth):
    low = shifted(lax.slice_in_dim(block, block.shape[axis_rows] - depth, None, axis=axis_rows), "space", 1)
    high = shifted(lax.slice_in_dim(block, 0, depth, axis=axis_rows), "space", -1)
    return jnp.concatenate([low, block, high], axis=axis_rows)


def input_slice(latents):
    clips, span, rows, cols, half = latents.shape
    spans, spaces, chans = lax.axis_size("tm"), lax.axis_size("space"), lax.axis_size("chan")
    me, row_block = lax.axis_index("tm"), lax.axis_index("space")
    depth = half * chans // spans
    per_half = half // depth
    if spaces == 2:
        whole = lax.all_gather(latents, ("tm", "space", "chan"))
        whole = whole.reshape(spans, spaces, chans, clips, span, rows, cols, per_half, depth)
        mine = lax.dynamic_index_in_dim(whole, me // per_half, axis=2, keepdims=False)
        mine = lax.dynamic_index_in_dim(mine, me % per_half, axis=7 - 1, keepdims=False)
        mine = mine.transpose(2, 0, 3, 1, 4, 5, 6).reshape(clips, spans * span, spaces * rows, cols, depth)
        mine = jnp.pad(mine, ((0, 0), (0, 0), (1, 1), (0, 0), (0, 0)))
        mine = lax.dynamic_slice_in_dim(mine, row_block * rows, rows + 2, axis=2)
    else:
        bordered = rows_around(latents, 2, 1)
        whole = lax.all_gather(bordered, ("tm", "chan"))
        whole = whole.reshape((spans, chans) + bordered.shape[:4] + (per_half, depth))
        mine = lax.dynamic_index_in_dim(whole, me // per_half, axis=1, keepdims=False)
        mine = lax.dynamic_index_in_dim(mine, me % per_half, axis=5, keepdims=False)
        mine = mine.transpose(1, 0, 2, 3, 4, 5).reshape(clips, spans * span, rows + 2, cols, depth)
    return jnp.stack([jnp.roll(mine[c], -c * span, axis=0) for c in range(clips)])


def general_plan(latents, conv_weight, conv_bias, gn_gain, gn_shift, up_weight, up_bias):
    clips, span, rows, cols, half = latents.shape
    spans, spaces, chans = lax.axis_size("tm"), lax.axis_size("space"), lax.axis_size("chan")
    me, row_block = lax.axis_index("tm"), lax.axis_index("space")
    frames, width = span * spans, cols // spans
    group_width = C // GROUPS

    mine = input_slice(latents)
    padded = jnp.pad(mine, ((0, 0), (2, 0), (0, 0), (1, 1), (0, 0)))
    partial = lax.conv_general_dilated(
        padded,
        conv_weight,
        (1, 1, 1),
        "VALID",
        dimension_numbers=("NDHWC", "DHWIO", "NDHWC"),
        preferred_element_type=jnp.float32,
    )
    partial = jnp.stack([jnp.roll(partial[c], c * span, axis=0) for c in range(clips)])
    parts = partial.reshape(clips, frames, rows, spans, width, half)
    parts = parts.transpose(3, 0, 1, 2, 4, 5)
    parts = lax.all_to_all(parts, "tm", split_axis=0, concat_axis=0, tiled=True)
    conved = (jnp.sum(parts, axis=0) + conv_bias).astype(jnp.bfloat16)

    values = conved.astype(jnp.float32).reshape(-1, half)
    values = values.reshape(clips, frames * rows * width, half // group_width, group_width)
    if spaces == 2:
        every = lax.all_gather(conved, ("tm", "space", "chan"))
        every = every.reshape(spans, spaces, chans, clips, frames, rows, width, half)
        every = every.transpose(3, 4, 1, 5, 0, 6, 2, 7).reshape(clips, frames, spaces * rows, cols, C)
        gain = lax.all_gather(gn_gain, "chan", tiled=True)
        shift = lax.all_gather(gn_shift, "chan", tiled=True)
        values = every.astype(jnp.float32).reshape(clips, -1, GROUPS, group_width)
        sums = jnp.sum(values, axis=(1, 3))
        squares = jnp.sum(values * values, axis=(1, 3))
        count = float(values.shape[1] * group_width)
        mean = sums / count
        factor = lax.rsqrt(squares / count - mean * mean + 1e-06)
        edged = jnp.pad(every, ((0, 0), (0, 0), (1, 1), (1, 1), (0, 0)))
        tile = lax.dynamic_slice(
            edged, (0, 0, row_block * rows, me * width, 0), (clips, frames, rows + 2, width + 2, C)
        )
    else:
        sums = jnp.sum(values, axis=(1, 3))
        squares = jnp.sum(values * values, axis=(1, 3))
        sums, squares = lax.psum((sums, squares), ("tm", "space"))
        count = float(values.shape[1] * group_width * spans * spaces)
        mean = sums / count
        factor = lax.rsqrt(squares / count - mean * mean + 1e-06)
        bordered = rows_around(conved, 2, 1)
        left = shifted(bordered[:, :, :, -1:], "tm", 1)
        right = shifted(bordered[:, :, :, :1], "tm", -1)
        tile = jnp.concatenate([left, bordered, right], axis=3)
        tile = lax.all_gather(tile, "chan", axis=4, tiled=True)
        gain, shift, mean, factor = (
            lax.all_gather(v, "chan", axis=v.ndim - 1, tiled=True) for v in (gn_gain, gn_shift, mean, factor)
        )
    mean = jnp.repeat(mean, group_width, axis=1)[:, None, None, None]
    factor = jnp.repeat(factor, group_width, axis=1)[:, None, None, None]
    normed = (tile.astype(jnp.float32) - mean) * factor * gain + shift
    row_at = row_block * rows - 1 + jnp.arange(rows + 2)
    col_at = me * width - 1 + jnp.arange(width + 2)
    inside = ((row_at >= 0) & (row_at < rows * spaces))[:, None] & ((col_at >= 0) & (col_at < cols))[None]
    active = jnp.where(inside[None, None, :, :, None], jax.nn.silu(normed), 0.0).astype(jnp.bfloat16)
    wide = jnp.repeat(jnp.repeat(active, 2, axis=2), 2, axis=3)[:, :, 1:-1, 1:-1]
    flat = wide.reshape((clips * frames,) + wide.shape[2:])
    output = lax.conv_general_dilated(
        flat,
        up_weight,
        (1, 1),
        "VALID",
        dimension_numbers=("NHWC", "HWIO", "NHWC"),
        preferred_element_type=jnp.float32,
    )
    output = (output + up_bias).astype(jnp.bfloat16)
    return output.reshape(clips, frames, 2 * rows, 2 * width, half)


def placed_at():
    return lax.axis_index("tm"), lax.axis_index("space"), lax.axis_index("chan")


def fetch_kernel(weight_ref, weight_out, sem):
    copy = pltpu.make_async_copy(weight_ref, weight_out, sem)
    copy.start()
    copy.wait()


def select_kernel(first_ref, second_ref, after_ref, out_ref):
    del after_ref
    tm, _, _ = placed_at()
    depth = out_ref.shape[2]
    upper = tm % 2 > 0
    for i, ref in enumerate((first_ref, second_ref)):
        out_ref[i] = jnp.where(upper, ref[:, depth:], ref[:, :depth])


def stack_kernel(own_ref, row_ref, out_ref):
    out_ref[0] = own_ref[...]
    out_ref[1] = row_ref[...]


def conv_of_clip(clip, near_ref, far_ref, weight_ref, latents, taps):
    spans, spaces, span, rows, cols, depth = latents.shape
    frames, tall = spans * span, spaces * rows
    tm, side, chan = placed_at()
    size = span * rows * cols
    part = pl.ds(pl.multiple_of(clip * size, size), size)
    for ref, core in ((near_ref, chan), (far_ref, 1 - chan)):
        home = core == tm // 2
        for j, source in enumerate((jnp.where(home, tm ^ 1, tm ^ 2), jnp.where(home, tm, tm ^ 3))):
            for i, at in enumerate((side, 1 - side)):
                latents[source, at] = ref[i, j, part, :].astype(jnp.float32).reshape(latents.shape[2:])
    column = lax.broadcasted_iota(jnp.int32, (1, cols, depth), 1)
    empty = jnp.zeros((frames, cols, depth), jnp.float32)
    lines = [[empty] * 3]
    for at in range(spaces):
        for row in range(rows):
            parts = [latents[(j + clip) % spans, at, :, row] for j in range(spans)]
            value = jnp.concatenate(parts, axis=0)
            lower = jnp.where(column > 0, pltpu.roll(value, 1, 1), 0.0)
            upper = jnp.where(column < cols - 1, pltpu.roll(value, cols - 1, 1), 0.0)
            lines.append([lower, value, upper])
    lines.append([empty] * 3)
    short = tall // 2
    for line in range(short + 2):
        taps[line, :2] = jnp.zeros((2,) + taps.shape[2:], taps.dtype)
        for e in range(3):
            piece = jnp.concatenate([lines[line][e], lines[line + short][e]], axis=1)
            taps[line, 2:, :, e * depth : (e + 1) * depth] = piece.astype(taps.dtype)
    total = None
    for a in range(3):
        wide = [taps[b : b + short, a : a + frames].reshape(frames * tall * cols, 3 * depth) for b in range(3)]
        right = weight_ref[a].reshape(9 * depth, weight_ref.shape[4])
        product = jnp.dot(jnp.concatenate(wide, axis=1), right, preferred_element_type=jnp.float32)
        total = product if total is None else total + product
    width = total.shape[1] // 2
    swapped = tm % 2 > 0
    lower, upper = total[:, :width], total[:, width:]
    return jnp.where(swapped, upper, lower), jnp.where(swapped, lower, upper)


def conv_far_kernel(near_ref, far_ref, weight_ref, same_ref, other_ref, latents, taps):
    tm, _, _ = placed_at()
    same, other = conv_of_clip(1 - tm // 2, near_ref, far_ref, weight_ref, latents, taps)
    same_ref[...] = same.astype(same_ref.dtype)
    other_ref[...] = other.astype(other_ref.dtype)


def conv_near_kernel(near_ref, far_ref, weight_ref, keep_ref, other_ref, latents, taps):
    tm, _, _ = placed_at()
    keep, other = conv_of_clip(tm // 2, near_ref, far_ref, weight_ref, latents, taps)
    keep_ref[...] = keep
    other_ref[...] = other.astype(other_ref.dtype)


def norm_kernel(*refs):
    partial, (bias_ref, gain_ref, shift_ref), sent = refs[:4], refs[4:7], refs[7:11]
    tiles = refs[11]
    tm, side, _ = placed_at()
    owners, reach, strip, depth = tiles.shape
    cols = 8
    frames = strip // (cols // owners + 2)
    tall = partial[0].shape[0] // (frames * cols)
    group = C // GROUPS
    block = pl.ds(tm % bias_ref.shape[0], 1)
    total = partial[0][...]
    for ref in partial[1:]:
        total = total + ref[...].astype(jnp.float32)
    flat = (total + bias_ref[block, :]).astype(jnp.bfloat16).astype(jnp.float32)
    sums = jnp.sum(flat, axis=0, keepdims=True)
    squares = jnp.sum(flat * flat, axis=0, keepdims=True)
    lane = lax.broadcasted_iota(jnp.int32, (depth, depth), 0) // group
    other = lax.broadcasted_iota(jnp.int32, (depth, depth), 1) // group
    same = (lane == other).astype(jnp.float32)
    both = jnp.concatenate([sums, squares, jnp.zeros((6, depth), jnp.float32)], axis=0)
    both = jnp.dot(both, same, precision=lax.Precision.HIGHEST, preferred_element_type=jnp.float32)
    both = both / float(flat.shape[0] * group)
    mean, square = both[0:1], both[1:2]
    factor = lax.rsqrt(square - mean * mean + 1e-06)
    normed = (flat - mean) * factor * gain_ref[block, :] + shift_ref[block, :]
    active = (normed / (1.0 + jnp.exp(-normed))).reshape(tall // 2, frames, 2, cols, depth)
    short = tall // 2
    cells = [jnp.swapaxes(active[row % short, :, row // short], 0, 1) for row in range(tall)]
    width = cols // owners
    empty = jnp.zeros((frames, depth), jnp.float32)
    for i in range(reach):
        chosen = jnp.where(side > 0, cells[i + tall - reach], cells[i])
        for owner in range(owners):
            picked = []
            for j in range(owner * width - 1, (owner + 1) * width + 1):
                picked.append(chosen[j] if 0 <= j < cols else empty)
            tiles[owner, i] = jnp.concatenate(picked, axis=0).astype(tiles.dtype)
    for m in range(owners):
        sent[m][...] = tiles[tm ^ m]


def cells_kernel(*refs):
    got, cells_ref, tiles = refs[:4], refs[4], refs[5]
    tm, _, _ = placed_at()
    for m in range(len(got)):
        tiles[tm ^ m] = got[m][...].astype(jnp.float32)
    reach, wide, tall, half = cells_ref.shape
    depth = tiles.shape[3]
    los = half // depth
    clips = tiles.shape[0] // los
    frames = tall // clips
    for i in range(reach):
        for j in range(wide):
            for x in range(los):
                stack = [tiles[clip * los + x, i, j * frames : (j + 1) * frames] for clip in range(clips)]
                piece = jnp.concatenate(stack, axis=0).astype(cells_ref.dtype)
                cells_ref[i, j, :, x * depth : (x + 1) * depth] = piece


def taps_of(side, half, cells_ref, weight_ref, cells, out_rows, out_cols):
    reach, width = cells_ref.shape[0], cells_ref.shape[3]
    cells[jnp.where(side > 0, reach, 0)] = jnp.zeros(cells.shape[1:], cells.dtype)
    for i in range(reach):
        cells[i + 1 - side] = cells_ref[i]
    rows = pl.ds(pl.multiple_of(half * width, width), width)
    total = None
    for b in range(3):
        lines = []
        for e in range(3):
            pieces = [
                cells[(r - 1 + b) // 2 + 1, (q - 1 + e) // 2 + 1]
                for r in range(out_rows)
                for q in range(out_cols)
            ]
            lines.append(jnp.concatenate(pieces, axis=0))
        right = jnp.concatenate([weight_ref[b, e, rows, :] for e in range(3)], axis=0)
        part = jnp.dot(jnp.concatenate(lines, axis=1), right, preferred_element_type=jnp.float32)
        total = part if total is None else total + part
    return total


def near_kernel(cells_ref, weight_ref, bias_ref, total_ref, cells):
    _, side, chan = placed_at()
    out_rows, out_cols = 2 * (cells_ref.shape[0] - 1), 2 * (cells_ref.shape[1] - 2)
    total = taps_of(side, chan, cells_ref, weight_ref, cells, out_rows, out_cols)
    total_ref[...] = total + bias_ref[...]


def far_kernel(cells_ref, weight_ref, total_ref, out_ref, cells):
    _, side, chan = placed_at()
    clips, frames, out_rows, out_cols, width = out_ref.shape
    total = taps_of(side, 1 - chan, cells_ref, weight_ref, cells, out_rows, out_cols)
    total = (total + total_ref[...]).reshape(out_rows * out_cols, clips, frames, width)
    span = frames // 4
    for clip in range(clips):
        turned = jnp.swapaxes(total[:, clip], 0, 1).astype(out_ref.dtype)
        for k in range(frames):
            slot = (k + clip * span) % frames
            for r in range(out_rows):
                out_ref[clip, slot, r] = turned[k, r * out_cols : (r + 1) * out_cols]


def run(kernel, shapes, scratch, *operands, flops=0, moved=0):
    several = isinstance(shapes, (list, tuple))
    vmem = pl.BlockSpec(memory_space=pltpu.VMEM)
    return pl.pallas_call(
        kernel,
        out_shape=shapes,
        in_specs=[vmem] * len(operands),
        out_specs=[vmem] * len(shapes) if several else vmem,
        scratch_shapes=scratch,
        compiler_params=pltpu.CompilerParams(vmem_limit_bytes=16 << 20),
        cost_estimate=pl.CostEstimate(flops=flops, bytes_accessed=moved, transcendentals=0),
    )(*operands)


def small_plan(latents, conv_weight, conv_bias, gn_gain, gn_shift, up_weight, up_bias):
    clips, span, rows, cols, half = latents.shape
    spans, spaces, chans = lax.axis_size("tm"), lax.axis_size("space"), lax.axis_size("chan")
    los = spans // clips
    frames, tall, width, depth = span * spans, rows * spaces, cols // spans, half // los
    low, full = jnp.bfloat16, jnp.float32
    shape = jax.ShapeDtypeStruct
    flip = ((0, 1), (1, 0))

    cells_in = latents.reshape(clips * span * rows * cols, half)
    turns = ((1, 2), (0, 3))
    got = []
    for at_home, across in turns:
        pairs = []
        for source in range(spans):
            for chan in range(chans):
                home = chan == source // 2
                target = (source ^ at_home, chan) if home else (source ^ across, 1 - chan)
                pairs.append((source * chans + chan, target[0] * chans + target[1]))
        got.append(lax.ppermute(cells_in, ("tm", "chan"), pairs))
    def across(value, axes, m):
        count = lax.axis_size(axes)
        return lax.ppermute(value, axes, [(i, i ^ m) for i in range(count)])

    weight = run(fetch_kernel, shape(conv_weight.shape, low), [pltpu.SemaphoreType.DMA], conv_weight, moved=4 << 20)
    own = run(select_kernel, shape((2, cells_in.shape[0], depth), low), [], *got, weight, moved=1 << 17)
    row = across(own, "space", 1)
    near = run(stack_kernel, shape((spaces,) + own.shape, low), [], own, row, moved=1 << 17)
    far = across(near, "chan", 1)

    count = frames * tall * cols
    part = [shape((count, depth), full), shape((count, depth), low)]
    scratch = [
        pltpu.VMEM((spans, spaces, span, rows, cols, depth), full),
        pltpu.VMEM((tall // 2 + 2, frames + 2, 2 * cols, 3 * depth), low),
    ]
    cost = {"flops": 2 * count * 27 * depth * half, "moved": 3 << 20}
    far_same, far_other = run(conv_far_kernel, [part[1], part[1]], scratch, near, far, weight, **cost)
    partial = [across(far_same, "tm", 2), across(far_other, "tm", 3)]
    keep, near_other = run(conv_near_kernel, part, scratch, near, far, weight, **cost)
    partial = [keep] + partial + [across(near_other, "tm", 1)]

    tile = shape((rows + 1, (width + 2) * frames, depth), low)
    tiles = run(
        norm_kernel,
        [tile] * spans,
        [pltpu.VMEM((spans,) + tile.shape, low)],
        *partial,
        *(vector.reshape(los, depth) for vector in (conv_bias, gn_gain, gn_shift)),
        moved=1 << 19,
    )
    tiles = [tiles[0]] + [across(tiles[m], "tm", m) for m in range(1, spans)]

    near = run(
        cells_kernel,
        shape((rows + 1, width + 2, clips * frames, half), low),
        [pltpu.VMEM((spans,) + tile.shape, full)],
        *tiles,
        moved=1 << 18,
    )
    far = lax.ppermute(near, "chan", flip)
    cells = pltpu.VMEM((rows + 2,) + near.shape[1:], low)
    outputs = clips * frames * 4 * rows * width
    flops = 2 * outputs * 9 * half * half
    total = run(
        near_kernel, shape((outputs, half), full), [cells], near, up_weight, up_bias[None],
        flops=flops, moved=2 << 20,
    )
    return run(
        far_kernel, shape((clips, frames, 2 * rows, 2 * width, half), low), [cells], far, up_weight, total,
        flops=flops, moved=2 << 20,
    )


def solution(mesh):
    sizes = dict(mesh.shape)
    small = sizes["tm"] == 4 and sizes["space"] == 2 and sizes["chan"] == 2
    placed = (
        P("groups", "tm", "space", None, "chan"),
        P(None, None, None, "tm", "chan"),
        P("chan"),
        P("chan"),
        P("chan"),
        P(None, None, None, "chan"),
        P("chan"),
    )
    return jax.shard_map(
        small_plan if small else general_plan,
        mesh=mesh,
        in_specs=placed,
        out_specs=P("groups", None, "space", "tm", "chan"),
        check_vma=False,
    )
```

```python
import jax
import jax.numpy as jnp
from jax import lax
from jax.experimental import pallas as pl
from jax.experimental.pallas import tpu as pltpu
from jax.sharding import PartitionSpec as P

C = 512
GROUPS = 32


def shifted(value, axis, step):
    count = lax.axis_size(axis)
    pairs = [(i, i + step) for i in range(count) if 0 <= i + step < count]
    return lax.ppermute(value, axis, pairs)


def rows_around(block, axis_rows, depth):
    low = shifted(lax.slice_in_dim(block, block.shape[axis_rows] - depth, None, axis=axis_rows), "space", 1)
    high = shifted(lax.slice_in_dim(block, 0, depth, axis=axis_rows), "space", -1)
    return jnp.concatenate([low, block, high], axis=axis_rows)


def input_slice(latents):
    clips, span, rows, cols, half = latents.shape
    spans, spaces, chans = lax.axis_size("tm"), lax.axis_size("space"), lax.axis_size("chan")
    me, row_block = lax.axis_index("tm"), lax.axis_index("space")
    depth = half * chans // spans
    per_half = half // depth
    if spaces == 2:
        whole = lax.all_gather(latents, ("tm", "space", "chan"))
        whole = whole.reshape(spans, spaces, chans, clips, span, rows, cols, per_half, depth)
        mine = lax.dynamic_index_in_dim(whole, me // per_half, axis=2, keepdims=False)
        mine = lax.dynamic_index_in_dim(mine, me % per_half, axis=7 - 1, keepdims=False)
        mine = mine.transpose(2, 0, 3, 1, 4, 5, 6).reshape(clips, spans * span, spaces * rows, cols, depth)
        mine = jnp.pad(mine, ((0, 0), (0, 0), (1, 1), (0, 0), (0, 0)))
        mine = lax.dynamic_slice_in_dim(mine, row_block * rows, rows + 2, axis=2)
    else:
        bordered = rows_around(latents, 2, 1)
        whole = lax.all_gather(bordered, ("tm", "chan"))
        whole = whole.reshape((spans, chans) + bordered.shape[:4] + (per_half, depth))
        mine = lax.dynamic_index_in_dim(whole, me // per_half, axis=1, keepdims=False)
        mine = lax.dynamic_index_in_dim(mine, me % per_half, axis=5, keepdims=False)
        mine = mine.transpose(1, 0, 2, 3, 4, 5).reshape(clips, spans * span, rows + 2, cols, depth)
    return jnp.stack([jnp.roll(mine[c], -c * span, axis=0) for c in range(clips)])


def general_plan(latents, conv_weight, conv_bias, gn_gain, gn_shift, up_weight, up_bias):
    clips, span, rows, cols, half = latents.shape
    spans, spaces, chans = lax.axis_size("tm"), lax.axis_size("space"), lax.axis_size("chan")
    me, row_block = lax.axis_index("tm"), lax.axis_index("space")
    frames, width = span * spans, cols // spans
    group_width = C // GROUPS

    mine = input_slice(latents)
    padded = jnp.pad(mine, ((0, 0), (2, 0), (0, 0), (1, 1), (0, 0)))
    partial = lax.conv_general_dilated(
        padded,
        conv_weight,
        (1, 1, 1),
        "VALID",
        dimension_numbers=("NDHWC", "DHWIO", "NDHWC"),
        preferred_element_type=jnp.float32,
    )
    partial = jnp.stack([jnp.roll(partial[c], c * span, axis=0) for c in range(clips)])
    parts = partial.reshape(clips, frames, rows, spans, width, half)
    parts = parts.transpose(3, 0, 1, 2, 4, 5)
    parts = lax.all_to_all(parts, "tm", split_axis=0, concat_axis=0, tiled=True)
    conved = (jnp.sum(parts, axis=0) + conv_bias).astype(jnp.bfloat16)

    values = conved.astype(jnp.float32).reshape(-1, half)
    values = values.reshape(clips, frames * rows * width, half // group_width, group_width)
    if spaces == 2:
        every = lax.all_gather(conved, ("tm", "space", "chan"))
        every = every.reshape(spans, spaces, chans, clips, frames, rows, width, half)
        every = every.transpose(3, 4, 1, 5, 0, 6, 2, 7).reshape(clips, frames, spaces * rows, cols, C)
        gain = lax.all_gather(gn_gain, "chan", tiled=True)
        shift = lax.all_gather(gn_shift, "chan", tiled=True)
        values = every.astype(jnp.float32).reshape(clips, -1, GROUPS, group_width)
        sums = jnp.sum(values, axis=(1, 3))
        squares = jnp.sum(values * values, axis=(1, 3))
        count = float(values.shape[1] * group_width)
        mean = sums / count
        factor = lax.rsqrt(squares / count - mean * mean + 1e-06)
        edged = jnp.pad(every, ((0, 0), (0, 0), (1, 1), (1, 1), (0, 0)))
        tile = lax.dynamic_slice(
            edged, (0, 0, row_block * rows, me * width, 0), (clips, frames, rows + 2, width + 2, C)
        )
    else:
        sums = jnp.sum(values, axis=(1, 3))
        squares = jnp.sum(values * values, axis=(1, 3))
        sums, squares = lax.psum((sums, squares), ("tm", "space"))
        count = float(values.shape[1] * group_width * spans * spaces)
        mean = sums / count
        factor = lax.rsqrt(squares / count - mean * mean + 1e-06)
        bordered = rows_around(conved, 2, 1)
        left = shifted(bordered[:, :, :, -1:], "tm", 1)
        right = shifted(bordered[:, :, :, :1], "tm", -1)
        tile = jnp.concatenate([left, bordered, right], axis=3)
        tile = lax.all_gather(tile, "chan", axis=4, tiled=True)
        gain, shift, mean, factor = (
            lax.all_gather(v, "chan", axis=v.ndim - 1, tiled=True) for v in (gn_gain, gn_shift, mean, factor)
        )
    mean = jnp.repeat(mean, group_width, axis=1)[:, None, None, None]
    factor = jnp.repeat(factor, group_width, axis=1)[:, None, None, None]
    normed = (tile.astype(jnp.float32) - mean) * factor * gain + shift
    row_at = row_block * rows - 1 + jnp.arange(rows + 2)
    col_at = me * width - 1 + jnp.arange(width + 2)
    inside = ((row_at >= 0) & (row_at < rows * spaces))[:, None] & ((col_at >= 0) & (col_at < cols))[None]
    active = jnp.where(inside[None, None, :, :, None], jax.nn.silu(normed), 0.0).astype(jnp.bfloat16)
    wide = jnp.repeat(jnp.repeat(active, 2, axis=2), 2, axis=3)[:, :, 1:-1, 1:-1]
    flat = wide.reshape((clips * frames,) + wide.shape[2:])
    output = lax.conv_general_dilated(
        flat,
        up_weight,
        (1, 1),
        "VALID",
        dimension_numbers=("NHWC", "HWIO", "NHWC"),
        preferred_element_type=jnp.float32,
    )
    output = (output + up_bias).astype(jnp.bfloat16)
    return output.reshape(clips, frames, 2 * rows, 2 * width, half)


def placed_at():
    return lax.axis_index("tm"), lax.axis_index("space"), lax.axis_index("chan")


def fetch_kernel(weight_ref, weight_out, sem):
    copy = pltpu.make_async_copy(weight_ref, weight_out, sem)
    copy.start()
    copy.wait()


def select_kernel(first_ref, second_ref, after_ref, out_ref):
    del after_ref
    tm, _, _ = placed_at()
    depth = out_ref.shape[2]
    upper = tm % 2 > 0
    for i, ref in enumerate((first_ref, second_ref)):
        out_ref[i] = jnp.where(upper, ref[:, depth:], ref[:, :depth])


def conv_of_clip(clip, got, weight_ref, latents, taps):
    spans, spaces, span, rows, cols, depth = latents.shape
    frames, tall = spans * span, spaces * rows
    tm, side, chan = placed_at()
    size = span * rows * cols
    part = pl.ds(pl.multiple_of(clip * size, size), size)
    for i, ref in enumerate(got):
        at = side if i < 2 else 1 - side
        home = (chan if i % 2 == 0 else 1 - chan) == tm // 2
        for j, source in enumerate((jnp.where(home, tm ^ 1, tm ^ 2), jnp.where(home, tm, tm ^ 3))):
            latents[source, at] = ref[j, part, :].astype(jnp.float32).reshape(latents.shape[2:])
    column = lax.broadcasted_iota(jnp.int32, (1, cols, depth), 1)
    empty = jnp.zeros((frames, cols, depth), jnp.float32)
    lines = [[empty] * 3]
    for at in range(spaces):
        for row in range(rows):
            parts = [latents[(j + clip) % spans, at, :, row] for j in range(spans)]
            value = jnp.concatenate(parts, axis=0)
            lower = jnp.where(column > 0, pltpu.roll(value, 1, 1), 0.0)
            upper = jnp.where(column < cols - 1, pltpu.roll(value, cols - 1, 1), 0.0)
            lines.append([lower, value, upper])
    lines.append([empty] * 3)
    short = tall // 2
    for line in range(short + 2):
        taps[line, :2] = jnp.zeros((2,) + taps.shape[2:], taps.dtype)
        for e in range(3):
            piece = jnp.concatenate([lines[line][e], lines[line + short][e]], axis=1)
            taps[line, 2:, :, e * depth : (e + 1) * depth] = piece.astype(taps.dtype)
    total = None
    for a in range(3):
        wide = [taps[b : b + short, a : a + frames].reshape(frames * tall * cols, 3 * depth) for b in range(3)]
        right = weight_ref[a].reshape(9 * depth, weight_ref.shape[4])
        product = jnp.dot(jnp.concatenate(wide, axis=1), right, preferred_element_type=jnp.float32)
        total = product if total is None else total + product
    width = total.shape[1] // 2
    swapped = tm % 2 > 0
    lower, upper = total[:, :width], total[:, width:]
    return jnp.where(swapped, upper, lower), jnp.where(swapped, lower, upper)


def conv_far_kernel(own_ref, core_ref, row_ref, both_ref, weight_ref, same_ref, other_ref, latents, taps):
    tm, _, _ = placed_at()
    got = (own_ref, core_ref, row_ref, both_ref)
    same, other = conv_of_clip(1 - tm // 2, got, weight_ref, latents, taps)
    same_ref[...] = same.astype(same_ref.dtype)
    other_ref[...] = other.astype(other_ref.dtype)


def conv_near_kernel(own_ref, core_ref, row_ref, both_ref, weight_ref, keep_ref, other_ref, latents, taps):
    tm, _, _ = placed_at()
    got = (own_ref, core_ref, row_ref, both_ref)
    keep, other = conv_of_clip(tm // 2, got, weight_ref, latents, taps)
    keep_ref[...] = keep
    other_ref[...] = other.astype(other_ref.dtype)


def norm_kernel(*refs):
    partial, (bias_ref, gain_ref, shift_ref), sent = refs[:4], refs[4:7], refs[7:11]
    tiles = refs[11]
    tm, side, _ = placed_at()
    owners, reach, strip, depth = tiles.shape
    cols = 8
    frames = strip // (cols // owners + 2)
    tall = partial[0].shape[0] // (frames * cols)
    group = C // GROUPS
    block = pl.ds(tm % bias_ref.shape[0], 1)
    total = partial[0][...]
    for ref in partial[1:]:
        total = total + ref[...].astype(jnp.float32)
    flat = (total + bias_ref[block, :]).astype(jnp.bfloat16).astype(jnp.float32)
    sums = jnp.sum(flat, axis=0, keepdims=True)
    squares = jnp.sum(flat * flat, axis=0, keepdims=True)
    lane = lax.broadcasted_iota(jnp.int32, (depth, depth), 0) // group
    other = lax.broadcasted_iota(jnp.int32, (depth, depth), 1) // group
    same = (lane == other).astype(jnp.float32)
    both = jnp.concatenate([sums, squares, jnp.zeros((6, depth), jnp.float32)], axis=0)
    both = jnp.dot(both, same, precision=lax.Precision.HIGHEST, preferred_element_type=jnp.float32)
    both = both / float(flat.shape[0] * group)
    mean, square = both[0:1], both[1:2]
    factor = lax.rsqrt(square - mean * mean + 1e-06)
    normed = (flat - mean) * factor * gain_ref[block, :] + shift_ref[block, :]
    active = (normed / (1.0 + jnp.exp(-normed))).reshape(tall // 2, frames, 2, cols, depth)
    short = tall // 2
    cells = [jnp.swapaxes(active[row % short, :, row // short], 0, 1) for row in range(tall)]
    width = cols // owners
    empty = jnp.zeros((frames, depth), jnp.float32)
    for i in range(reach):
        chosen = jnp.where(side > 0, cells[i + tall - reach], cells[i])
        for owner in range(owners):
            picked = []
            for j in range(owner * width - 1, (owner + 1) * width + 1):
                picked.append(chosen[j] if 0 <= j < cols else empty)
            tiles[owner, i] = jnp.concatenate(picked, axis=0).astype(tiles.dtype)
    for m in range(owners):
        sent[m][...] = tiles[tm ^ m]


def cells_kernel(*refs):
    got, cells_ref, tiles = refs[:4], refs[4], refs[5]
    tm, _, _ = placed_at()
    for ref, m in zip(got, (0, 3, 2, 1)):
        tiles[tm ^ m] = ref[...].astype(jnp.float32)
    reach, wide, tall, half = cells_ref.shape
    depth = tiles.shape[3]
    los = half // depth
    clips = tiles.shape[0] // los
    frames = tall // clips
    for i in range(reach):
        for j in range(wide):
            for x in range(los):
                stack = [tiles[clip * los + x, i, j * frames : (j + 1) * frames] for clip in range(clips)]
                piece = jnp.concatenate(stack, axis=0).astype(cells_ref.dtype)
                cells_ref[i, j, :, x * depth : (x + 1) * depth] = piece


def taps_of(side, half, cells_ref, weight_ref, cells, out_rows, out_cols):
    reach, width = cells_ref.shape[0], cells_ref.shape[3]
    cells[jnp.where(side > 0, reach, 0)] = jnp.zeros(cells.shape[1:], cells.dtype)
    for i in range(reach):
        cells[i + 1 - side] = cells_ref[i]
    rows = pl.ds(pl.multiple_of(half * width, width), width)
    total = None
    for b in range(3):
        lines = []
        for e in range(3):
            pieces = [
                cells[(r - 1 + b) // 2 + 1, (q - 1 + e) // 2 + 1]
                for r in range(out_rows)
                for q in range(out_cols)
            ]
            lines.append(jnp.concatenate(pieces, axis=0))
        right = jnp.concatenate([weight_ref[b, e, rows, :] for e in range(3)], axis=0)
        part = jnp.dot(jnp.concatenate(lines, axis=1), right, preferred_element_type=jnp.float32)
        total = part if total is None else total + part
    return total


def near_kernel(cells_ref, weight_ref, bias_ref, total_ref, cells):
    _, side, chan = placed_at()
    out_rows, out_cols = 2 * (cells_ref.shape[0] - 1), 2 * (cells_ref.shape[1] - 2)
    total = taps_of(side, chan, cells_ref, weight_ref, cells, out_rows, out_cols)
    total_ref[...] = total + bias_ref[...]


def far_kernel(cells_ref, weight_ref, total_ref, out_ref, cells):
    _, side, chan = placed_at()
    clips, frames, out_rows, out_cols, width = out_ref.shape
    total = taps_of(side, 1 - chan, cells_ref, weight_ref, cells, out_rows, out_cols)
    total = (total + total_ref[...]).reshape(out_rows * out_cols, clips, frames, width)
    span = frames // 4
    for clip in range(clips):
        turned = jnp.swapaxes(total[:, clip], 0, 1).astype(out_ref.dtype)
        for k in range(frames):
            slot = (k + clip * span) % frames
            for r in range(out_rows):
                out_ref[clip, slot, r] = turned[k, r * out_cols : (r + 1) * out_cols]


def run(kernel, shapes, scratch, *operands, flops=0, moved=0):
    several = isinstance(shapes, (list, tuple))
    vmem = pl.BlockSpec(memory_space=pltpu.VMEM)
    return pl.pallas_call(
        kernel,
        out_shape=shapes,
        in_specs=[vmem] * len(operands),
        out_specs=[vmem] * len(shapes) if several else vmem,
        scratch_shapes=scratch,
        compiler_params=pltpu.CompilerParams(vmem_limit_bytes=16 << 20),
        cost_estimate=pl.CostEstimate(flops=flops, bytes_accessed=moved, transcendentals=0),
    )(*operands)


def small_plan(latents, conv_weight, conv_bias, gn_gain, gn_shift, up_weight, up_bias):
    clips, span, rows, cols, half = latents.shape
    spans, spaces, chans = lax.axis_size("tm"), lax.axis_size("space"), lax.axis_size("chan")
    los = spans // clips
    frames, tall, width, depth = span * spans, rows * spaces, cols // spans, half // los
    low, full = jnp.bfloat16, jnp.float32
    shape = jax.ShapeDtypeStruct
    flip = ((0, 1), (1, 0))

    cells_in = latents.reshape(clips * span * rows * cols, half)
    turns = ((1, 2), (0, 3))
    got = []
    for at_home, across in turns:
        pairs = []
        for source in range(spans):
            for chan in range(chans):
                home = chan == source // 2
                target = (source ^ at_home, chan) if home else (source ^ across, 1 - chan)
                pairs.append((source * chans + chan, target[0] * chans + target[1]))
        got.append(lax.ppermute(cells_in, ("tm", "chan"), pairs))
    weight = run(fetch_kernel, shape(conv_weight.shape, low), [pltpu.SemaphoreType.DMA], conv_weight, moved=4 << 20)
    own = run(select_kernel, shape((2, cells_in.shape[0], depth), low), [], *got, weight, moved=1 << 17)
    every = [own] + [
        lax.ppermute(own, ("space", "chan"), [(i, i ^ m) for i in range(spaces * chans)]) for m in range(1, spaces * chans)
    ]

    count = frames * tall * cols
    part = shape((count, depth), low)
    scratch = [
        pltpu.VMEM((spans, spaces, span, rows, cols, depth), full),
        pltpu.VMEM((tall // 2 + 2, frames + 2, 2 * cols, 3 * depth), low),
    ]
    flops = 2 * count * 27 * depth * half
    far_same, far_other = run(
        conv_far_kernel, [part, part], scratch, *every, weight, flops=flops, moved=3 << 20
    )
    partial = [
        lax.ppermute(value, "tm", [(i, i ^ m) for i in range(spans)]) for m, value in ((2, far_same), (3, far_other))
    ]
    keep, near_other = run(
        conv_near_kernel, [shape(part.shape, full), part], scratch, *every, weight, flops=flops, moved=3 << 20
    )
    partial = [keep] + partial + [lax.ppermute(near_other, "tm", [(i, i ^ 1) for i in range(spans)])]

    tile = shape((rows + 1, (width + 2) * frames, depth), low)
    tiles = run(
        norm_kernel,
        [tile] * spans,
        [pltpu.VMEM((spans,) + tile.shape, low)],
        *partial,
        *(vector.reshape(los, depth) for vector in (conv_bias, gn_gain, gn_shift)),
        moved=1 << 19,
    )
    tiles = [tiles[0]] + [
        lax.ppermute(tiles[m], "tm", [(i, i ^ m) for i in range(spans)]) for m in range(spans - 1, 0, -1)
    ]

    near = run(
        cells_kernel,
        shape((rows + 1, width + 2, clips * frames, half), low),
        [pltpu.VMEM((spans,) + tile.shape, full)],
        *tiles,
        moved=1 << 18,
    )
    far = lax.ppermute(near, "chan", flip)
    cells = pltpu.VMEM((rows + 2,) + near.shape[1:], low)
    outputs = clips * frames * 4 * rows * width
    flops = 2 * outputs * 9 * half * half
    total = run(
        near_kernel, shape((outputs, half), full), [cells], near, up_weight, up_bias[None],
        flops=flops, moved=2 << 20,
    )
    return run(
        far_kernel, shape((clips, frames, 2 * rows, 2 * width, half), low), [cells], far, up_weight, total,
        flops=flops, moved=2 << 20,
    )


def solution(mesh):
    sizes = dict(mesh.shape)
    small = sizes["tm"] == 4 and sizes["space"] == 2 and sizes["chan"] == 2
    placed = (
        P("groups", "tm", "space", None, "chan"),
        P(None, None, None, "tm", "chan"),
        P("chan"),
        P("chan"),
        P("chan"),
        P(None, None, None, "chan"),
        P("chan"),
    )
    return jax.shard_map(
        small_plan if small else general_plan,
        mesh=mesh,
        in_specs=placed,
        out_specs=P("groups", None, "space", "tm", "chan"),
        check_vma=False,
    )
```
